32 devices in a mesh: fsdp: 32 (over z, y, x, core).
Axes of the slice: x: 2, y: 2, z: 4, core: 2. Of those that a mesh axis runs over, the one named last changes fastest.
Arguments:
- tokens: bfloat16 [8192, 2048], P('fsdp'), may hold values from -6 to 6
- cotangent: bfloat16 [8192, 2048], P('fsdp'), may hold values from -6 to 6
- lengths: int32 [4], replicated, may hold values from 1024 to 4096, as said below
- attend_in: float32 [2048, 6144], P('fsdp'), may hold values from -0.125 to 0.125
- widening: float32 [2048, 8192], P('fsdp'), may hold values from -0.125 to 0.125
- attend_out: float32 [2048, 2048], P('fsdp'), may hold values from -2.5 to 2.5
- narrowing: float32 [2048, 8192], P('fsdp'), may hold values from -0.0625 to 0.0625
- small_params: float32 [2048, 13], P('fsdp'), as said below
- first_attend_in: float32 [2048, 6144], P('fsdp'), may hold values from -64 to 64
- first_widening: float32 [2048, 8192], P('fsdp'), may hold values from -20 to 20
- first_attend_out: float32 [2048, 2048], P('fsdp'), may hold values from -4 to 4
- first_narrowing: float32 [2048, 8192], P('fsdp'), may hold values from -32 to 32
- first_small: float32 [2048, 13], P('fsdp'), may hold values from -64 to 64
- second_attend_in: float32 [2048, 6144], P('fsdp'), may hold values from 434.176 to 1720.32
- second_widening: float32 [2048, 8192], P('fsdp'), may hold values from 53.248 to 212.992
- second_attend_out: float32 [2048, 2048], P('fsdp'), may hold values from 1 to 4
- second_narrowing: float32 [2048, 8192], P('fsdp'), may hold values from 155.648 to 622.592
- second_small: float32 [2048, 13], P('fsdp'), may hold values from 434.176 to 1720.32
Outputs:
- block_out: bfloat16 [8192, 2048], P('fsdp')
- token_grad: float32 [8192, 2048], P('fsdp')
- new_attend_in: float32 [2048, 6144], P('fsdp')
- new_widening: float32 [2048, 8192], P('fsdp')
- new_attend_out: float32 [2048, 2048], P('fsdp')
- new_narrowing: float32 [2048, 8192], P('fsdp')
- new_small: float32 [2048, 13], P('fsdp')
- mean_attend_in: float32 [2048, 6144], P('fsdp')
- mean_widening: float32 [2048, 8192], P('fsdp')
- mean_attend_out: float32 [2048, 2048], P('fsdp')
- mean_narrowing: float32 [2048, 8192], P('fsdp')
- mean_small: float32 [2048, 13], P('fsdp')
- square_attend_in: float32 [2048, 6144], P('fsdp')
- square_widening: float32 [2048, 8192], P('fsdp')
- square_attend_out: float32 [2048, 2048], P('fsdp')
- square_narrowing: float32 [2048, 8192], P('fsdp')
- square_small: float32 [2048, 13], P('fsdp')
The draws below stay inside these ranges and needn't reach their ends.
Inputs may be any that keep to these rules, and one draw needn't show every extreme that they name: The 4 lengths sum to 8192; each is 1024 or more and one is exactly 4096. `small_params`: gains near one in columns 0 and 2, biases of a tenth elsewhere.
All inputs are finite; a program needn't handle non-finite values.
Results may differ from the reference program's by a relative error of at most 0.011.
Values may be sent and summed in bfloat16 or wider, within the bound.
A program may use at most 704 MiB of HBM per device.

```python
import math
import jax
import jax.numpy as jnp
from jax import lax

D = 2048
HEADS = 8
FF = 8192
SMALLC = 13
TOK_DEV = 256
LMAX = 4096
LMIN = 1024
STEPS = 10
TOKENS = 8192
NSEQ = 4
BACK = 16


def draw_lengths(key, part):
    key = jax.random.fold_in(key, 11)
    key_weights, key_place = jax.random.split(key)
    others = NSEQ - 1
    spare = TOKENS - NSEQ * LMIN - (LMAX - LMIN)
    weights = jax.random.randint(key_weights, (others,), 50, 101).astype(jnp.int32)
    cumulative = jnp.cumsum(weights).astype(jnp.int32)
    bounds = spare * cumulative // cumulative[-1]
    extras = bounds - jnp.concatenate([jnp.zeros((1,), jnp.int32), bounds[:-1]])
    place = jax.random.randint(key_place, (), 0, NSEQ)
    slots = jnp.arange(NSEQ, dtype=jnp.int32)
    taken = jnp.clip(jnp.where(slots < place, slots, slots - 1), 0, others - 1)
    picked = extras[taken]
    return (LMIN + jnp.where(slots == place, LMAX - LMIN, picked)).astype(jnp.int32)


def draw_small_params(key, part):
    key = jax.random.fold_in(key, 23)
    base = 0.1 * jax.random.normal(key, (D, SMALLC), jnp.float32)
    column = jnp.arange(SMALLC)
    gains = jnp.where((column == 0) | (column == 2), 1.0, 0.0).astype(jnp.float32)
    return base + gains[None, :]


def strengthened(drawn, stream_key, source, target, shards_of, factor):
    def block_of(dim):
        return (jnp.arange(drawn.shape[dim]) // (drawn.shape[dim] // shards_of)).reshape((-1,) + (1,) * (drawn.ndim - 1 - dim))

    one_side = jax.random.permutation(stream_key, shards_of)[block_of(target)]
    other_side = (block_of(target) + shards_of // 2) % shards_of
    return jnp.where((block_of(source) == one_side) | (block_of(source) == other_side), factor * drawn, drawn)


def shard_levels(own_key, dims, cuts, smallest, high):
    def one(position, blocks):
        heights = jax.random.uniform(jax.random.fold_in(jax.random.fold_in(own_key, 6), position), (blocks,), jnp.float32, smallest / len(cuts), high / len(cuts))
        return jnp.repeat(jnp.exp(heights), dims[position] // blocks).reshape((-1,) + (1,) * (len(dims) - position - 1))

    gain = one(*cuts[0])
    for cut in cuts[1:]:
        gain = gain * one(*cut)
    return gain


def normal_values(key, extent, scale, reach, pieces=(), kind=jnp.bfloat16):
    level = shard_levels(key, extent, pieces, -0.22, 0.18) if pieces else 1.0
    entries = jax.random.normal(key, extent, jnp.float32) * scale * level
    return jnp.minimum(jnp.maximum(entries, -reach), reach).astype(kind)


def heavy_noise(key, shape, width, reach, shards, heavy, kind=jnp.bfloat16):
    values = width * jax.random.normal(key, shape, jnp.float32)
    if shards:
        values = values * shard_levels(key, shape, shards, -0.22, 0.18)
    return jnp.clip(strengthened(values, jax.random.fold_in(key, 3), *heavy), -reach, reach).astype(kind)


def setup_inputs(seed: int = 0) -> dict:
    arg_keys = jax.random.split(jax.random.key(seed), 19)
    return {
        "tokens": normal_values(arg_keys[0], (TOKENS, D), 1.0, 6.0, ((0, 32),)),
        "cotangent": heavy_noise(arg_keys[1], (TOKENS, D), 1.0, 6.0, ((0, 32),), (0, 1, 32, 2.75)),
        "lengths": draw_lengths(jax.random.fold_in(arg_keys[18], 71), 0),
        "attend_in": normal_values(arg_keys[3], (D, 3 * D), D ** -0.5, 0.125, ((0, 32),), jnp.float32),
        "widening": normal_values(arg_keys[4], (D, FF), D ** -0.5, 0.125, ((0, 32),), jnp.float32),
        "attend_out": normal_values(arg_keys[5], (D, D), (D * 11 // LMAX) ** -0.5, 2.5, ((0, 32),), jnp.float32),
        "narrowing": normal_values(arg_keys[6], (D, FF), FF ** -0.5, 0.0625, ((0, 32),), jnp.float32),
        "small_params": draw_small_params(jax.random.fold_in(arg_keys[18], 71), 0),
        "first_attend_in": normal_values(arg_keys[8], (D, 3 * D), (0.11 * TOKENS ** 0.5), 64.0, ((0, 32),), jnp.float32),
        "first_widening": normal_values(arg_keys[9], (D, FF), (0.04 * TOKENS ** 0.5), 20.0, ((0, 32),), jnp.float32),
        "first_attend_out": normal_values(arg_keys[10], (D, D), (0.36 * (TOKENS // LMAX) ** 0.5), 4.0, ((0, 32),), jnp.float32),
        "first_narrowing": normal_values(arg_keys[11], (D, FF), (0.066 * TOKENS ** 0.5), 32.0, ((0, 32),), jnp.float32),
        "first_small": normal_values(arg_keys[12], (D, SMALLC), (0.11 * TOKENS ** 0.5), 64.0, ((0, 32),), jnp.float32),
        "second_attend_in": jnp.clip(jnp.exp(math.log(1720.32) - 1.3768156 * jax.random.uniform(arg_keys[13], (D, 3 * D), jnp.float32) ** shard_levels(arg_keys[13], (D, 3 * D), ((0, 32),), -0.2, 0.2)), 434.176, 1720.32),
        "second_widening": jnp.clip(jnp.exp(math.log(212.992) - 1.3862944 * jax.random.uniform(arg_keys[14], (D, FF), jnp.float32) ** shard_levels(arg_keys[14], (D, FF), ((0, 32),), -0.2, 0.2)), 53.248, 212.992),
        "second_attend_out": jnp.clip(jnp.exp(math.log(4.0) - 1.3862944 * jax.random.uniform(arg_keys[15], (D, D), jnp.float32) ** shard_levels(arg_keys[15], (D, D), ((0, 32),), -0.2, 0.2)), 1.0, 4.0),
        "second_narrowing": jnp.clip(jnp.exp(math.log(622.592) - 1.3862944 * jax.random.uniform(arg_keys[16], (D, FF), jnp.float32) ** shard_levels(arg_keys[16], (D, FF), ((0, 32),), -0.2, 0.2)), 155.648, 622.592),
        "second_small": jnp.clip(jnp.exp(math.log(1720.32) - 1.3768156 * jax.random.uniform(arg_keys[17], (D, SMALLC), jnp.float32) ** shard_levels(arg_keys[17], (D, SMALLC), ((0, 32),), -0.2, 0.2)), 434.176, 1720.32),
    }


NORM_EPS = 1e-05
ADAM_EPS = 1e-08
BETA_ONE = 0.9
BETA_TWO = 0.95
WEIGHT_DECAY = 0.01
NEGATIVE = -1e+30
ROPE_BASE = 10000.0
HIGHEST = lax.Precision.HIGHEST

@jax.custom_vjp
def low(v):
    return lax.optimization_barrier(v.astype(jnp.bfloat16)).astype(jnp.float32)

@jax.custom_vjp
def low_back(v):
    return v

def low_keep(v):
    return (low(v), None)

def low_pass(kept, grad):
    return (grad,)

def back_keep(v):
    return (v, None)

def back_low(kept, grad):
    return (low(grad),)
low.defvjp(low_keep, low_pass)
low_back.defvjp(back_keep, back_low)

def matmul(left, right):
    return jnp.dot(left, right, preferred_element_type=jnp.float32, precision=HIGHEST)

def layer_norm(values, gain_vector, shift_vector):
    average = lax.optimization_barrier(jnp.mean(values, axis=-1, keepdims=True))
    centred = values - average
    spread = lax.optimization_barrier(jnp.mean(centred * centred, axis=-1, keepdims=True))
    return centred * lax.rsqrt(spread + NORM_EPS) * gain_vector + shift_vector

def token_places(global_rows, lengths):
    seq_ends = jnp.cumsum(lengths).astype(jnp.int32)
    starts = (seq_ends - lengths).astype(jnp.int32)
    member = (global_rows[:, None] >= starts[None, :]) & (global_rows[:, None] < seq_ends[None, :])
    numbers = jnp.arange(lengths.shape[0], dtype=jnp.int32)
    seq_ids = lax.optimization_barrier(jnp.sum(jnp.where(member, numbers[None, :], 0), axis=1)).astype(jnp.int32)
    offsets = (global_rows - lax.optimization_barrier(jnp.sum(jnp.where(member, starts[None, :], 0), axis=1))).astype(jnp.int32)
    return (seq_ids, offsets, jnp.any(member, axis=1))

def rotate(values, offsets):
    rotary = values.shape[-1] // 4
    half_rotary = rotary // 2
    frequency = ROPE_BASE ** (-2.0 * jnp.arange(half_rotary, dtype=jnp.float32) / rotary)
    angles = offsets.astype(jnp.float32)[:, None] * frequency[None, :]
    cosine = jnp.cos(angles)[:, None, :]
    sine_part = jnp.sin(angles)[:, None, :]
    first_half = values[..., :half_rotary]
    second_half = values[..., half_rotary:rotary]
    return jnp.concatenate([first_half * cosine - second_half * sine_part, second_half * cosine + first_half * sine_part, values[..., rotary:]], axis=-1)

def attention(queries, keys, values, seq_ids, valid):
    total_rows, model_width = queries.shape
    head_size = model_width // HEADS
    score_scale = head_size ** (-0.5)
    pad_rows = BACK * TOK_DEV
    window_rows = pad_rows + TOK_DEV
    keys_padded = jnp.concatenate([jnp.zeros((pad_rows, model_width), jnp.float32), keys])
    values_padded = jnp.concatenate([jnp.zeros((pad_rows, model_width), jnp.float32), values])
    ids_padded = jnp.concatenate([jnp.zeros((pad_rows,), jnp.int32), seq_ids])
    valid_padded = jnp.concatenate([jnp.zeros((pad_rows,), jnp.bool_), valid])

    def one_block(first_row):
        query_block = lax.dynamic_slice_in_dim(queries, first_row, TOK_DEV, 0).reshape(TOK_DEV, HEADS, head_size)
        key_block = lax.dynamic_slice_in_dim(keys_padded, first_row, window_rows, 0).reshape(window_rows, HEADS, head_size)
        value_block = lax.dynamic_slice_in_dim(values_padded, first_row, window_rows, 0).reshape(window_rows, HEADS, head_size)
        query_ids = lax.dynamic_slice_in_dim(seq_ids, first_row, TOK_DEV, 0)
        key_ids = lax.dynamic_slice_in_dim(ids_padded, first_row, window_rows, 0)
        key_valid = lax.dynamic_slice_in_dim(valid_padded, first_row, window_rows, 0)
        query_pos = first_row + jnp.arange(TOK_DEV, dtype=jnp.int32)
        key_pos = first_row - pad_rows + jnp.arange(window_rows, dtype=jnp.int32)
        visible = (key_pos[None, :] <= query_pos[:, None]) & (key_ids[None, :] == query_ids[:, None]) & key_valid[None, :]
        scores = jnp.einsum('thd,whd->htw', query_block, key_block, precision=HIGHEST) * score_scale
        scores = jnp.where(visible[None], low_back(scores), NEGATIVE)
        row_top = lax.optimization_barrier(jnp.max(scores, axis=-1, keepdims=True))
        log_total = jnp.log(lax.optimization_barrier(jnp.sum(jnp.exp(scores - row_top), axis=-1, keepdims=True))) + row_top
        soft_weights = low(jnp.exp(scores - log_total))
        mixed = jnp.einsum('htw,whd->thd', soft_weights, value_block, precision=HIGHEST)
        return mixed.reshape(TOK_DEV, model_width)
    firsts = jnp.arange(total_rows // TOK_DEV, dtype=jnp.int32) * TOK_DEV
    return lax.map(jax.checkpoint(one_block), firsts).reshape(total_rows, model_width)

def forward(resid, small, attend_in, widening, attend_out, narrowing, seq_ids, offsets, valid):
    total_rows, model_width = resid.shape
    head_size = model_width // HEADS
    bias_joint = jnp.concatenate([small[:, 4], small[:, 5], small[:, 6]])
    bias_up = small[:, 9:].reshape(-1)
    normed_one = low(layer_norm(resid, small[:, 0], small[:, 1]))
    normed_two = low(layer_norm(resid, small[:, 2], small[:, 3]))
    joint = low_back(matmul(normed_one, low(attend_in)) + bias_joint)
    queries = joint[:, :model_width].reshape(total_rows, HEADS, head_size)
    keys = joint[:, model_width:2 * model_width].reshape(total_rows, HEADS, head_size)
    queries = low(rotate(queries, offsets).reshape(total_rows, model_width))
    keys = low(rotate(keys, offsets).reshape(total_rows, model_width))
    values = low(joint[:, 2 * model_width:])
    attended = low(low_back(attention(queries, keys, values, seq_ids, valid)))
    branch_attend = matmul(attended, low(attend_out).T) + small[:, 7]
    hidden = low_back(matmul(normed_two, low(widening)) + bias_up)
    activated = low(jax.nn.gelu(hidden, approximate=False))
    branch_mlp = matmul(activated, low(narrowing).T) + small[:, 8]
    return resid + branch_attend + branch_mlp

def adam_step(parameter, gradient, first_moment, second_moment, step_rate):
    first_new = BETA_ONE * first_moment + (1.0 - BETA_ONE) * gradient
    second_new = BETA_TWO * second_moment + (1.0 - BETA_TWO) * gradient * gradient
    first_hat = first_new / (1.0 - BETA_ONE ** STEPS)
    second_hat = second_new / (1.0 - BETA_TWO ** STEPS)
    parameter_new = parameter - step_rate * (first_hat / (jnp.sqrt(second_hat) + ADAM_EPS) + WEIGHT_DECAY * parameter)
    return (first_new, second_new, parameter_new)

def reference(tokens, cotangent, lengths, attend_in, widening, attend_out, narrowing, small_params, first_attend_in, first_widening, first_attend_out, first_narrowing, first_small, second_attend_in, second_widening, second_attend_out, second_narrowing, second_small):
    all_rows = jnp.arange(tokens.shape[0], dtype=jnp.int32)
    seq_ids, offsets, valid = token_places(all_rows, lengths)
    resid = tokens.astype(jnp.float32)

    def wrapped(resid_in, small_in, inner_in, wide_in, outer_in, narrow_in):
        return forward(resid_in, small_in, inner_in, wide_in, outer_in, narrow_in, seq_ids, offsets, valid)
    result, pullback = jax.vjp(wrapped, resid, small_params, attend_in, widening, attend_out, narrowing)
    grads = pullback(cotangent.astype(jnp.float32))
    rate_inner = 2.5 * D ** (-0.5)
    rate_outer = 2.5 * (D * 11 // LMAX) ** (-0.5)
    rate_down = 2.5 * FF ** (-0.5)
    rate_small = 0.5
    mean_in, square_in, new_in = adam_step(attend_in, grads[2], first_attend_in, second_attend_in, rate_inner)
    mean_wide, square_wide, new_wide = adam_step(widening, grads[3], first_widening, second_widening, rate_inner)
    mean_out, square_out, new_out = adam_step(attend_out, grads[4], first_attend_out, second_attend_out, rate_outer)
    mean_narrow, square_narrow, new_narrow = adam_step(narrowing, grads[5], first_narrowing, second_narrowing, rate_down)
    mean_small, square_small, new_small = adam_step(small_params, grads[1], first_small, second_small, rate_small)
    return (result.astype(jnp.bfloat16), grads[0], new_in, new_wide, new_out, new_narrow, new_small, mean_in, mean_wide, mean_out, mean_narrow, mean_small, square_in, square_wide, square_out, square_narrow, square_small)
```

```python
import math

import jax
import jax.numpy as jnp
from jax import lax
from jax.experimental import pallas as pl
from jax.experimental.pallas import tpu as pltpu
from jax.sharding import PartitionSpec as P

D = 2048
HEADS = 8
HEAD = D // HEADS
FF = 8192
FFT = FF // HEADS
LMAX = 4096
STEPS = 10
TOK = 256
RUN = 2 * TOK
BACK_RUNS = LMAX // RUN + 1

NORM_EPS = 1e-05
ADAM_EPS = 1e-08
BETA_ONE = 0.9
BETA_TWO = 0.95
WEIGHT_DECAY = 0.01
NEGATIVE = -1e30
ROPE_BASE = 10000.0
SMALLC = 13
SMALLR = 16

BF = jnp.bfloat16
F32 = jnp.float32
ANY = pl.BlockSpec(memory_space=pl.ANY)
VM = pl.BlockSpec(memory_space=pltpu.VMEM)
MIB = 1024 * 1024
WEIGHTS = ((3, HEAD), (1, FFT), (1, HEAD), (1, FFT))


class Place:
    def __init__(self, n):
        self.n = n
        self.S = n // 4
        self.R = self.S // 2
        self.bits = int(math.log2(self.R))
        me = lax.axis_index("fsdp")
        self.me = me
        self.zt = me // self.S
        self.rr = (me % self.S) // 2
        self.c = me % 2
        self.z1 = self.zt // 2
        self.z0 = self.zt % 2
        self.t = self.zt * 2 + self.c

    def zt_of(self, s):
        z1 = 1 - self.z1 if s & 1 else self.z1
        z0 = 1 - self.z0 if s & 2 else self.z0
        return z1 * 2 + z0

    def zt_of_run(self, u):
        z1 = self.z1 + (1 - 2 * self.z1) * (u % 2)
        z0 = self.z0 + (1 - 2 * self.z0) * (u // 2)
        return z1 * 2 + z0

    def c_of(self, s):
        return 1 - self.c if s & 4 else self.c

    def t_of(self, s):
        return self.zt_of(s) * 2 + self.c_of(s)

    def rr_of(self, i):
        out = 0
        for k in range(self.bits):
            bit = (self.rr // (1 << k)) % 2
            out = out + (1 - bit if i >> k & 1 else bit) * (1 << k)
        return out

    def dev_t(self, s):
        return self.zt_of(s) * self.S + self.rr * 2 + self.c_of(s)

    def dev_r(self, i):
        return self.zt * self.S + self.rr_of(i) * 2 + self.c


class Copies:
    def __init__(self, send, recv):
        self.send, self.recv, self.count, self.started = send, recv, 0, []

    def remote(self, src, dst, dev):
        k = self.count
        self.count += 1
        copy = pltpu.make_async_remote_copy(
            src_ref=src,
            dst_ref=dst,
            send_sem=self.send.at[k],
            recv_sem=self.recv.at[k],
            device_id=(dev,),
            device_id_type=pl.DeviceIdType.MESH,
        )
        copy.start()
        self.started.append(copy)
        return copy

    def local(self, src, dst):
        k = self.count
        self.count += 1
        copy = pltpu.make_async_copy(src, dst, self.send.at[k])
        copy.start()
        return copy

    def finish(self):
        for copy in self.started:
            copy.wait_send()


def greet(place, t_group, r_group):
    barrier = pltpu.get_barrier_semaphore()
    peers = [place.dev_t(s) for s in t_group] + [place.dev_r(i) for i in r_group]
    for dev in peers:
        pl.semaphore_signal(barrier, inc=1, device_id=(dev,), device_id_type=pl.DeviceIdType.MESH)
    pl.semaphore_wait(barrier, len(peers))


def top_bit(s):
    return 1 << (s.bit_length() - 1)


def orders(bits):
    up = [1 << k for k in range(bits)]
    return [up, up[::-1]]


def spread(order):
    have, out = [0], []
    for bit in order:
        new = [i | bit for i in have]
        out += [(i, bit) for i in new]
        have = have + new
    return out


def collected(order):
    left, out = list(range(1 << len(order))), []
    for bit in order:
        out.append((bit, [i for i in left if i & bit]))
        left = [i for i in left if not i & bit]
    return out


def add_rows(dst, a, b):
    lead = dst.shape[:-2]
    rows, columns = dst.shape[-2:]
    size = min(rows, max(16, 1 << int(math.log2(16384 // columns))))
    for flat in range(math.prod(lead)):
        where, rest = [], flat
        for extent in lead[::-1]:
            where.insert(0, rest % extent)
            rest //= extent

        def step(k, carry, where=tuple(where)):
            at = where + (pl.ds(pl.multiple_of(k * size, size), size), slice(None))
            dst[at] = (a[at].astype(F32) + b[at].astype(F32)).astype(dst.dtype)
            return carry

        lax.fori_loop(0, rows // size, step, 0)


def call(kernel, ins, in_specs, outs, out_specs, scratch, collective_id, copies, vmem=60):
    return pl.pallas_call(
        kernel,
        out_shape=outs,
        in_specs=in_specs,
        out_specs=out_specs,
        scratch_shapes=[
            *scratch,
            pltpu.SemaphoreType.DMA((copies,)),
            pltpu.SemaphoreType.DMA((copies,)),
        ],
        compiler_params=pltpu.CompilerParams(
            collective_id=collective_id, has_side_effects=True, vmem_limit_bytes=vmem * MIB
        ),
    )(*ins)


class Net:
    def __init__(self, send, recv):
        self.send, self.recv, self.makers, self.count = send, recv, [], 0

    def add(self, maker, many=1):
        base = self.count
        self.count += many

        def build(k=0):
            src, dst, dev = maker(k)
            return pltpu.make_async_remote_copy(
                src_ref=src,
                dst_ref=dst,
                send_sem=self.send.at[base + k],
                recv_sem=self.recv.at[base + k],
                device_id=(dev,),
                device_id_type=pl.DeviceIdType.MESH,
            )

        self.makers.append((build, many))
        return build

    def finish(self):
        for build, many in self.makers:
            if many == 1:
                build().wait_send()
            else:

                def one(k, carry, build=build):
                    build(k).wait_send()
                    return carry

                lax.fori_loop(0, many, one, 0)


class GatherT:
    def __init__(self, net, place, own, out):
        self.ops = {}
        for s in range(1, 8):
            hop = top_bit(s)
            src = own if s == hop else out.at[(s - hop) // 4, (s - hop) % 4]
            self.ops[s] = net.add(
                lambda k, src=src, s=s, hop=hop: (src, out.at[s // 4, s % 4], place.dev_t(hop))
            )

    def start(self, *which):
        for s in which:
            self.ops[s]().start()

    def wait(self, *which):
        for s in which:
            self.ops[s]().wait_recv()


class GatherR:
    def __init__(self, net, place, region, order):
        self.plan = spread(order)
        self.ops = {}
        self.later = [(i, bit) for i, bit in self.plan if i != bit]
        self.used = {i ^ bit for i, bit in self.later}
        for i, bit in self.plan:
            self.ops[i] = net.add(
                lambda k, i=i, bit=bit: (region(i ^ bit), region(i ^ bit), place.dev_r(bit))
            )

    def begin(self):
        for i, bit in self.plan:
            if i == bit:
                self.ops[i]().start()

    def advance(self):
        seen = set()
        for i, bit in self.later:
            if i ^ bit not in seen:
                self.ops[i ^ bit]().wait_recv()
                seen.add(i ^ bit)
            self.ops[i]().start()

    def end(self):
        for i, _ in self.plan:
            if i not in self.used:
                self.ops[i]().wait_recv()


def cosine_and_sine(x):
    turns = jnp.floor(x * (2.0 / math.pi) + 0.5)
    r = ((x - turns * 1.5703125) - turns * 4.837512969970703e-4) - turns * 7.549789954891882e-8
    z = r * r
    sine = ((-1.9515295891e-4 * z + 8.3321608736e-3) * z - 1.6666654611e-1) * z * r + r
    cosine = (
        ((2.443315711809948e-5 * z - 1.388731625493765e-3) * z + 4.166664568298827e-2) * z * z
        - 0.5 * z
        + 1.0
    )
    quarter = turns - 4.0 * jnp.floor(turns * 0.25)
    odd = (quarter == 1.0) | (quarter == 3.0)
    first, second = jnp.where(odd, sine, cosine), jnp.where(odd, cosine, sine)
    return (
        jnp.where((quarter == 1.0) | (quarter == 2.0), -first, first),
        jnp.where(quarter >= 2.0, -second, second),
    )


def shuffle_matrix():
    turned, half = HEAD // 8, HEAD // 2
    into = lax.broadcasted_iota(jnp.int32, (HEAD, HEAD), 1)
    source = lax.broadcasted_iota(jnp.int32, (HEAD, HEAD), 0)
    moved = jnp.where((into >= turned) & (into < half), into + turned, into)
    moved = jnp.where((into >= half) & (into < half + turned), into - (half - turned), moved)
    return jnp.where(source == moved, 1.0, 0.0).astype(F32)


def weight_halves(net, place, ref):
    both = orders(place.bits)
    return [
        GatherR(net, place, lambda i, h=h: ref.at[pl.ds(2 * h, 2), place.rr_of(i)], both[h])
        for h in range(2)
    ]


def forward_kernel(
    n, nseq, x, gy, wi, wu, wo, wd, small, lengths, frequency,
    xg, gg, a1g, a2g, oi, ou, oo, od, qo, kg, vg, zo, dho, dout, smt, sums, stats, cosine, sine,
    xv, gv, sm, ti, tu, to, td, slope, a2v, kt, vt, at, ztile, dht, bias, dhsum,
    send, recv, local, out_sem, g_sem,
):
    place = Place(n)
    rb = D // n
    net = Net(send, recv)
    weights = list(zip((wi, wu, wo, wd), (ti, tu, to, td), WEIGHTS))
    greet(place, range(1, 8), [1 << k for k in range(place.bits)])
    mine = pl.ds(pl.multiple_of(place.c * rb, rb), rb)

    small_t = [
        net.add(lambda k, s=s: (small, sm.at[place.zt, place.rr, mine, :], place.dev_t(s)))
        for s in range(1, 8)
    ]

    def columns(p, width, t):
        return pl.ds(pl.multiple_of(p * D + t * width, 128), width)

    def exchange(which):
        src, dst, (parts, width) = weights[which]
        return [
            net.add(
                lambda k, s=s, p=p: (
                    src.at[:, columns(p, width, place.t_of(s))],
                    dst.at[place.zt, place.rr, mine, pl.ds(p * width, width)],
                    place.dev_t(s),
                )
            )
            for s in range(1, 8)
            for p in range(parts)
        ]

    to_t = [exchange(k) for k in range(4)]
    small_r = GatherR(net, place, lambda i: sm.at[:, place.rr_of(i)], orders(place.bits)[0])
    to_r = [weight_halves(net, place, w[1]) for w in weights]
    x_t = GatherT(net, place, x, xv)
    g_t = GatherT(net, place, gy, gv)
    both = orders(place.bits)
    keys = []
    for own, out, order in ((kt, kg, both[0]), (vt, vg, both[1])):
        ops = {}
        for i, bit in spread(order):
            ops[i] = net.add(
                lambda s, i=i, bit=bit, own=own, out=out: (
                    own.at[s // 4, s % 4] if i == bit else out.at[i ^ bit, s // 4, s % 4],
                    out.at[i, s // 4, s % 4],
                    place.dev_r(bit),
                ),
                8,
            )
        keys.append((ops, spread(order)))

    def start(ops):
        for op in ops:
            op().start()

    def wait(ops):
        for op in ops:
            op().wait_recv()

    locals_ = [
        pltpu.make_async_copy(x, xv.at[0, 0], local.at[0]),
        pltpu.make_async_copy(gy, gv.at[0, 0], local.at[1]),
        pltpu.make_async_copy(small, sm.at[place.zt, place.rr, mine, :], local.at[2]),
    ]
    for src, dst, (parts, width) in weights:
        for p in range(parts):
            locals_.append(
                pltpu.make_async_copy(
                    src.at[:, columns(p, width, place.t)],
                    dst.at[place.zt, place.rr, mine, pl.ds(p * width, width)],
                    local.at[len(locals_)],
                )
            )
    for copy in locals_:
        copy.start()
    start(small_t)
    start(to_t[0])
    x_t.start(4)
    for copy in locals_:
        copy.wait()
    wait(small_t)
    small_r.begin()
    wait(to_t[0])
    for part in to_r[0]:
        part.begin()
    start(to_t[1])
    x_t.start(2, 1)
    small_r.advance()
    for part in to_r[0]:
        part.advance()

    def tables(s, carry):
        core, u = s // 4, s % 4
        device = (
            place.zt_of_run(u) * place.S + place.rr * 2 + place.c + (1 - 2 * place.c) * core
        )
        token = device * TOK + lax.broadcasted_iota(jnp.int32, (TOK, HEAD // 2), 0)
        offset = token - start_of(token, lengths, nseq)
        angles = offset.astype(F32) * frequency[0:1, :]
        cosine[core, u], sine[core, u] = cosine_and_sine(angles)
        return carry

    lax.fori_loop(0, 8, tables, 0)
    wait(to_t[1])
    for part in to_r[1]:
        part.begin()
    start(to_t[3])
    start(to_t[2])
    small_r.end()

    smt[...] = sm[...].reshape(D, 128).T[:SMALLR, :]
    head_cols = pl.ds(pl.multiple_of(place.t * HEAD, HEAD), HEAD)
    shuffle = shuffle_matrix()
    three = jnp.dot(
        smt[0:8, head_cols], shuffle, precision=lax.Precision.HIGHEST, preferred_element_type=F32
    )
    for p in range(2):
        bias[0:1, p * HEAD : (p + 1) * HEAD] = three[4 + p : 5 + p, :]
    bias[0:1, 2 * HEAD : 3 * HEAD] = smt[6:7, head_cols]

    def repeat_matrix():
        lane = lax.broadcasted_iota(jnp.int32, (HEAD, FFT), 1)
        row = lax.broadcasted_iota(jnp.int32, (HEAD, FFT), 0)
        return jnp.where(lane // 4 == row, 1.0, 0.0).astype(F32)

    four = jnp.dot(
        smt[8:16, head_cols],
        repeat_matrix(),
        precision=lax.Precision.HIGHEST,
        preferred_element_type=F32,
    )
    lane8 = lax.broadcasted_iota(jnp.int32, (8, FFT), 1)
    row8 = lax.broadcasted_iota(jnp.int32, (8, FFT), 0)
    bias[1:2, :] = jnp.sum(jnp.where(lane8 % 4 + 1 == row8, four, 0.0), axis=0, keepdims=True)

    for part in to_r[0]:
        part.end()
    copy_out = [pltpu.make_async_copy(ti, oi, local.at[0])]
    copy_out[0].start()

    def norms(u):
        def chunk(r, carry):
            at_rows = (r // 16, pl.ds(pl.multiple_of(r % 16 * 16, 16), 16), slice(None))
            in_rows = (at_rows[0], u, *at_rows[1:])
            xf = xv[in_rows].astype(F32)
            average = jnp.mean(xf, axis=1, keepdims=True)
            centred = xf - average
            var = jnp.mean(centred * centred, axis=1, keepdims=True)
            inverse = lax.rsqrt(var + NORM_EPS)
            xhat = centred * inverse
            at[at_rows] = (xhat * smt[0:1, :] + smt[1:2, :]).astype(BF)
            a2v[in_rows] = (xhat * smt[2:3, :] + smt[3:4, :]).astype(BF)
            lanes = lax.broadcasted_iota(jnp.int32, (16, 128), 1)
            stats[in_rows] = jnp.where(lanes == 0, average, inverse)
            return carry

        lax.fori_loop(0, 2 * TOK // 16, chunk, 0, unroll=4)

    def place_of(k):
        return k % 2 * 2 + k // 2

    def events(k, table):
        for when, what in table.items():

            @pl.when(k == when)
            def _(what=what):
                for fn in what:
                    fn()

    def staged(buffer, out, u, sem):
        return pltpu.make_async_copy(buffer, out.at[:, u], out_sem.at[sem])

    def free(buffer, out, k, sem):
        @pl.when(k >= 1)
        def _():
            staged(buffer, out, 0, sem).wait()

    def forward_keys(s):
        for ops, plan in keys:
            seen = set()
            for i, bit in plan:
                if i != bit:
                    if i ^ bit not in seen:
                        ops[i ^ bit](s).wait_recv()
                        seen.add(i ^ bit)
                    ops[i](s).start()

    def hidden_units(k):
        u = place_of(k)
        hidden = jnp.dot(
            a2v[:, u].reshape(RUN, D), tu[...].reshape(D, FFT), preferred_element_type=F32
        )
        slope[:, u] = (hidden + bias[1:2, :]).reshape(2, TOK, FFT)
        free(ztile, zo, k, 1)

        def chunk(r, carry):
            at_rows = (r // 16, pl.ds(pl.multiple_of(r % 16 * 16, 16), 16), slice(None))
            in_rows = (at_rows[0], u, *at_rows[1:])
            h = slope[in_rows]
            bell = jnp.exp(-0.5 * h * h)
            t = 1.0 / (1.0 + (0.3275911 * 0.5**0.5) * jnp.abs(h))
            series = t * (
                0.254829592
                + t * (-0.284496736 + t * (1.421413741 + t * (-1.453152027 + t * 1.061405429)))
            )
            tail = 0.5 * series * bell
            phi = jnp.where(h < 0.0, tail, 1.0 - tail)
            ztile[at_rows] = (h * phi).astype(BF)
            slope[in_rows] = phi + h * bell * (1.0 / math.sqrt(2.0 * math.pi))
            return carry

        lax.fori_loop(0, 2 * TOK // 16, chunk, 0, unroll=2)
        staged(ztile, zo, u, 1).start()

    def projections(k):
        u = place_of(k)
        free(at, a1g, k, 0)
        norms(u)
        joint = (
            jnp.dot(
                at[...].reshape(RUN, D), ti[...].reshape(D, 3 * HEAD), preferred_element_type=F32
            )
            + bias[0:1, : 3 * HEAD]
        )
        staged(at, a1g, u, 0).start()
        half = HEAD // 2
        cs, sn = cosine[:, u].reshape(RUN, half), sine[:, u].reshape(RUN, half)
        for p, (dst, scale) in enumerate(((qo, HEAD**-0.5), (kt, None))):
            one = joint[:, p * HEAD : p * HEAD + half]
            two = joint[:, p * HEAD + half : (p + 1) * HEAD]
            for at_col, value in ((0, one * cs - two * sn), (half, two * cs + one * sn)):
                value = value.astype(BF)
                if scale is not None:
                    value = (value.astype(F32) * scale).astype(BF)
                dst[:, u, :, at_col : at_col + half] = value.reshape(2, TOK, half)
        vt[:, u] = joint[:, 2 * HEAD :].astype(BF).reshape(2, TOK, HEAD)
        for core in range(2):
            for ops, plan in keys:
                for i, bit in plan:
                    if i == bit:
                        ops[i](core * 4 + u).start()

    def first(k, carry):
        events(
            k,
            {
                0: [lambda: x_t.wait(4)],
                1: [
                    lambda: [p.advance() for p in to_r[1]],
                    lambda: x_t.wait(2),
                    lambda: x_t.start(6),
                    lambda: x_t.wait(6),
                ],
                2: [
                    lambda: x_t.wait(1),
                    lambda: x_t.start(3, 5),
                    lambda: [p.end() for p in to_r[1]],
                    lambda: pltpu.make_async_copy(tu, ou, local.at[1]).start(),
                ],
                3: [
                    lambda: wait(to_t[3]),
                    lambda: wait(to_t[2]),
                    lambda: [p.begin() for p in to_r[3] + to_r[2]],
                    lambda: g_t.start(1, 4),
                ],
                4: [lambda: x_t.wait(5)],
                5: [
                    lambda: [p.advance() for p in to_r[3] + to_r[2]],
                    lambda: x_t.wait(3),
                    lambda: x_t.start(7),
                    lambda: g_t.start(2),
                    lambda: x_t.wait(7),
                ],
                7: [lambda: g_t.wait(1), lambda: g_t.start(3, 5)],
            },
        )
        late = k // 4

        @pl.when(k % 4 < 2)
        def _():
            projections(k - 2 * late)

        @pl.when(k % 4 >= 2)
        def _():
            hidden_units(k - 2 - 2 * late)

        @pl.when((k == 3) | (k >= 5))
        def _():
            pair = k - 3 - late
            for core in range(2):
                forward_keys(core * 4 + place_of(pair))

        return carry

    lax.fori_loop(0, 8, first, 0)
    own_out = [
        pltpu.make_async_copy(kt, kg.at[0], local.at[4]),
        pltpu.make_async_copy(vt, vg.at[0], local.at[5]),
        pltpu.make_async_copy(xv, xg, local.at[6]),
        pltpu.make_async_copy(a2v, a2g, local.at[8]),
    ]
    for copy in own_out:
        copy.start()
    copy_out.append(pltpu.make_async_copy(tu, ou, local.at[1]))

    def finish_keys(s, carry):
        for ops, plan in keys:
            used = {i ^ bit for i, bit in plan if i != bit}
            for i, bit in plan:
                if i not in used:
                    ops[i](s).wait_recv()
        return carry

    for part in to_r[3] + to_r[2]:
        part.end()
    copy_out += [
        pltpu.make_async_copy(to, oo, local.at[2]),
        pltpu.make_async_copy(td, od, local.at[3]),
    ]
    copy_out[2].start()
    copy_out[3].start()
    dhsum[...] = jnp.zeros_like(dhsum)

    def third(k, carry):
        u = place_of(k)
        events(
            k,
            {
                0: [lambda: g_t.wait(4)],
                1: [lambda: g_t.wait(2), lambda: g_t.start(6), lambda: g_t.wait(6)],
                2: [lambda: g_t.wait(5)],
                3: [lambda: g_t.wait(3), lambda: g_t.start(7), lambda: g_t.wait(7)],
            },
        )
        free(dht, dho, k, 2)
        pltpu.make_async_copy(gv.at[:, u], gg.at[:, u], g_sem.at[u]).start()
        grad = gv[:, u].reshape(RUN, D)
        dz = jnp.dot(grad, td[...].reshape(D, FFT), preferred_element_type=F32)
        dh = (dz * slope[:, u].reshape(RUN, FFT)).astype(BF)
        dht[...] = dh.reshape(2, TOK, FFT)
        staged(dht, dho, u, 2).start()
        dhsum[0:1, :] += jnp.sum(dh.astype(F32), axis=0, keepdims=True)
        dout[:, u] = (
            jnp.dot(grad, to[...].reshape(D, HEAD), preferred_element_type=F32)
            .astype(BF)
            .reshape(2, TOK, HEAD)
        )
        return carry

    lax.fori_loop(0, 4, third, 0)
    four = jnp.dot(
        jnp.where(lane8 % 4 + 1 == row8, dhsum[0:1, :], 0.0),
        repeat_matrix().T,
        precision=lax.Precision.HIGHEST,
        preferred_element_type=F32,
    )
    sums[...] = jnp.zeros_like(sums)
    sums[8:16, head_cols] = four
    sums[8:9, :] = jnp.sum(gv[0, 0].astype(F32), axis=0, keepdims=True)
    sums[7:8, :] = sums[8:9, :]
    lax.fori_loop(0, 8, finish_keys, 0)
    for sem, (buffer, out) in enumerate(((at, a1g), (ztile, zo), (dht, dho))):
        staged(buffer, out, 0, sem).wait()
    for copy in copy_out + own_out:
        copy.wait()
    for u in range(4):
        pltpu.make_async_copy(gv.at[:, u], gg.at[:, u], g_sem.at[u]).wait()
    net.finish()


def forward(n, x, gy, weights, small, lengths, frequency):
    rb = D // n
    R = n // 8

    def shape(*dims, kind=BF):
        return jax.ShapeDtypeStruct(dims, kind)

    w_shapes = [(4, R, 2 * rb, parts * width) for parts, width in WEIGHTS]
    block, cols, head = (2, 4, TOK, D), (2, 4, TOK, FFT), (2, 4, TOK, HEAD)
    outs = [shape(*block) for _ in range(4)]
    outs += [shape(*w) for w in w_shapes]
    outs += [shape(*head), shape(R, *head), shape(R, *head), shape(*cols), shape(*cols)]
    outs += [shape(*head), shape(SMALLR, D, kind=F32), shape(SMALLR, D, kind=F32)]
    outs += [shape(2, 4, TOK, 128, kind=F32)]
    outs += [shape(2, 4, TOK, HEAD // 2, kind=F32) for _ in range(2)]
    out_specs = [ANY] * 8 + [VM] + [ANY] * 4 + [VM] * 6
    scratch = [
        pltpu.VMEM(block, BF),
        pltpu.VMEM(block, BF),
        pltpu.VMEM((4, R, 2 * rb, 128), F32),
        *[pltpu.VMEM(w, BF) for w in w_shapes],
        pltpu.VMEM(cols, F32),
        pltpu.VMEM(block, BF),
        pltpu.VMEM(head, BF),
        pltpu.VMEM(head, BF),
        pltpu.VMEM((2, TOK, D), BF),
        pltpu.VMEM((2, TOK, FFT), BF),
        pltpu.VMEM((2, TOK, FFT), BF),
        pltpu.VMEM((8, FFT), F32),
        pltpu.VMEM((8, FFT), F32),
    ]
    copies = 7 + 7 * 6 + (R - 1) * (1 + 8 + 2 * 8) + 14

    def kernel(*refs):
        forward_kernel(n, lengths.shape[0], *refs)

    return pl.pallas_call(
        kernel,
        out_shape=outs,
        in_specs=[ANY] * 7 + [pl.BlockSpec(memory_space=pltpu.SMEM), VM],
        out_specs=out_specs,
        scratch_shapes=[
            *scratch,
            pltpu.SemaphoreType.DMA((copies,)),
            pltpu.SemaphoreType.DMA((copies,)),
            pltpu.SemaphoreType.DMA((16,)),
            pltpu.SemaphoreType.DMA((3,)),
            pltpu.SemaphoreType.DMA((4,)),
        ],
        compiler_params=pltpu.CompilerParams(
            collective_id=0, has_side_effects=True, vmem_limit_bytes=62 * MIB
        ),
    )(x, gy, *weights, small, lengths, frequency)


class SumT:
    def __init__(self, copies, place, data, slots, out):
        self.copies, self.place, self.data, self.slots, self.out = copies, place, data, slots, out
        self.ops = {}
        self.cur = {s: data.at[s] for s in range(8)}

    def send(self, s):
        hop = top_bit(s)
        self.ops[s] = self.copies.remote(self.cur[s], self.slots.at[s - 1], self.place.dev_t(hop))

    def add(self, s):
        to = s - top_bit(s)
        self.ops[s].wait_recv()
        slot = self.slots.at[s - 1]
        if to == 0 and s == 1:
            add_rows(self.out, self.cur[0], slot)
        else:
            add_rows(slot, self.cur[to], slot)
            self.cur[to] = slot

    def start(self):
        for s in (6, 7, 5, 4):
            self.send(s)

    def middle(self):
        for s in (6, 7):
            self.add(s)
            self.send(s - 4)
        self.add(5)

    def late(self):
        self.add(3)
        self.send(1)
        self.add(4)
        self.add(2)

    def end(self):
        self.add(1)


class SumR:
    def __init__(self, copies, place, piece, slots, order):
        self.copies, self.place, self.slots = copies, place, slots
        self.steps = collected(order)
        self.cur = {i: piece(i) for i in range(1 << len(order))}
        self.ops = {}

    def send(self, step):
        bit, members = self.steps[step]
        for i in members:
            self.ops[i] = self.copies.remote(
                self.cur[i], self.slots.at[i - 1], self.place.dev_r(bit)
            )

    def add(self, step):
        bit, members = self.steps[step]
        for i in members:
            self.ops[i].wait_recv()
            slot = self.slots.at[i - 1]
            add_rows(slot, self.cur[i ^ bit], slot)
            self.cur[i ^ bit] = slot


def return_keys_kernel(n, have, *refs):
    place = Place(n)
    refs = list(refs)
    count = len(have)
    ins, refs = refs[:count], refs[count:]
    outs, refs = refs[:count], refs[count:]
    slots, (send, recv) = refs[:count], refs[count:]
    copies = Copies(send, recv)
    both = orders(place.bits)
    r_group = [1 << b for b in range(place.bits)] if set(have) - {"p"} else []
    t_group = (1, 2, 4) if "p" in have else ()
    greet(place, t_group, r_group)
    total, sums = None, []
    for name, src, dst, slot in zip(have, ins, outs, slots):
        if name == "p":
            total = SumT(copies, place, src, slot, dst)
        else:
            order = both[0] if name == "k" else both[1]
            sums.append((SumR(copies, place, lambda i, src=src: src.at[i], slot, order), dst))
    for part, _ in sums:
        part.send(0)
    if total:
        total.start()
        total.middle()
    for step in range(place.bits):
        for part, _ in sums:
            part.add(step)
            if step + 1 < place.bits:
                part.send(step + 1)
    if total:
        total.late()
    for part, dst in sums:
        copy = copies.local(part.cur[0], dst)
        copy.wait()
    if total:
        total.end()
    copies.finish()


def return_keys(n, ins, collective_id):
    R = n // 8
    outs, scratch, copies = [], [], 0
    for name in ins:
        if name == "p":
            outs.append(jax.ShapeDtypeStruct((TOK, D), F32))
            scratch.append(pltpu.VMEM((7, TOK, D), BF))
            copies += 7
        else:
            outs.append(jax.ShapeDtypeStruct((8, TOK, HEAD), BF))
            scratch.append(pltpu.VMEM((R - 1, 8, TOK, HEAD), BF))
            copies += R

    def kernel(*refs):
        return_keys_kernel(n, tuple(ins), *refs)

    out = call(
        kernel,
        tuple(ins.values()),
        [VM] * len(ins),
        outs,
        [VM] * len(ins),
        scratch,
        collective_id,
        copies,
    )
    return dict(zip(ins, out))


def return_grads_kernel(
    n, gi, gu, go, gd, e, small, oi, ou, oo, od, oe, osmall, si, su, so, sd, se, ss, send, recv
):
    place = Place(n)
    copies = Copies(send, recv)
    rb = D // n
    both = orders(place.bits)
    greet(place, range(1, 8), [1 << b for b in range(place.bits)])
    total = SumT(copies, place, e, se, oe)
    total.start()

    tasks = []
    for src, slot, dst, (parts, width) in zip(
        (gu, gd, gi, go), (su, sd, si, so), (ou, od, oi, oo), [WEIGHTS[k] for k in (1, 3, 0, 2)]
    ):
        for half in range(2):

            def piece(i, src=src, half=half):
                return src.at[pl.ds(2 * half, 2), place.rr_of(i)]

            part = SumR(copies, place, piece, slot.at[half], both[half])
            tasks.append((part, half, dst, parts, width))
    small_sum = SumR(copies, place, lambda i: small.at[:, place.rr_of(i)], ss, both[0])
    for part, *_ in tasks:
        part.send(0)
    small_sum.send(0)
    total.middle()
    for step in range(place.bits):
        for part, *_ in tasks:
            part.add(step)
            if step + 1 < place.bits:
                part.send(step + 1)
        small_sum.add(step)
        if step + 1 < place.bits:
            small_sum.send(step + 1)
    total.late()

    finals = {}
    for k in range(4):
        pieces = [tasks[2 * k + half][0].cur[0] for half in range(2)]
        finals[k] = pieces
    ops = []
    for k in range(4):
        _, _, dst, parts, width = tasks[2 * k]
        for zz in range(4):
            for cc in range(2):
                src = finals[k][zz // 2].at[zz % 2, pl.ds(cc * rb, rb), :]
                ops.append((zz, cc, src, dst, parts, width))
    sends = []
    for k in range(4):
        _, _, dst, parts, width = tasks[2 * k]
        store = tasks[2 * k][0].slots
        slot = store
        del slot
        for s in range(8):
            for p in range(parts):
                cols = pl.ds(pl.multiple_of(p * D + place.t * width, 128), width)
                sends.append((k, s, p, cols, dst, width))
    remote = []
    joined = {}
    for k, (ref, outbuf) in enumerate(((gu, ou), (gd, od), (gi, oi), (go, oo))):
        del ref, outbuf
        joined[k] = finals[k]
    for k, s, p, cols, dst, width in sends:
        base = (su, sd, si, so)[k]
        last = tasks[2 * k][0].steps[-1][1][0], tasks[2 * k + 1][0].steps[-1][1][0]
        zt = place.zt_of(s)
        rows = pl.ds(pl.multiple_of(place.c_of(s) * rb, rb), rb)
        which = zt // 2
        index = (1 - which) * (last[0] - 1) + which * (last[1] - 1)
        src = base.at[which, index, zt % 2, rows, pl.ds(p * width, width)]
        if s == 0:
            remote.append(("local", copies.local(src, dst.at[:, cols])))
        else:
            remote.append(("remote", copies.remote(src, dst.at[:, cols], place.dev_t(s))))
    last = small_sum.steps[-1][1][0] - 1
    for s in range(8):
        rows = pl.ds(pl.multiple_of(place.c_of(s) * SMALLR, SMALLR), SMALLR)
        src = ss.at[last, place.zt_of(s), rows, :]
        if s == 0:
            remote.append(("local", copies.local(src, osmall.at[place.t])))
        else:
            remote.append(("remote", copies.remote(src, osmall.at[place.t], place.dev_t(s))))
    total.end()
    for kind, copy in remote:
        if kind == "local":
            copy.wait()
        else:
            copy.wait_recv()
    copies.finish()


def return_grads(n, grads, e, small, collective_id):
    R = n // 8
    rb = D // n
    outs = [jax.ShapeDtypeStruct((rb, parts * D if parts > 1 else HEADS * width), BF) for parts, width in WEIGHTS]
    outs += [jax.ShapeDtypeStruct((TOK, D), F32), jax.ShapeDtypeStruct((8, SMALLR, 128), F32)]
    scratch = [
        pltpu.VMEM((2, R - 1, 2, 2 * rb, parts * width), BF) for parts, width in WEIGHTS
    ] + [
        pltpu.VMEM((7, TOK, D), BF),
        pltpu.VMEM((R - 1, 4, 2 * SMALLR, 128), F32),
    ]
    copies = 7 + 9 * (R - 1) + 8 * 6 + 8

    def kernel(*refs):
        return_grads_kernel(n, *refs)

    return call(
        kernel,
        (*grads, e, small),
        [VM] * 6,
        outs,
        [ANY] * 4 + [VM, ANY],
        scratch,
        collective_id,
        copies,
    )


WIDE = 512


class FoldT:
    def __init__(self, net, place, data, cs, zs, ys, out):
        self.data, self.cs, self.zs, self.ys, self.out = data, cs, zs, ys, out
        self.hop_c = net.add(lambda k: (data.at[k], cs.at[k], place.dev_t(4)), 4)
        self.hop_z0 = net.add(lambda k: (cs.at[2 + k], zs.at[k], place.dev_t(2)), 2)
        self.hop_z1 = net.add(lambda k: (zs.at[1], ys.at[0], place.dev_t(1)))

    @staticmethod
    def order(idx):
        return 7 - idx // 4 - 2 * (idx % 4)

    def loop(self, make, emit, after):
        def step(idx, carry):
            s = self.order(idx)
            make(s, idx)
            k = s % 4

            def far(where, value):
                self.data[(k, *where)] = value.astype(BF)

            def near(where, value):
                self.cs[(k, *where)] = (value + self.cs[(k, *where)].astype(F32)).astype(BF)

            @pl.when(s >= 4)
            def _():
                emit(s, idx, far)
                self.hop_c(k).start()

            @pl.when(s < 4)
            def _():
                self.hop_c(k).wait_recv()
                emit(s, idx, near)

                @pl.when(s >= 2)
                def _():
                    self.hop_z0(s - 2).start()

            after(idx)
            return carry

        lax.fori_loop(0, 8, step, 0)

    def turn_z1(self):
        self.hop_z0(1).wait_recv()
        add_rows(self.zs.at[1], self.cs.at[1], self.zs.at[1])
        self.hop_z1().start()

    def turn_own(self):
        self.hop_z0(0).wait_recv()
        add_rows(self.zs.at[0], self.cs.at[0], self.zs.at[0])

    def end(self):
        self.hop_z1().wait_recv()
        add_rows(self.out, self.zs.at[0], self.ys.at[0])


def fold_scratch():
    return [
        pltpu.VMEM((4, TOK, D), BF),
        pltpu.VMEM((4, TOK, D), BF),
        pltpu.VMEM((2, TOK, D), BF),
        pltpu.VMEM((1, TOK, D), BF),
    ]


class FoldR:
    def __init__(self, net, place, far, own, slots, order):
        one, two = order
        self.own, self.slots = own, slots
        self.both = net.add(lambda k: (far(3), slots.at[0], place.dev_r(one)))
        self.first = net.add(lambda k: (far(one), slots.at[1], place.dev_r(one)))
        self.second = net.add(lambda k: (slots.at[0], slots.at[2], place.dev_r(two)))

    def begin(self):
        self.both().start()
        self.first().start()

    def advance(self):
        self.both().wait_recv()
        add_rows(self.slots.at[0], self.own.at[1], self.slots.at[0])
        self.second().start()

    def gather(self):
        self.first().wait_recv()
        add_rows(self.slots.at[1], self.own.at[0], self.slots.at[1])

    def end(self, out=None):
        self.second().wait_recv()
        out = self.slots.at[2] if out is None else out
        add_rows(out, self.slots.at[1], self.slots.at[2])


def weight_folds(n, net, place, grads, own, slots):
    view = grads.reshape(4, n // 8, 2 * (D // n), grads.shape[-1])
    both = orders(2)
    halves, pieces = [], []
    for h in range(2):

        def piece(i, h=h):
            return view.at[pl.ds(2 * h, 2), place.rr_of(i)]

        halves.append(FoldR(net, place, piece, own.at[h], slots.at[h], both[h]))
        pieces.append((piece(0), own.at[h, 0]))
        pieces.append((piece(both[h][1]), own.at[h, 1]))
    return halves, pieces


def gradient_tiles(lhs, tiles, sem, products):
    wide = tiles.shape[-1]
    count = D // wide

    def fetch(f):
        cols = pl.ds(pl.multiple_of(f * wide, wide), wide)
        return pltpu.make_async_copy(lhs.at[:, :, cols], tiles.at[f % 2], sem.at[f % 2])

    def put(f, stage, out, sems):
        rows = pl.ds(pl.multiple_of(f * wide, wide), wide)
        return pltpu.make_async_copy(stage.at[f % 2], out.at[rows, :], sems.at[f % 2])

    fetch(0).start()

    def step(f, carry):
        fetch(f).wait()

        @pl.when(f + 1 < count)
        def _():
            fetch(f + 1).start()

        left = tiles[f % 2].reshape(8 * TOK, wide)
        for rhs, stage, out, sems in products:

            @pl.when(f >= 2)
            def _(stage=stage, out=out, sems=sems):
                put(f - 2, stage, out, sems).wait()

            right = rhs[...].reshape(8 * TOK, rhs.shape[-1])
            stage[f % 2] = contract_rows(left, right).astype(BF)
            put(f, stage, out, sems).start()
        return carry

    lax.fori_loop(0, count, step, 0)
    for f in (count - 2, count - 1):
        for _, stage, out, sems in products:
            put(f, stage, out, sems).wait()


def half_fold(net, place, grads, h, own, slots):
    order = orders(2)[h]
    cols = pl.ds(h * (FFT // 2), FFT // 2)

    def piece(i):
        return grads.at[:, place.rr_of(i), :, cols]

    fold = FoldR(net, place, piece, own, slots, order)
    return fold, [(piece(0), own.at[0]), (piece(order[1]), own.at[1])]


def return_one_kernel(
    n, dk, dv, o, z, w_out, w_down, gy, a2, dh,
    p_own, dk_own, dv_own, up_sum, g_out, g_down, g_up,
    zov, wdo, dhv, kown, vown, data, cs, zs, ys, ks, vs, tiles, st_wide, st_head, uown, us,
    send, recv, load, fetch_sem, put_sem, near,
):
    place = Place(n)
    net = Net(send, recv)
    greet(place, (1, 2, 4), (1, 2))
    both = orders(2)
    keys = FoldR(net, place, lambda i: dk.at[i], kown, ks, both[0])
    values = FoldR(net, place, lambda i: dv.at[i], vown, vs, both[1])
    total = FoldT(net, place, data, cs, zs, ys, p_own)
    up, pieces = half_fold(
        net, place, g_up.reshape(4, n // 8, 2 * (D // n), FFT), 0, uown, us
    )
    keys.both().start()
    values.both().start()

    loads = [
        pltpu.make_async_copy(src, dst, load.at[k])
        for k, (src, dst) in enumerate(
            (
                (z, zov.at[:, :, :FFT]),
                (o, zov.at[:, :, FFT:]),
                (w_down, wdo.at[:, :FFT]),
                (w_out, wdo.at[:, FFT:]),
                (dk.at[2], kown.at[1]),
                (dv.at[1], vown.at[1]),
                (dk.at[0], kown.at[0]),
                (dv.at[0], vown.at[0]),
                (dh, dhv),
            )
        )
    ]
    for copy in loads:
        copy.start()
    for copy in loads[:4]:
        copy.wait()

    def make(s, idx):
        del s, idx

    def emit(s, idx, put):
        put((slice(None), slice(None)), contract_cols(zov[s], wdo[...]))

    def after(idx):
        @pl.when(idx == 3)
        def _():
            keys.first().start()
            values.first().start()

        @pl.when(idx == 6)
        def _():
            for copy in loads[4:]:
                copy.wait()
            keys.advance()
            values.advance()

    total.loop(make, emit, after)
    total.turn_z1()
    gradient_tiles(a2, tiles, fetch_sem, [(dhv, st_wide, g_up, put_sem.at[0])])
    own_loads = [
        pltpu.make_async_copy(src, dst, near.at[k]) for k, (src, dst) in enumerate(pieces)
    ]
    up.begin()
    for copy in own_loads:
        copy.start()
    keys.gather()
    values.gather()
    gradient_tiles(
        gy, tiles, fetch_sem,
        [
            (zov.at[:, :, :FFT], st_wide, g_down, put_sem.at[0]),
            (zov.at[:, :, FFT:], st_head, g_out, put_sem.at[1]),
        ],
    )
    for copy in own_loads:
        copy.wait()
    up.advance()
    keys.end(dk_own)
    values.end(dv_own)
    total.turn_own()
    up.gather()
    up.end(up_sum)
    total.end()
    net.finish()


def return_one(n, dk, dv, o, z, w_out, w_down, gy, a2, dh):
    rows = 2 * (D // n)
    head, cols = (8, TOK, HEAD), (8, TOK, FFT)
    half = (4, rows, FFT // 2)
    outs = [
        jax.ShapeDtypeStruct((TOK, D), F32),
        jax.ShapeDtypeStruct(head, BF),
        jax.ShapeDtypeStruct(head, BF),
        jax.ShapeDtypeStruct(half, BF),
        jax.ShapeDtypeStruct((D, HEAD), BF),
        jax.ShapeDtypeStruct((D, FFT), BF),
        jax.ShapeDtypeStruct((D, FFT), BF),
    ]
    scratch = [
        pltpu.VMEM((8, TOK, FFT + HEAD), BF),
        pltpu.VMEM((D, FFT + HEAD), BF),
        pltpu.VMEM(cols, BF),
        pltpu.VMEM((2, *head), BF),
        pltpu.VMEM((2, *head), BF),
        *fold_scratch(),
        pltpu.VMEM((3, *head), BF),
        pltpu.VMEM((3, *head), BF),
        pltpu.VMEM((2, 8, TOK, WIDE), BF),
        pltpu.VMEM((2, WIDE, FFT), BF),
        pltpu.VMEM((2, WIDE, HEAD), BF),
        pltpu.VMEM((2, *half), BF),
        pltpu.VMEM((3, *half), BF),
    ]

    def kernel(*refs):
        return_one_kernel(n, *refs)

    return pl.pallas_call(
        kernel,
        out_shape=outs,
        in_specs=[ANY] * 9,
        out_specs=[VM] * 4 + [ANY] * 3,
        scratch_shapes=[
            *scratch,
            pltpu.SemaphoreType.DMA((16,)),
            pltpu.SemaphoreType.DMA((16,)),
            pltpu.SemaphoreType.DMA((9,)),
            pltpu.SemaphoreType.DMA((2,)),
            pltpu.SemaphoreType.DMA((2, 2)),
            pltpu.SemaphoreType.DMA((2,)),
        ],
        compiler_params=pltpu.CompilerParams(
            collective_id=2, has_side_effects=True, vmem_limit_bytes=62 * MIB
        ),
    )(dk, dv, o, z, w_out, w_down, gy, a2, dh)


def return_two_kernel(
    n, gi, gu0, gu, go, gd, dq, dk, dv, a1, x, dh, w_in, w_up, cosine, sine, smt, stats, sums,
    oi, ou, oo, od, e_own, osmall, gi_out,
    dqv, dkv, dvv, djp, djn, dhv, wi, wu, xt, cst, snt, data, cs, zs, ys, tile, other,
    uown, us, ui, uo, ud, si, so, sd, term, blocks, sslots, tiles, st_in,
    send, recv, load, near, x_sem, fetch_sem, put_sem, last_sem,
):
    del gi
    place = Place(n)
    net = Net(send, recv)
    rb = D // n
    R = place.R
    both = orders(2)
    greet(place, range(1, 8), (1, 2))
    names = ((gd, ud, sd, od, 3), (go, uo, so, oo, 2), (gi_out, ui, si, oi, 0))
    parts, pieces = [], []
    for src, own, slots, _, _ in names:
        halves, near_pieces = weight_folds(n, net, place, src, own, slots)
        parts.append(halves)
        pieces += near_pieces
    small = FoldR(
        net, place, lambda i: blocks.at[place.rr_of(i)], None, sslots, both[0]
    )
    total = FoldT(net, place, data, cs, zs, ys, e_own)
    up, up_pieces = half_fold(net, place, gu.reshape(4, R, 2 * rb, FFT), 1, uown, us)

    finals = []
    ends = []
    for _, _, slots, dst, k in names:
        count, width = WEIGHTS[k]
        ends.append(
            (
                lambda zt, rows, cols, slots=slots: slots.at[zt // 2, 2, zt % 2, rows, cols],
                dst, width, [(p * width, p * D) for p in range(count)],
            )
        )
    for h in range(2):
        summed = us.at[2] if h else gu0
        ends.append(
            (
                lambda zt, rows, cols, summed=summed: summed.at[zt, rows, cols],
                ou, FFT // 2, [(0, h * (FFT // 2))],
            )
        )
    for which, (summed, dst, width, spans) in enumerate(ends):
        stride = FFT if dst is ou else width
        ops = []
        for s in range(8):
            rows = pl.ds(pl.multiple_of(place.c_of(s) * rb, rb), rb)
            for p, (at, into) in enumerate(spans):
                cols = pl.ds(pl.multiple_of(into + place.t * stride, 128), width)
                piece = summed(place.zt_of(s), rows, pl.ds(at, width))
                if s == 0:
                    ops.append(
                        pltpu.make_async_copy(
                            piece, dst.at[:, cols], last_sem.at[which * 3 + p]
                        )
                    )
                else:
                    ops.append(
                        net.add(
                            lambda k, piece=piece, dst=dst, cols=cols, s=s: (
                                piece, dst.at[:, cols], place.dev_t(s),
                            )
                        )
                    )
        finals.append(ops)
    small_last = [
        net.add(
            lambda k, s=s: (
                sslots.at[2, place.zt_of(s)], osmall.at[place.t], place.dev_t(s),
            )
        )
        for s in range(1, 8)
    ]
    small_mine = pltpu.make_async_copy(
        sslots.at[2, place.zt], osmall.at[place.t], last_sem.at[15]
    )

    def send_finals(which):
        for k, op in enumerate(finals[which]):
            (op if k < len(ends[which][3]) else op()).start()

    def wait_finals(which):
        for k, op in enumerate(finals[which]):
            if k < len(ends[which][3]):
                op.wait()
            else:
                op().wait_recv()

    up.begin()
    send_finals(3)
    loads = [
        pltpu.make_async_copy(src, dst, load.at[k])
        for k, (src, dst) in enumerate(
            (
                (dq, dqv), (dk, dkv), (dv, dvv), (cosine, cst), (sine, snt),
                (w_in, wi), (dh, dhv), (w_up, wu),
            )
        )
    ]
    for copy in loads:
        copy.start()
    own_loads = [
        pltpu.make_async_copy(src, dst, near.at[k])
        for k, (src, dst) in enumerate(pieces + up_pieces)
    ]
    for copy in own_loads[:8] + own_loads[12:]:
        copy.start()

    def fetch_x(s, slot):
        return pltpu.make_async_copy(x.at[s], xt.at[slot], x_sem.at[slot])

    fetch_x(7, 0).start()
    term[...] = sums[...]
    shuffle = shuffle_matrix().astype(BF)
    head_cols = pl.ds(pl.multiple_of(place.t * HEAD, HEAD), HEAD)
    for copy in loads:
        copy.wait()
    chunk_cols = 256

    def joint(s):
        csn, sn = cst[s], snt[s]
        half = HEAD // 2
        for p, src in enumerate((dqv, dkv)):
            one = src[s, :, :half].astype(F32)
            two = src[s, :, half:].astype(F32)
            cols = slice(p * HEAD, (p + 1) * HEAD)
            djp[:, p * HEAD : p * HEAD + half] = (one * csn + two * sn).astype(BF)
            djp[:, p * HEAD + half : (p + 1) * HEAD] = (two * csn - one * sn).astype(BF)
            natural = contract_cols(djp[:, cols], shuffle)
            djn[s, :, cols] = natural.astype(BF)
            term[4 + p : 5 + p, head_cols] += jnp.sum(natural, axis=0, keepdims=True)
        value = dvv[s]
        djp[:, 2 * HEAD :] = value
        djn[s, :, 2 * HEAD :] = value
        term[6:7, head_cols] += jnp.sum(value.astype(F32), axis=0, keepdims=True)

    def make(s, idx):
        joint(s)
        fetch_x(s, idx % 2).wait()

        @pl.when(idx < 7)
        def _():
            fetch_x(total.order(idx + 1), (idx + 1) % 2).start()

        tile[...] = contract_cols(djp[...], wi[...])
        other[...] = contract_cols(dhv[s], wu[...])

    def emit(s, idx, put):
        average = stats[s, :, 0:1]
        inverse = stats[s, :, 1:2]

        def chunk(k, carry):
            cols = pl.ds(pl.multiple_of(k * chunk_cols, chunk_cols), chunk_cols)
            xhat = (xt[idx % 2, :, cols].astype(F32) - average) * inverse
            one, two = tile[:, cols], other[:, cols]
            for row, value in ((0, one * xhat), (1, one), (2, two * xhat), (3, two)):
                term[row : row + 1, cols] += jnp.sum(value, axis=0, keepdims=True)
            put((slice(None), cols), one * smt[0:1, cols] + two * smt[2:3, cols])
            return carry

        lax.fori_loop(0, D // chunk_cols, chunk, 0)

    def after(idx):
        @pl.when(idx == 1)
        def _():
            for part in parts[0]:
                part.begin()

        @pl.when(idx == 3)
        def _():
            for copy in own_loads[12:]:
                copy.wait()
            up.advance()

        @pl.when(idx == 4)
        def _():
            for part in parts[1]:
                part.begin()

        @pl.when(idx == 5)
        def _():
            up.gather()
            up.end()
            send_finals(4)

        @pl.when(idx == 6)
        def _():
            for copy in own_loads[:4]:
                copy.wait()
            for part in parts[0]:
                part.advance()
            total.turn_z1()

    total.loop(make, emit, after)

    for rr in range(R):
        for zt in range(4):
            at = (zt * R + rr) * 128
            blocks[rr, zt] = term[:, at : at + 128]
    small.both().start()
    small.first().start()
    gradient_tiles(a1, tiles, fetch_sem, [(djn, st_in, gi_out, put_sem)])
    for part in parts[2]:
        part.begin()
    for copy in own_loads[8:12]:
        copy.start()
    for part in parts[0]:
        part.gather()
        part.end()
    send_finals(0)
    for copy in own_loads[4:8]:
        copy.wait()
    for part in parts[1]:
        part.advance()
    total.turn_own()
    small.both().wait_recv()
    sslots[0] = sslots[0] + blocks[place.rr_of(2)]
    small.second().start()
    for copy in own_loads[8:12]:
        copy.wait()
    for part in parts[2]:
        part.advance()
    for part in parts[1]:
        part.gather()
        part.end()
    send_finals(1)
    small.first().wait_recv()
    small.second().wait_recv()
    sslots[2] = sslots[2] + (sslots[1] + blocks[place.rr])
    small_mine.start()
    for op in small_last:
        op().start()
    for part in parts[2]:
        part.gather()
        part.end()
    send_finals(2)
    total.end()
    for which in range(5):
        wait_finals(which)
    small_mine.wait()
    for op in small_last:
        op().wait_recv()
    net.finish()


def return_two(n, up_sum, g_up, g_out, g_down, dq, dk, dv, a1, x, dh, w_in, w_up, cosine, sine, smt, stats, sums):
    rb = D // n
    R = n // 8
    head, cols, block = (8, TOK, HEAD), (8, TOK, FFT), (8, TOK, D)
    outs = [jax.ShapeDtypeStruct((rb, HEADS * parts * width), BF) for parts, width in WEIGHTS]
    outs += [
        jax.ShapeDtypeStruct((TOK, D), F32),
        jax.ShapeDtypeStruct((8, SMALLR, 128), F32),
        jax.ShapeDtypeStruct((D, 3 * HEAD), BF),
    ]
    wide = [parts * width for parts, width in WEIGHTS]
    scratch = [
        pltpu.VMEM(head, F32),
        pltpu.VMEM(head, BF),
        pltpu.VMEM(head, BF),
        pltpu.VMEM((TOK, 3 * HEAD), BF),
        pltpu.VMEM((8, TOK, 3 * HEAD), BF),
        pltpu.VMEM(cols, BF),
        pltpu.VMEM((D, 3 * HEAD), BF),
        pltpu.VMEM((D, FFT), BF),
        pltpu.VMEM((2, TOK, D), BF),
        pltpu.VMEM((8, TOK, HEAD // 2), F32),
        pltpu.VMEM((8, TOK, HEAD // 2), F32),
        *fold_scratch(),
        pltpu.VMEM((TOK, D), F32),
        pltpu.VMEM((TOK, D), F32),
        pltpu.VMEM((2, 4, 2 * rb, FFT // 2), BF),
        pltpu.VMEM((3, 4, 2 * rb, FFT // 2), BF),
        *[pltpu.VMEM((2, 2, 2, 2 * rb, wide[k]), BF) for k in (0, 2, 3)],
        *[pltpu.VMEM((2, 3, 2, 2 * rb, wide[k]), BF) for k in (0, 2, 3)],
        pltpu.VMEM((SMALLR, D), F32),
        pltpu.VMEM((R, 4, SMALLR, 128), F32),
        pltpu.VMEM((3, 4, SMALLR, 128), F32),
        pltpu.VMEM((2, 8, TOK, HEAD), BF),
        pltpu.VMEM((2, HEAD, 3 * HEAD), BF),
    ]
    copies = 6 * 3 + 3 + 3 + 7 + 7 * 7 + 7

    def kernel(*refs):
        return_two_kernel(n, None, *refs)

    return pl.pallas_call(
        kernel,
        out_shape=outs,
        in_specs=[ANY] * 14 + [VM] * 3,
        out_specs=[ANY] * 4 + [VM] + [ANY] * 2,
        scratch_shapes=[
            *scratch,
            pltpu.SemaphoreType.DMA((copies,)),
            pltpu.SemaphoreType.DMA((copies,)),
            pltpu.SemaphoreType.DMA((8,)),
            pltpu.SemaphoreType.DMA((16,)),
            pltpu.SemaphoreType.DMA((2,)),
            pltpu.SemaphoreType.DMA((2,)),
            pltpu.SemaphoreType.DMA((2,)),
            pltpu.SemaphoreType.DMA((16,)),
        ],
        compiler_params=pltpu.CompilerParams(
            collective_id=3, has_side_effects=True, vmem_limit_bytes=62 * MIB
        ),
    )(up_sum, g_up, g_out, g_down, dq, dk, dv, a1, x, dh, w_in, w_up, cosine, sine, smt, stats, sums)


def token_row(base, core, size=RUN):
    lane = lax.broadcasted_iota(jnp.int32, (1, size), 1)
    return base + (lane + core * TOK) % RUN


def token_col(base, core, size=RUN):
    row = lax.broadcasted_iota(jnp.int32, (size, 1), 0)
    return base + (row + core * TOK) % RUN


def start_of(tokens, lengths, nseq):
    out, begin = tokens * 0, lengths[0] * 0
    for s in range(nseq):
        out = jnp.where(tokens >= begin, begin, out)
        begin = begin + lengths[s]
    return out


def run_facts(place, lengths, nseq, u):
    number = place.zt_of_run(u) * place.R + place.rr
    count = number - start_of(number * RUN, lengths, nseq) // RUN + 1
    return number, count, start_of(number * RUN + RUN - 1, lengths, nseq)


def scores_of(key, query):
    return lax.dot_general(key, query, (((1,), (1,)), ((), ())), preferred_element_type=F32)


def seen_mask(core, gq, gk, lengths, nseq):
    tq = token_row(gq * RUN, core)
    tk = token_col(gk * RUN, core)
    return (tk <= tq) & (tk >= start_of(tq, lengths, nseq))


def attend_kernel(
    n, nseq, lengths, q, dout, kg, vg, o, stats, m, l, acc, kv, sem
):
    u = pl.program_id(0)
    place = Place(n)
    number, count, last = run_facts(place, lengths, nseq, u)
    m[...] = jnp.full_like(m, NEGATIVE)
    l[...] = jnp.zeros_like(l)
    acc[...] = jnp.zeros_like(acc)

    def fetch(d, slot):
        far = number - d
        moved = (far // place.R) ^ place.zt
        i, ku = (far % place.R) ^ place.rr, moved % 2 * 2 + moved // 2
        return [
            pltpu.make_async_copy(src.at[i, :, ku], kv.at[slot, p], sem.at[slot, p])
            for p, src in enumerate((kg, vg))
        ]

    def block(slot, far, masked):
        query = q[...].reshape(RUN, HEAD)
        key = kv[slot, 0].reshape(RUN, HEAD)
        value = kv[slot, 1].reshape(RUN, HEAD)
        s = scores_of(key, query)
        if masked:
            s = jnp.where(seen_mask(place.c, number, number - far, lengths, nseq), s, NEGATIVE)
        old = m[0:1, :]
        new = jnp.maximum(old, jnp.max(s, axis=0, keepdims=True))
        p = jnp.exp(s - new)
        fade = jnp.exp(old - new)
        l[0:1, :] = l[0:1, :] * fade + jnp.sum(p, axis=0, keepdims=True)
        m[0:1, :] = new
        mixed = lax.dot_general(
            value, p.astype(BF), (((0,), (0,)), ((), ())), preferred_element_type=F32
        )
        acc[...] = acc[...] * fade + mixed

    for copy in fetch(0, 0):
        copy.start()

    def step(d, carry):
        slot = d % 2
        for copy in fetch(d, slot):
            copy.wait()

        @pl.when(d + 1 < count)
        def _():
            for copy in fetch(d + 1, 1 - slot):
                copy.start()

        edge = (d == 0) | ((number - d) * RUN < last)

        @pl.when(edge)
        def _():
            block(slot, d, True)

        @pl.when(jnp.logical_not(edge))
        def _():
            block(slot, d, False)

        return carry

    lax.fori_loop(0, count, step, 0)
    out = acc[...] / l[0:1, :]
    rows = out.T
    o[...] = rows.astype(BF).reshape(o.shape)
    grad = dout[...].reshape(RUN, HEAD).astype(F32).T
    stats[0, 0:1, :] = m[0:1, :] + jnp.log(l[0:1, :])
    stats[0, 1:2, :] = jnp.sum(out * grad, axis=0, keepdims=True)
    stats[0, 2:8, :] = jnp.zeros((6, RUN), F32)


def attend(n, lengths, q, dout, kg, vg):
    run = pl.BlockSpec((2, 1, TOK, HEAD), lambda u, *_: (0, u, 0, 0))

    def kernel(*refs):
        attend_kernel(n, lengths.shape[0], *refs)

    return pl.pallas_call(
        kernel,
        out_shape=[
            jax.ShapeDtypeStruct((2, 4, TOK, HEAD), BF),
            jax.ShapeDtypeStruct((4, 8, RUN), F32),
        ],
        grid_spec=pltpu.PrefetchScalarGridSpec(
            num_scalar_prefetch=1,
            grid=(4,),
            in_specs=[run, run, ANY, ANY],
            out_specs=[run, pl.BlockSpec((1, 8, RUN), lambda u, *_: (u, 0, 0))],
            scratch_shapes=[
                pltpu.VMEM((8, RUN), F32),
                pltpu.VMEM((8, RUN), F32),
                pltpu.VMEM((HEAD, RUN), F32),
                pltpu.VMEM((2, 2, 2, TOK, HEAD), BF),
                pltpu.SemaphoreType.DMA((2, 2)),
            ],
        ),
        compiler_params=pltpu.CompilerParams(vmem_limit_bytes=62 * MIB),
        cost_estimate=pl.CostEstimate(
            flops=4 * 16 * RUN * RUN * HEAD, bytes_accessed=12 * MIB, transcendentals=16 * RUN * RUN
        ),
    )(lengths, q, dout, kg, vg)


def attend_back_kernel(
    n, nseq, lengths, q, dout, stats, k, v, dq, dk, dv, tq, tk, tv, facts
):
    block_at = pl.program_id(0)
    steps = pl.num_programs(0)

    place = Place(n)

    @pl.when(block_at == 0)
    def _():
        tq[...] = jnp.zeros_like(tq)
        for u in range(4):
            for f, value in enumerate(run_facts(place, lengths, nseq, u)):
                facts[4 * f + u] = value

    tk[...] = jnp.zeros_like(tk)
    tv[...] = jnp.zeros_like(tv)
    here = place.zt_of_run(block_at % 4) * place.R + (place.rr ^ (block_at // 4))

    for u in range(4):
        far = facts[u] - here
        active = (far >= 0) & (far < facts[4 + u])
        edge = (far == 0) | (here * RUN < facts[8 + u])

        def block(masked, u=u):
            query = q[:, u].reshape(RUN, HEAD)
            grad = dout[:, u].reshape(RUN, HEAD)
            key = k[...].reshape(RUN, HEAD)
            value = v[...].reshape(RUN, HEAD)
            s = scores_of(key, query)
            p = jnp.exp(s - stats[u, 0:1, :])
            if masked:
                p = jnp.where(seen_mask(place.c, facts[u], here, lengths, nseq), p, 0.0)
            dp = scores_of(value, grad)
            ds = (p * (dp - stats[u, 1:2, :])).astype(BF)
            tv[...] += jnp.dot(p.astype(BF), grad, preferred_element_type=F32)
            tk[...] += jnp.dot(ds, query, preferred_element_type=F32)
            tq[u] += lax.dot_general(
                ds, key, (((0,), (0,)), ((), ())), preferred_element_type=F32
            )

        @pl.when(active & edge)
        def _(block=block):
            block(True)

        @pl.when(active & jnp.logical_not(edge))
        def _(block=block):
            block(False)

    dk[...] = tk[...].astype(BF).reshape(dk.shape)
    dv[...] = tv[...].astype(BF).reshape(dv.shape)

    @pl.when(block_at == steps - 1)
    def _():
        for u in range(4):
            dq[:, u] = (tq[u] * HEAD**-0.5).reshape(2, TOK, HEAD)


def attend_back(n, lengths, q, dout, stats, kg, vg):
    R = n // 8
    whole = pl.BlockSpec((2, 4, TOK, HEAD), lambda b, *_: (0, 0, 0, 0))
    key = pl.BlockSpec((1, 2, 1, TOK, HEAD), lambda b, *_: (b // 4, 0, b % 4, 0, 0))

    def kernel(*refs):
        attend_back_kernel(n, lengths.shape[0], *refs)

    return pl.pallas_call(
        kernel,
        out_shape=[
            jax.ShapeDtypeStruct((2, 4, TOK, HEAD), F32),
            jax.ShapeDtypeStruct((R, 2, 4, TOK, HEAD), BF),
            jax.ShapeDtypeStruct((R, 2, 4, TOK, HEAD), BF),
        ],
        grid_spec=pltpu.PrefetchScalarGridSpec(
            num_scalar_prefetch=1,
            grid=(4 * R,),
            in_specs=[
                whole,
                whole,
                pl.BlockSpec((4, 8, RUN), lambda b, *_: (0, 0, 0)),
                key,
                key,
            ],
            out_specs=[whole, key, key],
            scratch_shapes=[
                pltpu.VMEM((4, RUN, HEAD), F32),
                pltpu.VMEM((RUN, HEAD), F32),
                pltpu.VMEM((RUN, HEAD), F32),
                pltpu.SMEM((12,), jnp.int32),
            ],
        ),
        compiler_params=pltpu.CompilerParams(vmem_limit_bytes=62 * MIB),
        cost_estimate=pl.CostEstimate(
            flops=10 * 16 * RUN * RUN * HEAD, bytes_accessed=24 * MIB, transcendentals=16 * RUN * RUN
        ),
    )(lengths, q, dout, stats, kg, vg)


def adam_step(parameter, gradient, first_moment, second_moment, step_rate):
    first_new = BETA_ONE * first_moment + (1.0 - BETA_ONE) * gradient
    second_new = BETA_TWO * second_moment + (1.0 - BETA_TWO) * gradient * gradient
    first_hat = first_new / (1.0 - BETA_ONE**STEPS)
    second_hat = second_new / (1.0 - BETA_TWO**STEPS)
    parameter_new = parameter - step_rate * (
        first_hat / (jnp.sqrt(second_hat) + ADAM_EPS) + WEIGHT_DECAY * parameter
    )
    return (first_new, second_new, parameter_new)


def adam_kernel(rates, *refs):
    count = len(rates)
    x, gy, e, part, small = refs[:5]
    groups = [refs[5 + k * count : 5 + (k + 1) * count] for k in range(7)]
    block_out, token_grad = refs[5 + 7 * count :]
    for p, g, m, v, rate, p_out, m_out, v_out in zip(
        *groups[:4], rates, *groups[4:]
    ):
        m_out[...], v_out[...], p_out[...] = adam_step(
            p[...], g[...].astype(F32), m[...], v[...], rate
        )
    xf, grad = x[...].astype(F32), e[...]
    block_out[...] = (xf + part[...] + small[7:8, :] + small[8:9, :]).astype(BF)
    centred = xf - jnp.mean(xf, axis=-1, keepdims=True)
    inverse = lax.rsqrt(jnp.mean(centred * centred, axis=-1, keepdims=True) + NORM_EPS)
    xhat = centred * inverse
    token_grad[...] = gy[...].astype(F32) + inverse * (
        grad
        - jnp.mean(grad, axis=-1, keepdims=True)
        - xhat * jnp.mean(grad * xhat, axis=-1, keepdims=True)
    )


def adam(own, params, grads, firsts, seconds, rates):
    steps = 8

    def spec(a):
        return pl.BlockSpec((a.shape[0], a.shape[1] // steps), lambda k: (0, k))

    tok = pl.BlockSpec((TOK // steps, D), lambda k: (k, 0))
    small = pl.BlockSpec((SMALLR, D), lambda k: (0, 0))
    arrays = [*params, *grads, *firsts, *seconds]
    outs = [jax.ShapeDtypeStruct(p.shape, F32) for _ in range(3) for p in params]
    own_outs = [jax.ShapeDtypeStruct((TOK, D), BF), jax.ShapeDtypeStruct((TOK, D), F32)]

    def kernel(*refs):
        adam_kernel(rates, *refs)

    out = pl.pallas_call(
        kernel,
        out_shape=[*outs, *own_outs],
        grid=(steps,),
        in_specs=[tok] * 4 + [small] + [spec(a) for a in arrays],
        out_specs=[spec(a) for a in outs] + [tok] * 2,
        compiler_params=pltpu.CompilerParams(vmem_limit_bytes=62 * MIB),
    )(*own, *arrays)
    count = len(params)
    return [out[k * count : (k + 1) * count] for k in range(3)] + list(out[3 * count :])


def contract_rows(left, right):
    return lax.dot_general(left, right, (((0,), (0,)), ((), ())), preferred_element_type=F32)


def contract_cols(left, right):
    return lax.dot_general(left, right, (((1,), (1,)), ((), ())), preferred_element_type=F32)


def paired(columns):
    turned, half = HEAD // 8, HEAD // 2
    heads = columns.reshape(columns.shape[0], -1, HEAD)
    cut = 2 * turned + half - turned
    order = [(0, turned), (2 * turned, cut), (turned, 2 * turned), (cut, HEAD)]
    return jnp.concatenate([heads[..., a:b] for a, b in order], axis=-1).reshape(columns.shape)


def unpaired(columns):
    turned, half = HEAD // 8, HEAD // 2
    heads = columns.reshape(columns.shape[0], -1, HEAD)
    order = [(0, turned), (half, half + turned), (turned, half), (half + turned, HEAD)]
    return jnp.concatenate([heads[..., a:b] for a, b in order], axis=-1).reshape(columns.shape)


def turn(values, cosine, sine):
    half = HEAD // 2
    one, two = values[:, :half], values[:, half:]
    return jnp.concatenate([one * cosine - two * sine, two * cosine + one * sine], axis=1)


def pack_small(columns, n):
    rb = D // n
    blocks = columns.reshape(SMALLR, n, rb).transpose(1, 0, 2)
    return jnp.pad(blocks, ((0, 0), (0, 0), (0, 128 - rb)))


def return_plain(n, gg, xg, a1, a2, z, dh, o, dq, dk, dv, ws, cosine, sine, small_all, sums):
    place = Place(n)
    R, rb, rows = n // 8, D // n, 8 * TOK
    a1, a2, gy, z, dh, o, dq = (v.reshape(rows, -1) for v in (a1, a2, gg, z, dh, o, dq))
    w_in, w_up, w_out, w_down = (g.reshape(D, -1) for g in ws)
    cosine, sine = cosine.reshape(rows, -1), sine.reshape(rows, -1)
    g1, g2 = small_all[0], small_all[2]
    xf = xg.reshape(rows, D).astype(F32)
    centred = xf - jnp.mean(xf, axis=-1, keepdims=True)
    xhat = centred * lax.rsqrt(jnp.mean(centred * centred, axis=-1, keepdims=True) + NORM_EPS)
    partial_out = (contract_cols(o, w_out) + contract_cols(z, w_down)).astype(BF)
    ins = {"k": dk, "v": dv, "p": partial_out.reshape(8, TOK, D)}
    back = {}
    for at, name in enumerate(ins):
        back |= return_keys(n, {name: ins[name]}, 4 + at)
    dq = turn(dq, cosine, -sine)
    dk = turn(back["k"].reshape(rows, HEAD).astype(F32), cosine, -sine)
    dj = jnp.concatenate([dq.astype(BF), dk.astype(BF), back["v"].reshape(rows, HEAD)], axis=1)
    da1 = contract_cols(dj, w_in)
    da2 = contract_cols(dh, w_up)
    e = (da1 * g1 + da2 * g2).astype(BF)
    norm_grads = [jnp.sum(v, axis=0) for v in (da1 * xhat, da1, da2 * xhat, da2)]
    dj = jnp.concatenate([unpaired(dj[:, : 2 * HEAD]), dj[:, 2 * HEAD :]], axis=1)
    dj_sum = jnp.sum(dj.astype(F32), axis=0).reshape(3, HEAD)
    own_cols = lax.dynamic_update_slice(
        jnp.zeros((SMALLR, D), F32), dj_sum, (jnp.int32(4), place.t * HEAD)
    )
    small_term = own_cols + sums
    small_term = small_term.at[:4].set(jnp.stack(norm_grads))
    small_blocks = pack_small(small_term, n).reshape(4, R, 2 * SMALLR, 128)
    grads = [
        contract_rows(left, right).astype(BF).reshape(4, R, 2 * rb, -1)
        for left, right in ((a1, dj), (a2, dh), (gy, o), (gy, z))
    ]
    *weight_grads, e_own, small_parts = return_grads(
        n, grads, e.reshape(8, TOK, D), small_blocks, 3
    )
    return back["p"], weight_grads, e_own, jnp.sum(small_parts, axis=0)[:SMALLC, :rb].T


def body(
    tokens, cotangent, lengths,
    attend_in, widening, attend_out, narrowing, small_params,
    first_attend_in, first_widening, first_attend_out, first_narrowing, first_small,
    second_attend_in, second_widening, second_attend_out, second_narrowing, second_small,
):
    n = lax.axis_size("fsdp")
    place = Place(n)
    R = place.R
    rb = D // n
    turned = HEAD // 8
    lanes = jnp.arange(HEAD // 2, dtype=jnp.int32)
    frequency = jnp.where(
        lanes < turned, ROPE_BASE ** (-2.0 * lanes.astype(F32) / (2 * turned)), 0.0
    )[None, :]

    small_rows = jnp.pad(small_params, ((0, 0), (0, 128 - SMALLC)))
    low_in = attend_in.astype(BF)
    low_in = jnp.concatenate([paired(low_in[:, : 2 * D]), low_in[:, 2 * D :]], axis=1)
    weights = [low_in] + [w.astype(BF) for w in (widening, attend_out, narrowing)]
    runs = (2, 4, TOK, HEAD)
    xg, gg, a1, a2, *ws, q, kg, vg, z, dh, dout, small_all, sums, stats_x, cosine, sine = forward(
        n, tokens, cotangent, weights, small_rows, lengths, frequency
    )
    xg, gg, a1, a2, z, dh, stats_x, cosine, sine = (
        v.reshape(8, TOK, v.shape[-1]) for v in (xg, gg, a1, a2, z, dh, stats_x, cosine, sine)
    )

    kg = kg.reshape(R, *runs)
    vg = vg.reshape(R, *runs)
    q4, dout4 = q.reshape(runs), dout.reshape(runs)
    o4, stats = attend(n, lengths, q4, dout4, kg, vg)
    dq4, dk5, dv5 = attend_back(n, lengths, q4, dout4, stats, kg, vg)
    o, dq = o4.reshape(8, TOK, HEAD), dq4.reshape(8, TOK, HEAD)
    dk, dv = dk5.reshape(R, 8, TOK, HEAD), dv5.reshape(R, 8, TOK, HEAD)
    if R == 4:
        p_own, dk, dv, up_sum, g_out, g_down, g_up = return_one(
            n, dk, dv, o, z, ws[2].reshape(D, -1), ws[3].reshape(D, -1), gg, a2, dh
        )
        *weight_grads, e_own, small_parts, _ = return_two(
            n, up_sum, g_up, g_out, g_down, dq, dk, dv, a1, xg, dh,
            ws[0].reshape(D, -1), ws[1].reshape(D, -1), cosine, sine, small_all, stats_x, sums,
        )
        own_lanes = lax.dynamic_slice(
            jnp.sum(small_parts, axis=0), (0, place.c * rb), (SMALLR, rb)
        )
        small_grad = own_lanes[:SMALLC].T
    else:
        p_own, weight_grads, e_own, small_grad = return_plain(
            n, gg, xg, a1, a2, z, dh, o, dq, dk, dv, ws, cosine, sine, small_all, sums
        )
    gr_in, gr_up, gr_out, gr_down = weight_grads
    rate_inner = 2.5 * D ** (-0.5)
    rate_outer = 2.5 * (D * 11 // LMAX) ** (-0.5)
    rate_down = 2.5 * FF ** (-0.5)
    rate_small = 0.5
    new, mean, square, block_out, token_grad = adam(
        (tokens, cotangent, e_own, p_own, small_all),
        (attend_in, widening, attend_out, narrowing),
        (gr_in, gr_up, gr_out, gr_down),
        (first_attend_in, first_widening, first_attend_out, first_narrowing),
        (second_attend_in, second_widening, second_attend_out, second_narrowing),
        (rate_inner, rate_inner, rate_outer, rate_down),
    )
    mean_small, square_small, new_small = adam_step(
        small_params, small_grad, first_small, second_small, rate_small
    )
    return (
        block_out,
        token_grad,
        *new,
        new_small,
        *mean,
        mean_small,
        *square,
        square_small,
    )


def solution(mesh):
    spec = P("fsdp", None)
    return jax.shard_map(
        body,
        mesh=mesh,
        in_specs=(spec, spec, P(), *[spec] * 15),
        out_specs=(spec,) * 17,
        check_vma=False,
    )
```

```python
import math

import jax
import jax.numpy as jnp
import numpy as np
from jax import lax
from jax.experimental import pallas as pl
from jax.experimental.pallas import tpu as pltpu
from jax.sharding import PartitionSpec as P

D = 2048
HEADS = 8
HEAD = D // HEADS
FF = 8192
FFT = FF // HEADS
LMAX = 4096
STEPS = 10
TOK = 256
RUN = 2 * TOK
BACK_RUNS = LMAX // RUN + 1

NORM_EPS = 1e-05
ADAM_EPS = 1e-08
BETA_ONE = 0.9
BETA_TWO = 0.95
WEIGHT_DECAY = 0.01
NEGATIVE = -1e30
ROPE_BASE = 10000.0
SMALLC = 13
SMALLR = 16

BF = jnp.bfloat16
F32 = jnp.float32
ANY = pl.BlockSpec(memory_space=pl.ANY)
VM = pl.BlockSpec(memory_space=pltpu.VMEM)
MIB = 1024 * 1024
WEIGHTS = ((3, HEAD), (1, FFT), (1, HEAD), (1, FFT))


class Place:
    def __init__(self, n):
        self.n = n
        self.S = n // 4
        self.R = self.S // 2
        self.bits = int(math.log2(self.R))
        me = lax.axis_index("fsdp")
        self.me = me
        self.zt = me // self.S
        self.rr = (me % self.S) // 2
        self.c = me % 2
        self.z1 = self.zt // 2
        self.z0 = self.zt % 2
        self.t = self.zt * 2 + self.c

    def zt_of(self, s):
        z1 = 1 - self.z1 if s & 1 else self.z1
        z0 = 1 - self.z0 if s & 2 else self.z0
        return z1 * 2 + z0

    def zt_of_run(self, u):
        z1 = self.z1 + (1 - 2 * self.z1) * (u % 2)
        z0 = self.z0 + (1 - 2 * self.z0) * (u // 2)
        return z1 * 2 + z0

    def c_of(self, s):
        return 1 - self.c if s & 4 else self.c

    def t_of(self, s):
        return self.zt_of(s) * 2 + self.c_of(s)

    def rr_of(self, i):
        out = 0
        for k in range(self.bits):
            bit = (self.rr // (1 << k)) % 2
            out = out + (1 - bit if i >> k & 1 else bit) * (1 << k)
        return out

    def dev_t(self, s):
        return self.zt_of(s) * self.S + self.rr * 2 + self.c_of(s)

    def dev_r(self, i):
        return self.zt * self.S + self.rr_of(i) * 2 + self.c


class Copies:
    def __init__(self, send, recv):
        self.send, self.recv, self.count, self.started = send, recv, 0, []

    def remote(self, src, dst, dev):
        k = self.count
        self.count += 1
        copy = pltpu.make_async_remote_copy(
            src_ref=src,
            dst_ref=dst,
            send_sem=self.send.at[k],
            recv_sem=self.recv.at[k],
            device_id=(dev,),
            device_id_type=pl.DeviceIdType.MESH,
        )
        copy.start()
        self.started.append(copy)
        return copy

    def local(self, src, dst):
        k = self.count
        self.count += 1
        copy = pltpu.make_async_copy(src, dst, self.send.at[k])
        copy.start()
        return copy

    def finish(self):
        for copy in self.started:
            copy.wait_send()


def greet(place, t_group, r_group):
    barrier = pltpu.get_barrier_semaphore()
    peers = [place.dev_t(s) for s in t_group] + [place.dev_r(i) for i in r_group]
    for dev in peers:
        pl.semaphore_signal(barrier, inc=1, device_id=(dev,), device_id_type=pl.DeviceIdType.MESH)
    pl.semaphore_wait(barrier, len(peers))


def top_bit(s):
    return 1 << (s.bit_length() - 1)


def orders(bits):
    up = [1 << k for k in range(bits)]
    return [up, up[::-1]]


def spread(order):
    have, out = [0], []
    for bit in order:
        new = [i | bit for i in have]
        out += [(i, bit) for i in new]
        have = have + new
    return out


def collected(order):
    left, out = list(range(1 << len(order))), []
    for bit in order:
        out.append((bit, [i for i in left if i & bit]))
        left = [i for i in left if not i & bit]
    return out


def add_rows(dst, a, b):
    lead = dst.shape[:-2]
    rows, columns = dst.shape[-2:]
    size = min(rows, max(16, 1 << int(math.log2(16384 // columns))))
    for flat in range(math.prod(lead)):
        where, rest = [], flat
        for extent in lead[::-1]:
            where.insert(0, rest % extent)
            rest //= extent

        def step(k, carry, where=tuple(where)):
            at = where + (pl.ds(pl.multiple_of(k * size, size), size), slice(None))
            dst[at] = (a[at].astype(F32) + b[at].astype(F32)).astype(dst.dtype)
            return carry

        lax.fori_loop(0, rows // size, step, 0)


def call(kernel, ins, in_specs, outs, out_specs, scratch, collective_id, copies, vmem=60):
    return pl.pallas_call(
        kernel,
        out_shape=outs,
        in_specs=in_specs,
        out_specs=out_specs,
        scratch_shapes=[
            *scratch,
            pltpu.SemaphoreType.DMA((copies,)),
            pltpu.SemaphoreType.DMA((copies,)),
        ],
        compiler_params=pltpu.CompilerParams(
            collective_id=collective_id, has_side_effects=True, vmem_limit_bytes=vmem * MIB
        ),
    )(*ins)


class Net:
    def __init__(self, send, recv):
        self.send, self.recv, self.makers, self.count = send, recv, [], 0

    def add(self, maker, many=1):
        base = self.count
        self.count += many

        def build(k=0):
            src, dst, dev = maker(k)
            return pltpu.make_async_remote_copy(
                src_ref=src,
                dst_ref=dst,
                send_sem=self.send.at[base + k],
                recv_sem=self.recv.at[base + k],
                device_id=(dev,),
                device_id_type=pl.DeviceIdType.MESH,
            )

        self.makers.append((build, many))
        return build

    def finish(self):
        for build, many in self.makers:
            if many == 1:
                build().wait_send()
            else:

                def one(k, carry, build=build):
                    build(k).wait_send()
                    return carry

                lax.fori_loop(0, many, one, 0)


class GatherT:
    def __init__(self, net, place, own, out):
        self.ops = {}
        for s in range(1, 8):
            hop = top_bit(s)
            src = own if s == hop else out.at[(s - hop) // 4, (s - hop) % 4]
            self.ops[s] = net.add(
                lambda k, src=src, s=s, hop=hop: (src, out.at[s // 4, s % 4], place.dev_t(hop))
            )

    def start(self, *which):
        for s in which:
            self.ops[s]().start()

    def wait(self, *which):
        for s in which:
            self.ops[s]().wait_recv()


class GatherR:
    def __init__(self, net, place, region, order):
        self.plan = spread(order)
        self.ops = {}
        self.later = [(i, bit) for i, bit in self.plan if i != bit]
        self.used = {i ^ bit for i, bit in self.later}
        for i, bit in self.plan:
            self.ops[i] = net.add(
                lambda k, i=i, bit=bit: (region(i ^ bit), region(i ^ bit), place.dev_r(bit))
            )

    def begin(self):
        for i, bit in self.plan:
            if i == bit:
                self.ops[i]().start()

    def advance(self):
        seen = set()
        for i, bit in self.later:
            if i ^ bit not in seen:
                self.ops[i ^ bit]().wait_recv()
                seen.add(i ^ bit)
            self.ops[i]().start()

    def end(self):
        for i, _ in self.plan:
            if i not in self.used:
                self.ops[i]().wait_recv()


def cosine_and_sine(x):
    turns = jnp.floor(x * (2.0 / math.pi) + 0.5)
    r = ((x - turns * 1.5703125) - turns * 4.837512969970703e-4) - turns * 7.549789954891882e-8
    z = r * r
    sine = ((-1.9515295891e-4 * z + 8.3321608736e-3) * z - 1.6666654611e-1) * z * r + r
    cosine = (
        ((2.443315711809948e-5 * z - 1.388731625493765e-3) * z + 4.166664568298827e-2) * z * z
        - 0.5 * z
        + 1.0
    )
    quarter = turns - 4.0 * jnp.floor(turns * 0.25)
    odd = (quarter == 1.0) | (quarter == 3.0)
    first, second = jnp.where(odd, sine, cosine), jnp.where(odd, cosine, sine)
    return (
        jnp.where((quarter == 1.0) | (quarter == 2.0), -first, first),
        jnp.where(quarter >= 2.0, -second, second),
    )


def shuffle_matrix():
    turned, half = HEAD // 8, HEAD // 2
    into = lax.broadcasted_iota(jnp.int32, (HEAD, HEAD), 1)
    source = lax.broadcasted_iota(jnp.int32, (HEAD, HEAD), 0)
    moved = jnp.where((into >= turned) & (into < half), into + turned, into)
    moved = jnp.where((into >= half) & (into < half + turned), into - (half - turned), moved)
    return jnp.where(source == moved, 1.0, 0.0).astype(F32)


def weight_halves(net, place, ref):
    both = orders(place.bits)
    return [
        GatherR(net, place, lambda i, h=h: ref.at[pl.ds(2 * h, 2), place.rr_of(i)], both[h])
        for h in range(2)
    ]


def forward_kernel(
    n, nseq, x, gy, wi, wu, wo, wd, small, lengths, frequency,
    xg, gg, a1g, a2g, oi, ou, oo, od, qo, kg, vg, zo, dho, dout, smt, sums, stats, cosine, sine,
    xv, gv, sm, ti, tu, to, td, slope, a2v, kt, vt, at, ztile, dht, bias, dhsum,
    send, recv, local, out_sem, g_sem,
):
    place = Place(n)
    rb = D // n
    net = Net(send, recv)
    weights = list(zip((wi, wu, wo, wd), (ti, tu, to, td), WEIGHTS))
    greet(place, range(1, 8), [1 << k for k in range(place.bits)])
    mine = pl.ds(pl.multiple_of(place.c * rb, rb), rb)

    small_t = [
        net.add(lambda k, s=s: (small, sm.at[place.zt, place.rr, mine, :], place.dev_t(s)))
        for s in range(1, 8)
    ]

    def columns(p, width, t):
        return pl.ds(pl.multiple_of(p * D + t * width, 128), width)

    def exchange(which):
        src, dst, (parts, width) = weights[which]
        return [
            net.add(
                lambda k, s=s, p=p: (
                    src.at[:, columns(p, width, place.t_of(s))],
                    dst.at[place.zt, place.rr, mine, pl.ds(p * width, width)],
                    place.dev_t(s),
                )
            )
            for s in range(1, 8)
            for p in range(parts)
        ]

    to_t = [exchange(k) for k in range(4)]
    small_r = GatherR(net, place, lambda i: sm.at[:, place.rr_of(i)], orders(place.bits)[0])
    to_r = [weight_halves(net, place, w[1]) for w in weights]
    x_t = GatherT(net, place, x, xv)
    g_t = GatherT(net, place, gy, gv)
    both = orders(place.bits)
    keys = []
    for own, out, order in ((kt, kg, both[0]), (vt, vg, both[1])):
        ops = {}
        for i, bit in spread(order):
            ops[i] = net.add(
                lambda s, i=i, bit=bit, own=own, out=out: (
                    own.at[s // 4, s % 4] if i == bit else out.at[i ^ bit, s // 4, s % 4],
                    out.at[i, s // 4, s % 4],
                    place.dev_r(bit),
                ),
                8,
            )
        keys.append((ops, spread(order)))

    def start(ops):
        for op in ops:
            op().start()

    def wait(ops):
        for op in ops:
            op().wait_recv()

    locals_ = [
        pltpu.make_async_copy(x, xv.at[0, 0], local.at[0]),
        pltpu.make_async_copy(gy, gv.at[0, 0], local.at[1]),
        pltpu.make_async_copy(small, sm.at[place.zt, place.rr, mine, :], local.at[2]),
    ]
    for src, dst, (parts, width) in weights:
        for p in range(parts):
            locals_.append(
                pltpu.make_async_copy(
                    src.at[:, columns(p, width, place.t)],
                    dst.at[place.zt, place.rr, mine, pl.ds(p * width, width)],
                    local.at[len(locals_)],
                )
            )
    for copy in locals_:
        copy.start()
    start(small_t)
    start(to_t[0])
    x_t.start(4)
    for copy in locals_:
        copy.wait()
    wait(small_t)
    small_r.begin()
    wait(to_t[0])
    for part in to_r[0]:
        part.begin()
    start(to_t[1])
    x_t.start(2)
    small_r.advance()
    for part in to_r[0]:
        part.advance()

    def tables(s, carry):
        core, u = s // 4, s % 4
        device = (
            place.zt_of_run(u) * place.S + place.rr * 2 + place.c + (1 - 2 * place.c) * core
        )
        token = device * TOK + lax.broadcasted_iota(jnp.int32, (TOK, HEAD // 2), 0)
        offset = token - start_of(token, lengths, nseq)
        angles = offset.astype(F32) * frequency[0:1, :]
        cosine[core, u], sine[core, u] = cosine_and_sine(angles)
        return carry

    lax.fori_loop(0, 8, tables, 0)
    wait(to_t[1])
    x_t.start(1)
    for part in to_r[1]:
        part.begin()
    small_r.end()

    smt[...] = sm[...].reshape(D, 128).T[:SMALLR, :]
    head_cols = pl.ds(pl.multiple_of(place.t * HEAD, HEAD), HEAD)
    shuffle = shuffle_matrix()
    three = jnp.dot(
        smt[0:8, head_cols], shuffle, precision=lax.Precision.HIGHEST, preferred_element_type=F32
    )
    for p in range(2):
        bias[0:1, p * HEAD : (p + 1) * HEAD] = three[4 + p : 5 + p, :]
    bias[0:1, 2 * HEAD : 3 * HEAD] = smt[6:7, head_cols]

    def repeat_matrix():
        lane = lax.broadcasted_iota(jnp.int32, (HEAD, FFT), 1)
        row = lax.broadcasted_iota(jnp.int32, (HEAD, FFT), 0)
        return jnp.where(lane // 4 == row, 1.0, 0.0).astype(F32)

    four = jnp.dot(
        smt[8:16, head_cols],
        repeat_matrix(),
        precision=lax.Precision.HIGHEST,
        preferred_element_type=F32,
    )
    lane8 = lax.broadcasted_iota(jnp.int32, (8, FFT), 1)
    row8 = lax.broadcasted_iota(jnp.int32, (8, FFT), 0)
    bias[1:2, :] = jnp.sum(jnp.where(lane8 % 4 + 1 == row8, four, 0.0), axis=0, keepdims=True)

    for part in to_r[0]:
        part.end()
    copy_out = [pltpu.make_async_copy(ti, oi, local.at[0])]
    copy_out[0].start()

    def norms(u):
        def chunk(r, carry):
            at_rows = (r // 16, pl.ds(pl.multiple_of(r % 16 * 16, 16), 16), slice(None))
            in_rows = (at_rows[0], u, *at_rows[1:])
            xf = xv[in_rows].astype(F32)
            average = jnp.mean(xf, axis=1, keepdims=True)
            centred = xf - average
            var = jnp.mean(centred * centred, axis=1, keepdims=True)
            inverse = lax.rsqrt(var + NORM_EPS)
            xhat = centred * inverse
            at[at_rows] = (xhat * smt[0:1, :] + smt[1:2, :]).astype(BF)
            a2v[in_rows] = (xhat * smt[2:3, :] + smt[3:4, :]).astype(BF)
            lanes = lax.broadcasted_iota(jnp.int32, (16, 128), 1)
            stats[in_rows] = jnp.where(lanes == 0, average, inverse)
            return carry

        lax.fori_loop(0, 2 * TOK // 16, chunk, 0, unroll=4)

    def place_of(k):
        return k % 2 * 2 + k // 2

    def events(k, table):
        for when, what in table.items():

            @pl.when(k == when)
            def _(what=what):
                for fn in what:
                    fn()

    def staged(buffer, out, u, sem):
        return pltpu.make_async_copy(buffer, out.at[:, u], out_sem.at[sem])

    def free(buffer, out, k, sem):
        @pl.when(k >= 1)
        def _():
            staged(buffer, out, 0, sem).wait()

    def forward_keys(s):
        for ops, plan in keys:
            seen = set()
            for i, bit in plan:
                if i != bit:
                    if i ^ bit not in seen:
                        ops[i ^ bit](s).wait_recv()
                        seen.add(i ^ bit)
                    ops[i](s).start()

    def hidden_units(k):
        u = place_of(k)
        hidden = jnp.dot(
            a2v[:, u].reshape(RUN, D), tu[...].reshape(D, FFT), preferred_element_type=F32
        )
        slope[:, u] = (hidden + bias[1:2, :]).reshape(2, TOK, FFT)
        free(ztile, zo, k, 1)

        def chunk(r, carry):
            at_rows = (r // 16, pl.ds(pl.multiple_of(r % 16 * 16, 16), 16), slice(None))
            in_rows = (at_rows[0], u, *at_rows[1:])
            h = slope[in_rows]
            bell = jnp.exp(-0.5 * h * h)
            t = 1.0 / (1.0 + (0.3275911 * 0.5**0.5) * jnp.abs(h))
            series = t * (
                0.254829592
                + t * (-0.284496736 + t * (1.421413741 + t * (-1.453152027 + t * 1.061405429)))
            )
            tail = 0.5 * series * bell
            phi = jnp.where(h < 0.0, tail, 1.0 - tail)
            ztile[at_rows] = (h * phi).astype(BF)
            slope[in_rows] = phi + h * bell * (1.0 / math.sqrt(2.0 * math.pi))
            return carry

        lax.fori_loop(0, 2 * TOK // 16, chunk, 0, unroll=2)
        staged(ztile, zo, u, 1).start()

    def projections(k):
        u = place_of(k)
        free(at, a1g, k, 0)
        norms(u)
        joint = (
            jnp.dot(
                at[...].reshape(RUN, D), ti[...].reshape(D, 3 * HEAD), preferred_element_type=F32
            )
            + bias[0:1, : 3 * HEAD]
        )
        staged(at, a1g, u, 0).start()
        half = HEAD // 2
        cs, sn = cosine[:, u].reshape(RUN, half), sine[:, u].reshape(RUN, half)
        for p, (dst, scale) in enumerate(((qo, HEAD**-0.5), (kt, None))):
            one = joint[:, p * HEAD : p * HEAD + half]
            two = joint[:, p * HEAD + half : (p + 1) * HEAD]
            for at_col, value in ((0, one * cs - two * sn), (half, two * cs + one * sn)):
                value = value.astype(BF)
                if scale is not None:
                    value = (value.astype(F32) * scale).astype(BF)
                dst[:, u, :, at_col : at_col + half] = value.reshape(2, TOK, half)
        vt[:, u] = joint[:, 2 * HEAD :].astype(BF).reshape(2, TOK, HEAD)
        for core in range(2):
            for ops, plan in keys:
                for i, bit in plan:
                    if i == bit:
                        ops[i](core * 4 + u).start()

    def first(k, carry):
        events(
            k,
            {
                0: [lambda: x_t.wait(4)],
                1: [
                    lambda: [p.advance() for p in to_r[1]],
                    lambda: x_t.wait(2),
                    lambda: x_t.start(6),
                    lambda: start(to_t[3]),
                    lambda: start(to_t[2]),
                    lambda: x_t.wait(6),
                ],
                2: [
                    lambda: x_t.wait(1),
                    lambda: x_t.start(3, 5),
                    lambda: [p.end() for p in to_r[1]],
                    lambda: pltpu.make_async_copy(tu, ou, local.at[1]).start(),
                ],
                3: [
                    lambda: wait(to_t[3]),
                    lambda: wait(to_t[2]),
                    lambda: [p.begin() for p in to_r[3] + to_r[2]],
                    lambda: g_t.start(1, 4),
                ],
                4: [lambda: x_t.wait(5)],
                5: [
                    lambda: [p.advance() for p in to_r[3] + to_r[2]],
                    lambda: x_t.wait(3),
                    lambda: x_t.start(7),
                    lambda: g_t.start(2),
                    lambda: x_t.wait(7),
                ],
                7: [lambda: g_t.wait(1), lambda: g_t.start(3, 5)],
            },
        )
        late = k // 4

        @pl.when(k % 4 < 2)
        def _():
            projections(k - 2 * late)

        @pl.when(k % 4 >= 2)
        def _():
            hidden_units(k - 2 - 2 * late)

        @pl.when((k == 3) | (k >= 5))
        def _():
            pair = k - 3 - late
            for core in range(2):
                forward_keys(core * 4 + place_of(pair))

        return carry

    lax.fori_loop(0, 8, first, 0)
    own_out = [
        pltpu.make_async_copy(kt, kg.at[0], local.at[4]),
        pltpu.make_async_copy(vt, vg.at[0], local.at[5]),
        pltpu.make_async_copy(xv, xg, local.at[6]),
        pltpu.make_async_copy(a2v, a2g, local.at[8]),
    ]
    for copy in own_out:
        copy.start()
    copy_out.append(pltpu.make_async_copy(tu, ou, local.at[1]))

    def finish_keys(s, carry):
        for ops, plan in keys:
            used = {i ^ bit for i, bit in plan if i != bit}
            for i, bit in plan:
                if i not in used:
                    ops[i](s).wait_recv()
        return carry

    for part in to_r[3] + to_r[2]:
        part.end()
    copy_out += [
        pltpu.make_async_copy(to, oo, local.at[2]),
        pltpu.make_async_copy(td, od, local.at[3]),
    ]
    copy_out[2].start()
    copy_out[3].start()
    dhsum[...] = jnp.zeros_like(dhsum)

    def third(k, carry):
        u = place_of(k)
        events(
            k,
            {
                0: [lambda: g_t.wait(4)],
                1: [lambda: g_t.wait(2), lambda: g_t.start(6), lambda: g_t.wait(6)],
                2: [lambda: g_t.wait(5)],
                3: [lambda: g_t.wait(3), lambda: g_t.start(7), lambda: g_t.wait(7)],
            },
        )
        free(dht, dho, k, 2)
        pltpu.make_async_copy(gv.at[:, u], gg.at[:, u], g_sem.at[u]).start()
        grad = gv[:, u].reshape(RUN, D)
        dz = jnp.dot(grad, td[...].reshape(D, FFT), preferred_element_type=F32)
        dh = (dz * slope[:, u].reshape(RUN, FFT)).astype(BF)
        dht[...] = dh.reshape(2, TOK, FFT)
        staged(dht, dho, u, 2).start()
        dhsum[0:1, :] += jnp.sum(dh.astype(F32), axis=0, keepdims=True)
        dout[:, u] = (
            jnp.dot(grad, to[...].reshape(D, HEAD), preferred_element_type=F32)
            .astype(BF)
            .reshape(2, TOK, HEAD)
        )
        return carry

    lax.fori_loop(0, 4, third, 0)
    four = jnp.dot(
        jnp.where(lane8 % 4 + 1 == row8, dhsum[0:1, :], 0.0),
        repeat_matrix().T,
        precision=lax.Precision.HIGHEST,
        preferred_element_type=F32,
    )
    sums[...] = jnp.zeros_like(sums)
    sums[8:16, head_cols] = four
    sums[8:9, :] = jnp.sum(gv[0, 0].astype(F32), axis=0, keepdims=True)
    sums[7:8, :] = sums[8:9, :]
    lax.fori_loop(0, 8, finish_keys, 0)
    for sem, (buffer, out) in enumerate(((at, a1g), (ztile, zo), (dht, dho))):
        staged(buffer, out, 0, sem).wait()
    for copy in copy_out + own_out:
        copy.wait()
    for u in range(4):
        pltpu.make_async_copy(gv.at[:, u], gg.at[:, u], g_sem.at[u]).wait()
    net.finish()


def forward(n, x, gy, weights, small, lengths, frequency):
    rb = D // n
    R = n // 8

    def shape(*dims, kind=BF):
        return jax.ShapeDtypeStruct(dims, kind)

    w_shapes = [(4, R, 2 * rb, parts * width) for parts, width in WEIGHTS]
    block, cols, head = (2, 4, TOK, D), (2, 4, TOK, FFT), (2, 4, TOK, HEAD)
    outs = [shape(*block) for _ in range(4)]
    outs += [shape(*w) for w in w_shapes]
    outs += [shape(*head), shape(R, *head), shape(R, *head), shape(*cols), shape(*cols)]
    outs += [shape(*head), shape(SMALLR, D, kind=F32), shape(SMALLR, D, kind=F32)]
    outs += [shape(2, 4, TOK, 128, kind=F32)]
    outs += [shape(2, 4, TOK, HEAD // 2, kind=F32) for _ in range(2)]
    out_specs = [ANY] * 8 + [VM] + [ANY] * 4 + [VM] * 6
    scratch = [
        pltpu.VMEM(block, BF),
        pltpu.VMEM(block, BF),
        pltpu.VMEM((4, R, 2 * rb, 128), F32),
        *[pltpu.VMEM(w, BF) for w in w_shapes],
        pltpu.VMEM(cols, F32),
        pltpu.VMEM(block, BF),
        pltpu.VMEM(head, BF),
        pltpu.VMEM(head, BF),
        pltpu.VMEM((2, TOK, D), BF),
        pltpu.VMEM((2, TOK, FFT), BF),
        pltpu.VMEM((2, TOK, FFT), BF),
        pltpu.VMEM((8, FFT), F32),
        pltpu.VMEM((8, FFT), F32),
    ]
    copies = 7 + 7 * 6 + (R - 1) * (1 + 8 + 2 * 8) + 14

    def kernel(*refs):
        forward_kernel(n, lengths.shape[0], *refs)

    return pl.pallas_call(
        kernel,
        out_shape=outs,
        in_specs=[ANY] * 7 + [pl.BlockSpec(memory_space=pltpu.SMEM), VM],
        out_specs=out_specs,
        scratch_shapes=[
            *scratch,
            pltpu.SemaphoreType.DMA((copies,)),
            pltpu.SemaphoreType.DMA((copies,)),
            pltpu.SemaphoreType.DMA((16,)),
            pltpu.SemaphoreType.DMA((3,)),
            pltpu.SemaphoreType.DMA((4,)),
        ],
        compiler_params=pltpu.CompilerParams(
            collective_id=0, has_side_effects=True, vmem_limit_bytes=62 * MIB
        ),
    )(x, gy, *weights, small, lengths, frequency)


class SumT:
    def __init__(self, copies, place, data, slots, out):
        self.copies, self.place, self.data, self.slots, self.out = copies, place, data, slots, out
        self.ops = {}
        self.cur = {s: data.at[s] for s in range(8)}

    def send(self, s):
        hop = top_bit(s)
        self.ops[s] = self.copies.remote(self.cur[s], self.slots.at[s - 1], self.place.dev_t(hop))

    def add(self, s):
        to = s - top_bit(s)
        self.ops[s].wait_recv()
        slot = self.slots.at[s - 1]
        if to == 0 and s == 1:
            add_rows(self.out, self.cur[0], slot)
        else:
            add_rows(slot, self.cur[to], slot)
            self.cur[to] = slot

    def start(self):
        for s in (6, 7, 5, 4):
            self.send(s)

    def middle(self):
        for s in (6, 7):
            self.add(s)
            self.send(s - 4)
        self.add(5)

    def late(self):
        self.add(3)
        self.send(1)
        self.add(4)
        self.add(2)

    def end(self):
        self.add(1)


class SumR:
    def __init__(self, copies, place, piece, slots, order):
        self.copies, self.place, self.slots = copies, place, slots
        self.steps = collected(order)
        self.cur = {i: piece(i) for i in range(1 << len(order))}
        self.ops = {}

    def send(self, step):
        bit, members = self.steps[step]
        for i in members:
            self.ops[i] = self.copies.remote(
                self.cur[i], self.slots.at[i - 1], self.place.dev_r(bit)
            )

    def add(self, step):
        bit, members = self.steps[step]
        for i in members:
            self.ops[i].wait_recv()
            slot = self.slots.at[i - 1]
            add_rows(slot, self.cur[i ^ bit], slot)
            self.cur[i ^ bit] = slot


def return_keys_kernel(n, have, *refs):
    place = Place(n)
    refs = list(refs)
    count = len(have)
    ins, refs = refs[:count], refs[count:]
    outs, refs = refs[:count], refs[count:]
    slots, (send, recv) = refs[:count], refs[count:]
    copies = Copies(send, recv)
    both = orders(place.bits)
    r_group = [1 << b for b in range(place.bits)] if set(have) - {"p"} else []
    t_group = (1, 2, 4) if "p" in have else ()
    greet(place, t_group, r_group)
    total, sums = None, []
    for name, src, dst, slot in zip(have, ins, outs, slots):
        if name == "p":
            total = SumT(copies, place, src, slot, dst)
        else:
            order = both[0] if name == "k" else both[1]
            sums.append((SumR(copies, place, lambda i, src=src: src.at[i], slot, order), dst))
    for part, _ in sums:
        part.send(0)
    if total:
        total.start()
        total.middle()
    for step in range(place.bits):
        for part, _ in sums:
            part.add(step)
            if step + 1 < place.bits:
                part.send(step + 1)
    if total:
        total.late()
    for part, dst in sums:
        copy = copies.local(part.cur[0], dst)
        copy.wait()
    if total:
        total.end()
    copies.finish()


def return_keys(n, ins, collective_id):
    R = n // 8
    outs, scratch, copies = [], [], 0
    for name in ins:
        if name == "p":
            outs.append(jax.ShapeDtypeStruct((TOK, D), F32))
            scratch.append(pltpu.VMEM((7, TOK, D), BF))
            copies += 7
        else:
            outs.append(jax.ShapeDtypeStruct((8, TOK, HEAD), BF))
            scratch.append(pltpu.VMEM((R - 1, 8, TOK, HEAD), BF))
            copies += R

    def kernel(*refs):
        return_keys_kernel(n, tuple(ins), *refs)

    out = call(
        kernel,
        tuple(ins.values()),
        [VM] * len(ins),
        outs,
        [VM] * len(ins),
        scratch,
        collective_id,
        copies,
    )
    return dict(zip(ins, out))


def return_grads_kernel(
    n, gi, gu, go, gd, e, small, oi, ou, oo, od, oe, osmall, si, su, so, sd, se, ss, send, recv
):
    place = Place(n)
    copies = Copies(send, recv)
    rb = D // n
    both = orders(place.bits)
    greet(place, range(1, 8), [1 << b for b in range(place.bits)])
    total = SumT(copies, place, e, se, oe)
    total.start()

    tasks = []
    for src, slot, dst, (parts, width) in zip(
        (gu, gd, gi, go), (su, sd, si, so), (ou, od, oi, oo), [WEIGHTS[k] for k in (1, 3, 0, 2)]
    ):
        for half in range(2):

            def piece(i, src=src, half=half):
                return src.at[pl.ds(2 * half, 2), place.rr_of(i)]

            part = SumR(copies, place, piece, slot.at[half], both[half])
            tasks.append((part, half, dst, parts, width))
    small_sum = SumR(copies, place, lambda i: small.at[:, place.rr_of(i)], ss, both[0])
    for part, *_ in tasks:
        part.send(0)
    small_sum.send(0)
    total.middle()
    for step in range(place.bits):
        for part, *_ in tasks:
            part.add(step)
            if step + 1 < place.bits:
                part.send(step + 1)
        small_sum.add(step)
        if step + 1 < place.bits:
            small_sum.send(step + 1)
    total.late()

    finals = {}
    for k in range(4):
        pieces = [tasks[2 * k + half][0].cur[0] for half in range(2)]
        finals[k] = pieces
    ops = []
    for k in range(4):
        _, _, dst, parts, width = tasks[2 * k]
        for zz in range(4):
            for cc in range(2):
                src = finals[k][zz // 2].at[zz % 2, pl.ds(cc * rb, rb), :]
                ops.append((zz, cc, src, dst, parts, width))
    sends = []
    for k in range(4):
        _, _, dst, parts, width = tasks[2 * k]
        store = tasks[2 * k][0].slots
        slot = store
        del slot
        for s in range(8):
            for p in range(parts):
                cols = pl.ds(pl.multiple_of(p * D + place.t * width, 128), width)
                sends.append((k, s, p, cols, dst, width))
    remote = []
    joined = {}
    for k, (ref, outbuf) in enumerate(((gu, ou), (gd, od), (gi, oi), (go, oo))):
        del ref, outbuf
        joined[k] = finals[k]
    for k, s, p, cols, dst, width in sends:
        base = (su, sd, si, so)[k]
        last = tasks[2 * k][0].steps[-1][1][0], tasks[2 * k + 1][0].steps[-1][1][0]
        zt = place.zt_of(s)
        rows = pl.ds(pl.multiple_of(place.c_of(s) * rb, rb), rb)
        which = zt // 2
        index = (1 - which) * (last[0] - 1) + which * (last[1] - 1)
        src = base.at[which, index, zt % 2, rows, pl.ds(p * width, width)]
        if s == 0:
            remote.append(("local", copies.local(src, dst.at[:, cols])))
        else:
            remote.append(("remote", copies.remote(src, dst.at[:, cols], place.dev_t(s))))
    last = small_sum.steps[-1][1][0] - 1
    for s in range(8):
        rows = pl.ds(pl.multiple_of(place.c_of(s) * SMALLR, SMALLR), SMALLR)
        src = ss.at[last, place.zt_of(s), rows, :]
        if s == 0:
            remote.append(("local", copies.local(src, osmall.at[place.t])))
        else:
            remote.append(("remote", copies.remote(src, osmall.at[place.t], place.dev_t(s))))
    total.end()
    for kind, copy in remote:
        if kind == "local":
            copy.wait()
        else:
            copy.wait_recv()
    copies.finish()


def return_grads(n, grads, e, small, collective_id):
    R = n // 8
    rb = D // n
    outs = [jax.ShapeDtypeStruct((rb, parts * D if parts > 1 else HEADS * width), BF) for parts, width in WEIGHTS]
    outs += [jax.ShapeDtypeStruct((TOK, D), F32), jax.ShapeDtypeStruct((8, SMALLR, 128), F32)]
    scratch = [
        pltpu.VMEM((2, R - 1, 2, 2 * rb, parts * width), BF) for parts, width in WEIGHTS
    ] + [
        pltpu.VMEM((7, TOK, D), BF),
        pltpu.VMEM((R - 1, 4, 2 * SMALLR, 128), F32),
    ]
    copies = 7 + 9 * (R - 1) + 8 * 6 + 8

    def kernel(*refs):
        return_grads_kernel(n, *refs)

    return call(
        kernel,
        (*grads, e, small),
        [VM] * 6,
        outs,
        [ANY] * 4 + [VM, ANY],
        scratch,
        collective_id,
        copies,
    )


WIDE = 512


class FoldT:
    def __init__(self, net, place, data, cs, zs, ys, out):
        self.data, self.cs, self.zs, self.ys, self.out = data, cs, zs, ys, out
        self.hop_c = net.add(lambda k: (data.at[k], cs.at[k], place.dev_t(4)), 4)
        self.hop_z0 = net.add(lambda k: (cs.at[2 + k], zs.at[k], place.dev_t(2)), 2)
        self.hop_z1 = net.add(lambda k: (zs.at[1], ys.at[0], place.dev_t(1)))

    @staticmethod
    def order(idx):
        return 7 - idx // 4 - 2 * (idx % 4)

    def loop(self, make, emit, after):
        def step(idx, carry):
            s = self.order(idx)
            make(s, idx)
            k = s % 4

            def far(where, value):
                self.data[(k, *where)] = value.astype(BF)

            def near(where, value):
                self.cs[(k, *where)] = (value + self.cs[(k, *where)].astype(F32)).astype(BF)

            @pl.when(s >= 4)
            def _():
                emit(s, idx, far)
                self.hop_c(k).start()

            @pl.when(s < 4)
            def _():
                self.hop_c(k).wait_recv()
                emit(s, idx, near)

                @pl.when(s >= 2)
                def _():
                    self.hop_z0(s - 2).start()

            after(idx)
            return carry

        lax.fori_loop(0, 8, step, 0)

    def turn_z1(self):
        self.hop_z0(1).wait_recv()
        add_rows(self.zs.at[1], self.cs.at[1], self.zs.at[1])
        self.hop_z1().start()

    def turn_own(self):
        self.hop_z0(0).wait_recv()
        add_rows(self.zs.at[0], self.cs.at[0], self.zs.at[0])

    def end(self):
        self.hop_z1().wait_recv()
        add_rows(self.out, self.zs.at[0], self.ys.at[0])


def fold_scratch():
    return [
        pltpu.VMEM((4, TOK, D), BF),
        pltpu.VMEM((4, TOK, D), BF),
        pltpu.VMEM((2, TOK, D), BF),
        pltpu.VMEM((1, TOK, D), BF),
    ]


class FoldR:
    def __init__(self, net, place, far, own, slots, order):
        one, two = order
        self.own, self.slots = own, slots
        self.both = net.add(lambda k: (far(3), slots.at[0], place.dev_r(one)))
        self.first = net.add(lambda k: (far(one), slots.at[1], place.dev_r(one)))
        self.second = net.add(lambda k: (slots.at[0], slots.at[2], place.dev_r(two)))

    def begin(self):
        self.both().start()
        self.first().start()

    def advance(self):
        self.both().wait_recv()
        add_rows(self.slots.at[0], self.own.at[1], self.slots.at[0])
        self.second().start()

    def gather(self):
        self.first().wait_recv()
        add_rows(self.slots.at[1], self.own.at[0], self.slots.at[1])

    def end(self, out=None):
        self.second().wait_recv()
        out = self.slots.at[2] if out is None else out
        add_rows(out, self.slots.at[1], self.slots.at[2])


def weight_folds(n, net, place, grads, own, slots):
    view = grads.reshape(4, n // 8, 2 * (D // n), grads.shape[-1])
    both = orders(2)
    halves, pieces = [], []
    for h in range(2):

        def piece(i, h=h):
            return view.at[pl.ds(2 * h, 2), place.rr_of(i)]

        halves.append(FoldR(net, place, piece, own.at[h], slots.at[h], both[h]))
        pieces.append((piece(0), own.at[h, 0]))
        pieces.append((piece(both[h][1]), own.at[h, 1]))
    return halves, pieces


def gradient_tiles(lhs, tiles, sem, products):
    wide = tiles.shape[-1]
    count = D // wide

    def fetch(f):
        cols = pl.ds(pl.multiple_of(f * wide, wide), wide)
        return pltpu.make_async_copy(lhs.at[:, :, cols], tiles.at[f % 2], sem.at[f % 2])

    def put(f, stage, out, sems):
        rows = pl.ds(pl.multiple_of(f * wide, wide), wide)
        return pltpu.make_async_copy(stage.at[f % 2], out.at[rows, :], sems.at[f % 2])

    fetch(0).start()

    def step(f, carry):
        fetch(f).wait()

        @pl.when(f + 1 < count)
        def _():
            fetch(f + 1).start()

        left = tiles[f % 2].reshape(8 * TOK, wide)
        for rhs, stage, out, sems in products:

            @pl.when(f >= 2)
            def _(stage=stage, out=out, sems=sems):
                put(f - 2, stage, out, sems).wait()

            right = rhs[...].reshape(8 * TOK, rhs.shape[-1])
            stage[f % 2] = contract_rows(left, right).astype(BF)
            put(f, stage, out, sems).start()
        return carry

    lax.fori_loop(0, count, step, 0)
    for f in (count - 2, count - 1):
        for _, stage, out, sems in products:
            put(f, stage, out, sems).wait()


def half_fold(net, place, grads, h, own, slots):
    order = orders(2)[h]
    cols = pl.ds(h * (FFT // 2), FFT // 2)

    def piece(i):
        return grads.at[:, place.rr_of(i), :, cols]

    fold = FoldR(net, place, piece, own, slots, order)
    return fold, [(piece(0), own.at[0]), (piece(order[1]), own.at[1])]


def return_one_kernel(
    n, dk, dv, o, z, w_out, w_down, gy, a2, dh,
    p_own, dk_own, dv_own, up_sum, g_out, g_down, g_up,
    zov, wdo, dhv, kown, vown, data, cs, zs, ys, ks, vs, tiles, st_wide, st_head, uown, us,
    send, recv, load, fetch_sem, put_sem, near,
):
    place = Place(n)
    net = Net(send, recv)
    greet(place, (1, 2, 4), (1, 2))
    both = orders(2)
    keys = FoldR(net, place, lambda i: dk.at[i], kown, ks, both[0])
    values = FoldR(net, place, lambda i: dv.at[i], vown, vs, both[1])
    total = FoldT(net, place, data, cs, zs, ys, p_own)
    up, pieces = half_fold(
        net, place, g_up.reshape(4, n // 8, 2 * (D // n), FFT), 0, uown, us
    )
    keys.both().start()
    values.both().start()

    loads = [
        pltpu.make_async_copy(src, dst, load.at[k])
        for k, (src, dst) in enumerate(
            (
                (z, zov.at[:, :, :FFT]),
                (o, zov.at[:, :, FFT:]),
                (w_down, wdo.at[:, :FFT]),
                (w_out, wdo.at[:, FFT:]),
                (dk.at[2], kown.at[1]),
                (dv.at[1], vown.at[1]),
                (dk.at[0], kown.at[0]),
                (dv.at[0], vown.at[0]),
                (dh, dhv),
            )
        )
    ]
    for copy in loads:
        copy.start()
    for copy in loads[:4]:
        copy.wait()

    def make(s, idx):
        del s, idx

    def emit(s, idx, put):
        put((slice(None), slice(None)), contract_cols(zov[s], wdo[...]))

    def after(idx):
        @pl.when(idx == 3)
        def _():
            keys.first().start()
            values.first().start()

        @pl.when(idx == 6)
        def _():
            for copy in loads[4:]:
                copy.wait()
            keys.advance()
            values.advance()

    total.loop(make, emit, after)
    total.turn_z1()
    gradient_tiles(a2, tiles, fetch_sem, [(dhv, st_wide, g_up, put_sem.at[0])])
    own_loads = [
        pltpu.make_async_copy(src, dst, near.at[k]) for k, (src, dst) in enumerate(pieces)
    ]
    up.begin()
    for copy in own_loads:
        copy.start()
    keys.gather()
    values.gather()
    gradient_tiles(
        gy, tiles, fetch_sem,
        [
            (zov.at[:, :, :FFT], st_wide, g_down, put_sem.at[0]),
            (zov.at[:, :, FFT:], st_head, g_out, put_sem.at[1]),
        ],
    )
    for copy in own_loads:
        copy.wait()
    up.advance()
    keys.end(dk_own)
    values.end(dv_own)
    total.turn_own()
    up.gather()
    up.end(up_sum)
    total.end()
    net.finish()


def return_one(n, dk, dv, o, z, w_out, w_down, gy, a2, dh):
    rows = 2 * (D // n)
    head, cols = (8, TOK, HEAD), (8, TOK, FFT)
    half = (4, rows, FFT // 2)
    outs = [
        jax.ShapeDtypeStruct((TOK, D), F32),
        jax.ShapeDtypeStruct(head, BF),
        jax.ShapeDtypeStruct(head, BF),
        jax.ShapeDtypeStruct(half, BF),
        jax.ShapeDtypeStruct((D, HEAD), BF),
        jax.ShapeDtypeStruct((D, FFT), BF),
        jax.ShapeDtypeStruct((D, FFT), BF),
    ]
    scratch = [
        pltpu.VMEM((8, TOK, FFT + HEAD), BF),
        pltpu.VMEM((D, FFT + HEAD), BF),
        pltpu.VMEM(cols, BF),
        pltpu.VMEM((2, *head), BF),
        pltpu.VMEM((2, *head), BF),
        *fold_scratch(),
        pltpu.VMEM((3, *head), BF),
        pltpu.VMEM((3, *head), BF),
        pltpu.VMEM((2, 8, TOK, WIDE), BF),
        pltpu.VMEM((2, WIDE, FFT), BF),
        pltpu.VMEM((2, WIDE, HEAD), BF),
        pltpu.VMEM((2, *half), BF),
        pltpu.VMEM((3, *half), BF),
    ]

    def kernel(*refs):
        return_one_kernel(n, *refs)

    return pl.pallas_call(
        kernel,
        out_shape=outs,
        in_specs=[ANY] * 9,
        out_specs=[VM] * 4 + [ANY] * 3,
        scratch_shapes=[
            *scratch,
            pltpu.SemaphoreType.DMA((16,)),
            pltpu.SemaphoreType.DMA((16,)),
            pltpu.SemaphoreType.DMA((9,)),
            pltpu.SemaphoreType.DMA((2,)),
            pltpu.SemaphoreType.DMA((2, 2)),
            pltpu.SemaphoreType.DMA((2,)),
        ],
        compiler_params=pltpu.CompilerParams(
            collective_id=2, has_side_effects=True, vmem_limit_bytes=62 * MIB
        ),
    )(dk, dv, o, z, w_out, w_down, gy, a2, dh)


def return_two_kernel(
    n, gi, gu0, gu, go, gd, dq, dk, dv, a1, x, dh, w_in, w_up, cosine, sine, smt, stats, sums,
    oi, ou, oo, od, e_own, osmall, gi_out,
    dqv, dkv, dvv, djp, djn, dhv, wi, wu, xt, cst, snt, data, cs, zs, ys, tile, other,
    uown, us, ui, uo, ud, si, so, sd, term, blocks, sslots, tiles, st_in,
    send, recv, load, near, x_sem, fetch_sem, put_sem, last_sem,
):
    del gi
    place = Place(n)
    net = Net(send, recv)
    rb = D // n
    R = place.R
    both = orders(2)
    greet(place, range(1, 8), (1, 2))
    names = ((gd, ud, sd, od, 3), (go, uo, so, oo, 2), (gi_out, ui, si, oi, 0))
    parts, pieces = [], []
    for src, own, slots, _, _ in names:
        halves, near_pieces = weight_folds(n, net, place, src, own, slots)
        parts.append(halves)
        pieces += near_pieces
    small = FoldR(
        net, place, lambda i: blocks.at[place.rr_of(i)], None, sslots, both[0]
    )
    total = FoldT(net, place, data, cs, zs, ys, e_own)
    up, up_pieces = half_fold(net, place, gu.reshape(4, R, 2 * rb, FFT), 1, uown, us)

    finals = []
    ends = []
    for _, _, slots, dst, k in names:
        count, width = WEIGHTS[k]
        ends.append(
            (
                lambda zt, rows, cols, slots=slots: slots.at[zt // 2, 2, zt % 2, rows, cols],
                dst, width, [(p * width, p * D) for p in range(count)],
            )
        )
    for h in range(2):
        summed = us.at[2] if h else gu0
        ends.append(
            (
                lambda zt, rows, cols, summed=summed: summed.at[zt, rows, cols],
                ou, FFT // 2, [(0, h * (FFT // 2))],
            )
        )
    for which, (summed, dst, width, spans) in enumerate(ends):
        stride = FFT if dst is ou else width
        ops = []
        for s in range(8):
            rows = pl.ds(pl.multiple_of(place.c_of(s) * rb, rb), rb)
            for p, (at, into) in enumerate(spans):
                cols = pl.ds(pl.multiple_of(into + place.t * stride, 128), width)
                piece = summed(place.zt_of(s), rows, pl.ds(at, width))
                if s == 0:
                    ops.append(
                        pltpu.make_async_copy(
                            piece, dst.at[:, cols], last_sem.at[which * 3 + p]
                        )
                    )
                else:
                    ops.append(
                        net.add(
                            lambda k, piece=piece, dst=dst, cols=cols, s=s: (
                                piece, dst.at[:, cols], place.dev_t(s),
                            )
                        )
                    )
        finals.append(ops)
    small_last = [
        net.add(
            lambda k, s=s: (
                sslots.at[2, place.zt_of(s)], osmall.at[place.t], place.dev_t(s),
            )
        )
        for s in range(1, 8)
    ]
    small_mine = pltpu.make_async_copy(
        sslots.at[2, place.zt], osmall.at[place.t], last_sem.at[15]
    )

    def send_finals(which):
        for k, op in enumerate(finals[which]):
            (op if k < len(ends[which][3]) else op()).start()

    def wait_finals(which):
        for k, op in enumerate(finals[which]):
            if k < len(ends[which][3]):
                op.wait()
            else:
                op().wait_recv()

    up.begin()
    send_finals(3)
    loads = [
        pltpu.make_async_copy(src, dst, load.at[k])
        for k, (src, dst) in enumerate(
            (
                (dq, dqv), (dk, dkv), (dv, dvv), (cosine, cst), (sine, snt),
                (w_in, wi), (dh, dhv), (w_up, wu),
            )
        )
    ]
    for copy in loads:
        copy.start()
    own_loads = [
        pltpu.make_async_copy(src, dst, near.at[k])
        for k, (src, dst) in enumerate(pieces + up_pieces)
    ]
    for copy in own_loads[:8] + own_loads[12:]:
        copy.start()

    def fetch_x(s, slot):
        return pltpu.make_async_copy(x.at[s], xt.at[slot], x_sem.at[slot])

    fetch_x(7, 0).start()
    term[...] = sums[...]
    shuffle = shuffle_matrix().astype(BF)
    head_cols = pl.ds(pl.multiple_of(place.t * HEAD, HEAD), HEAD)
    for copy in loads:
        copy.wait()
    chunk_cols = 256

    def joint(s):
        csn, sn = cst[s], snt[s]
        half = HEAD // 2
        for p, src in enumerate((dqv, dkv)):
            one = src[s, :, :half].astype(F32)
            two = src[s, :, half:].astype(F32)
            cols = slice(p * HEAD, (p + 1) * HEAD)
            djp[:, p * HEAD : p * HEAD + half] = (one * csn + two * sn).astype(BF)
            djp[:, p * HEAD + half : (p + 1) * HEAD] = (two * csn - one * sn).astype(BF)
            natural = contract_cols(djp[:, cols], shuffle)
            djn[s, :, cols] = natural.astype(BF)
            term[4 + p : 5 + p, head_cols] += jnp.sum(natural, axis=0, keepdims=True)
        value = dvv[s]
        djp[:, 2 * HEAD :] = value
        djn[s, :, 2 * HEAD :] = value
        term[6:7, head_cols] += jnp.sum(value.astype(F32), axis=0, keepdims=True)

    def make(s, idx):
        joint(s)
        fetch_x(s, idx % 2).wait()

        @pl.when(idx < 7)
        def _():
            fetch_x(total.order(idx + 1), (idx + 1) % 2).start()

        tile[...] = contract_cols(djp[...], wi[...])
        other[...] = contract_cols(dhv[s], wu[...])

    def emit(s, idx, put):
        average = stats[s, :, 0:1]
        inverse = stats[s, :, 1:2]

        def chunk(k, carry):
            cols = pl.ds(pl.multiple_of(k * chunk_cols, chunk_cols), chunk_cols)
            xhat = (xt[idx % 2, :, cols].astype(F32) - average) * inverse
            one, two = tile[:, cols], other[:, cols]
            for row, value in ((0, one * xhat), (1, one), (2, two * xhat), (3, two)):
                term[row : row + 1, cols] += jnp.sum(value, axis=0, keepdims=True)
            put((slice(None), cols), one * smt[0:1, cols] + two * smt[2:3, cols])
            return carry

        lax.fori_loop(0, D // chunk_cols, chunk, 0)

    def after(idx):
        @pl.when(idx == 1)
        def _():
            for part in parts[0]:
                part.begin()

        @pl.when(idx == 3)
        def _():
            for copy in own_loads[12:]:
                copy.wait()
            up.advance()

        @pl.when(idx == 4)
        def _():
            for part in parts[1]:
                part.begin()

        @pl.when(idx == 5)
        def _():
            up.gather()
            up.end()
            send_finals(4)

        @pl.when(idx == 6)
        def _():
            for copy in own_loads[:4]:
                copy.wait()
            for part in parts[0]:
                part.advance()
            total.turn_z1()

    total.loop(make, emit, after)

    for rr in range(R):
        for zt in range(4):
            at = (zt * R + rr) * 128
            blocks[rr, zt] = term[:, at : at + 128]
    small.both().start()
    small.first().start()
    gradient_tiles(a1, tiles, fetch_sem, [(djn, st_in, gi_out, put_sem)])
    for part in parts[2]:
        part.begin()
    for copy in own_loads[8:12]:
        copy.start()
    for part in parts[0]:
        part.gather()
        part.end()
    send_finals(0)
    for copy in own_loads[4:8]:
        copy.wait()
    for part in parts[1]:
        part.advance()
    small.both().wait_recv()
    sslots[0] = sslots[0] + blocks[place.rr_of(2)]
    small.second().start()
    for copy in own_loads[8:12]:
        copy.wait()
    for part in parts[2]:
        part.advance()
    for part in parts[1]:
        part.gather()
        part.end()
    send_finals(1)
    small.first().wait_recv()
    small.second().wait_recv()
    sslots[2] = sslots[2] + (sslots[1] + blocks[place.rr])
    small_mine.start()
    for op in small_last:
        op().start()
    for part in parts[2]:
        part.gather()
        part.end()
    send_finals(2)
    total.turn_own()
    total.end()
    for which in range(5):
        wait_finals(which)
    small_mine.wait()
    for op in small_last:
        op().wait_recv()
    net.finish()


def return_two(n, up_sum, g_up, g_out, g_down, dq, dk, dv, a1, x, dh, w_in, w_up, cosine, sine, smt, stats, sums):
    rb = D // n
    R = n // 8
    head, cols, block = (8, TOK, HEAD), (8, TOK, FFT), (8, TOK, D)
    outs = [jax.ShapeDtypeStruct((rb, HEADS * parts * width), BF) for parts, width in WEIGHTS]
    outs += [
        jax.ShapeDtypeStruct((TOK, D), F32),
        jax.ShapeDtypeStruct((8, SMALLR, 128), F32),
        jax.ShapeDtypeStruct((D, 3 * HEAD), BF),
    ]
    wide = [parts * width for parts, width in WEIGHTS]
    scratch = [
        pltpu.VMEM(head, F32),
        pltpu.VMEM(head, BF),
        pltpu.VMEM(head, BF),
        pltpu.VMEM((TOK, 3 * HEAD), BF),
        pltpu.VMEM((8, TOK, 3 * HEAD), BF),
        pltpu.VMEM(cols, BF),
        pltpu.VMEM((D, 3 * HEAD), BF),
        pltpu.VMEM((D, FFT), BF),
        pltpu.VMEM((2, TOK, D), BF),
        pltpu.VMEM((8, TOK, HEAD // 2), F32),
        pltpu.VMEM((8, TOK, HEAD // 2), F32),
        *fold_scratch(),
        pltpu.VMEM((TOK, D), F32),
        pltpu.VMEM((TOK, D), F32),
        pltpu.VMEM((2, 4, 2 * rb, FFT // 2), BF),
        pltpu.VMEM((3, 4, 2 * rb, FFT // 2), BF),
        *[pltpu.VMEM((2, 2, 2, 2 * rb, wide[k]), BF) for k in (0, 2, 3)],
        *[pltpu.VMEM((2, 3, 2, 2 * rb, wide[k]), BF) for k in (0, 2, 3)],
        pltpu.VMEM((SMALLR, D), F32),
        pltpu.VMEM((R, 4, SMALLR, 128), F32),
        pltpu.VMEM((3, 4, SMALLR, 128), F32),
        pltpu.VMEM((2, 8, TOK, HEAD), BF),
        pltpu.VMEM((2, HEAD, 3 * HEAD), BF),
    ]
    copies = 6 * 3 + 3 + 3 + 7 + 7 * 7 + 7

    def kernel(*refs):
        return_two_kernel(n, None, *refs)

    return pl.pallas_call(
        kernel,
        out_shape=outs,
        in_specs=[ANY] * 14 + [VM] * 3,
        out_specs=[ANY] * 4 + [VM] + [ANY] * 2,
        scratch_shapes=[
            *scratch,
            pltpu.SemaphoreType.DMA((copies,)),
            pltpu.SemaphoreType.DMA((copies,)),
            pltpu.SemaphoreType.DMA((8,)),
            pltpu.SemaphoreType.DMA((16,)),
            pltpu.SemaphoreType.DMA((2,)),
            pltpu.SemaphoreType.DMA((2,)),
            pltpu.SemaphoreType.DMA((2,)),
            pltpu.SemaphoreType.DMA((16,)),
        ],
        compiler_params=pltpu.CompilerParams(
            collective_id=3, has_side_effects=True, vmem_limit_bytes=62 * MIB
        ),
    )(up_sum, g_up, g_out, g_down, dq, dk, dv, a1, x, dh, w_in, w_up, cosine, sine, smt, stats, sums)


def token_row(base, core, size=RUN):
    lane = lax.broadcasted_iota(jnp.int32, (1, size), 1)
    return base + (lane + core * TOK) % RUN


def token_col(base, core, size=RUN):
    row = lax.broadcasted_iota(jnp.int32, (size, 1), 0)
    return base + (row + core * TOK) % RUN


def start_of(tokens, lengths, nseq):
    out, begin = tokens * 0, lengths[0] * 0
    for s in range(nseq):
        out = jnp.where(tokens >= begin, begin, out)
        begin = begin + lengths[s]
    return out


def run_facts(place, lengths, nseq, u):
    number = place.zt_of_run(u) * place.R + place.rr
    count = number - start_of(number * RUN, lengths, nseq) // RUN + 1
    return number, count, start_of(number * RUN + RUN - 1, lengths, nseq)


def scores_of(key, query):
    return lax.dot_general(key, query, (((1,), (1,)), ((), ())), preferred_element_type=F32)


def seen_mask(core, gq, gk, lengths, nseq):
    tq = token_row(gq * RUN, core)
    tk = token_col(gk * RUN, core)
    return (tk <= tq) & (tk >= start_of(tq, lengths, nseq))


def attend_kernel(
    n, nseq, lengths, q, dout, kg, vg, o, stats, m, l, acc, kv, sem
):
    u = pl.program_id(0)
    place = Place(n)
    number, count, last = run_facts(place, lengths, nseq, u)
    m[...] = jnp.full_like(m, NEGATIVE)
    l[...] = jnp.zeros_like(l)
    acc[...] = jnp.zeros_like(acc)

    def fetch(d, slot):
        far = number - d
        moved = (far // place.R) ^ place.zt
        i, ku = (far % place.R) ^ place.rr, moved % 2 * 2 + moved // 2
        return [
            pltpu.make_async_copy(src.at[i, :, ku], kv.at[slot, p], sem.at[slot, p])
            for p, src in enumerate((kg, vg))
        ]

    def block(slot, far, masked):
        query = q[...].reshape(RUN, HEAD)
        key = kv[slot, 0].reshape(RUN, HEAD)
        value = kv[slot, 1].reshape(RUN, HEAD)
        s = scores_of(key, query)
        if masked:
            s = jnp.where(seen_mask(place.c, number, number - far, lengths, nseq), s, NEGATIVE)
        old = m[0:1, :]
        new = jnp.maximum(old, jnp.max(s, axis=0, keepdims=True))
        p = jnp.exp(s - new)
        fade = jnp.exp(old - new)
        l[0:1, :] = l[0:1, :] * fade + jnp.sum(p, axis=0, keepdims=True)
        m[0:1, :] = new
        mixed = lax.dot_general(
            value, p.astype(BF), (((0,), (0,)), ((), ())), preferred_element_type=F32
        )
        acc[...] = acc[...] * fade + mixed

    for copy in fetch(0, 0):
        copy.start()

    def step(d, carry):
        slot = d % 2
        for copy in fetch(d, slot):
            copy.wait()

        @pl.when(d + 1 < count)
        def _():
            for copy in fetch(d + 1, 1 - slot):
                copy.start()

        edge = (d == 0) | ((number - d) * RUN < last)

        @pl.when(edge)
        def _():
            block(slot, d, True)

        @pl.when(jnp.logical_not(edge))
        def _():
            block(slot, d, False)

        return carry

    lax.fori_loop(0, count, step, 0)
    out = acc[...] / l[0:1, :]
    rows = out.T
    o[...] = rows.astype(BF).reshape(o.shape)
    grad = dout[...].reshape(RUN, HEAD).astype(F32).T
    stats[0, 0:1, :] = m[0:1, :] + jnp.log(l[0:1, :])
    stats[0, 1:2, :] = jnp.sum(out * grad, axis=0, keepdims=True)
    stats[0, 2:8, :] = jnp.zeros((6, RUN), F32)


def attend(n, lengths, q, dout, kg, vg):
    run = pl.BlockSpec((2, 1, TOK, HEAD), lambda u, *_: (0, u, 0, 0))

    def kernel(*refs):
        attend_kernel(n, lengths.shape[0], *refs)

    return pl.pallas_call(
        kernel,
        out_shape=[
            jax.ShapeDtypeStruct((2, 4, TOK, HEAD), BF),
            jax.ShapeDtypeStruct((4, 8, RUN), F32),
        ],
        grid_spec=pltpu.PrefetchScalarGridSpec(
            num_scalar_prefetch=1,
            grid=(4,),
            in_specs=[run, run, ANY, ANY],
            out_specs=[run, pl.BlockSpec((1, 8, RUN), lambda u, *_: (u, 0, 0))],
            scratch_shapes=[
                pltpu.VMEM((8, RUN), F32),
                pltpu.VMEM((8, RUN), F32),
                pltpu.VMEM((HEAD, RUN), F32),
                pltpu.VMEM((2, 2, 2, TOK, HEAD), BF),
                pltpu.SemaphoreType.DMA((2, 2)),
            ],
        ),
        compiler_params=pltpu.CompilerParams(vmem_limit_bytes=62 * MIB),
        cost_estimate=pl.CostEstimate(
            flops=4 * 16 * RUN * RUN * HEAD, bytes_accessed=12 * MIB, transcendentals=16 * RUN * RUN
        ),
    )(lengths, q, dout, kg, vg)


def attend_back_kernel(
    n, nseq, lengths, q, dout, stats, k, v, dq, dk, dv, tq, tk, tv, facts
):
    block_at = pl.program_id(0)
    steps = pl.num_programs(0)

    place = Place(n)

    @pl.when(block_at == 0)
    def _():
        tq[...] = jnp.zeros_like(tq)
        for u in range(4):
            for f, value in enumerate(run_facts(place, lengths, nseq, u)):
                facts[4 * f + u] = value

    tk[...] = jnp.zeros_like(tk)
    tv[...] = jnp.zeros_like(tv)
    here = place.zt_of_run(block_at % 4) * place.R + (place.rr ^ (block_at // 4))

    for u in range(4):
        far = facts[u] - here
        active = (far >= 0) & (far < facts[4 + u])
        edge = (far == 0) | (here * RUN < facts[8 + u])

        def block(masked, u=u):
            query = q[:, u].reshape(RUN, HEAD)
            grad = dout[:, u].reshape(RUN, HEAD)
            key = k[...].reshape(RUN, HEAD)
            value = v[...].reshape(RUN, HEAD)
            s = scores_of(key, query)
            p = jnp.exp(s - stats[u, 0:1, :])
            if masked:
                p = jnp.where(seen_mask(place.c, facts[u], here, lengths, nseq), p, 0.0)
            dp = scores_of(value, grad)
            ds = (p * (dp - stats[u, 1:2, :])).astype(BF)
            tv[...] += jnp.dot(p.astype(BF), grad, preferred_element_type=F32)
            tk[...] += jnp.dot(ds, query, preferred_element_type=F32)
            tq[u] += lax.dot_general(
                ds, key, (((0,), (0,)), ((), ())), preferred_element_type=F32
            )

        @pl.when(active & edge)
        def _(block=block):
            block(True)

        @pl.when(active & jnp.logical_not(edge))
        def _(block=block):
            block(False)

    dk[...] = tk[...].astype(BF).reshape(dk.shape)
    dv[...] = tv[...].astype(BF).reshape(dv.shape)

    @pl.when(block_at == steps - 1)
    def _():
        for u in range(4):
            dq[:, u] = (tq[u] * HEAD**-0.5).reshape(2, TOK, HEAD)


def attend_back(n, lengths, q, dout, stats, kg, vg):
    R = n // 8
    whole = pl.BlockSpec((2, 4, TOK, HEAD), lambda b, *_: (0, 0, 0, 0))
    key = pl.BlockSpec((1, 2, 1, TOK, HEAD), lambda b, *_: (b // 4, 0, b % 4, 0, 0))

    def kernel(*refs):
        attend_back_kernel(n, lengths.shape[0], *refs)

    return pl.pallas_call(
        kernel,
        out_shape=[
            jax.ShapeDtypeStruct((2, 4, TOK, HEAD), F32),
            jax.ShapeDtypeStruct((R, 2, 4, TOK, HEAD), BF),
            jax.ShapeDtypeStruct((R, 2, 4, TOK, HEAD), BF),
        ],
        grid_spec=pltpu.PrefetchScalarGridSpec(
            num_scalar_prefetch=1,
            grid=(4 * R,),
            in_specs=[
                whole,
                whole,
                pl.BlockSpec((4, 8, RUN), lambda b, *_: (0, 0, 0)),
                key,
                key,
            ],
            out_specs=[whole, key, key],
            scratch_shapes=[
                pltpu.VMEM((4, RUN, HEAD), F32),
                pltpu.VMEM((RUN, HEAD), F32),
                pltpu.VMEM((RUN, HEAD), F32),
                pltpu.SMEM((12,), jnp.int32),
            ],
        ),
        compiler_params=pltpu.CompilerParams(vmem_limit_bytes=62 * MIB),
        cost_estimate=pl.CostEstimate(
            flops=10 * 16 * RUN * RUN * HEAD, bytes_accessed=24 * MIB, transcendentals=16 * RUN * RUN
        ),
    )(lengths, q, dout, stats, kg, vg)


def adam_step(parameter, gradient, first_moment, second_moment, step_rate):
    first_new = BETA_ONE * first_moment + (1.0 - BETA_ONE) * gradient
    second_new = BETA_TWO * second_moment + (1.0 - BETA_TWO) * gradient * gradient
    first_hat = first_new * (1.0 / (1.0 - BETA_ONE**STEPS))
    second_hat = second_new * (1.0 / (1.0 - BETA_TWO**STEPS))
    parameter_new = parameter - step_rate * (
        first_hat / (jnp.sqrt(second_hat) + ADAM_EPS) + WEIGHT_DECAY * parameter
    )
    return (first_new, second_new, parameter_new)


def adam_kernel(rates, *refs):
    count = len(rates)
    x, gy, e, part, small = refs[:5]
    groups = [refs[5 + k * count : 5 + (k + 1) * count] for k in range(7)]
    block_out, token_grad = refs[5 + 7 * count :]
    for p, g, m, v, rate, p_out, m_out, v_out in zip(
        *groups[:4], rates, *groups[4:]
    ):
        m_out[...], v_out[...], p_out[...] = adam_step(
            p[...], g[...].astype(F32), m[...], v[...], rate
        )
    xf, grad = x[...].astype(F32), e[...]
    block_out[...] = (xf + part[...] + small[7:8, :] + small[8:9, :]).astype(BF)
    centred = xf - jnp.mean(xf, axis=-1, keepdims=True)
    inverse = lax.rsqrt(jnp.mean(centred * centred, axis=-1, keepdims=True) + NORM_EPS)
    xhat = centred * inverse
    token_grad[...] = gy[...].astype(F32) + inverse * (
        grad
        - jnp.mean(grad, axis=-1, keepdims=True)
        - xhat * jnp.mean(grad * xhat, axis=-1, keepdims=True)
    )


def adam(own, params, grads, firsts, seconds, rates):
    steps = 8

    def spec(a):
        return pl.BlockSpec((a.shape[0], a.shape[1] // steps), lambda k: (0, k))

    tok = pl.BlockSpec((TOK // steps, D), lambda k: (k, 0))
    small = pl.BlockSpec((SMALLR, D), lambda k: (0, 0))
    arrays = [*params, *grads, *firsts, *seconds]
    outs = [jax.ShapeDtypeStruct(p.shape, F32) for _ in range(3) for p in params]
    own_outs = [jax.ShapeDtypeStruct((TOK, D), BF), jax.ShapeDtypeStruct((TOK, D), F32)]

    def kernel(*refs):
        adam_kernel(rates, *refs)

    out = pl.pallas_call(
        kernel,
        out_shape=[*outs, *own_outs],
        grid=(steps,),
        in_specs=[tok] * 4 + [small] + [spec(a) for a in arrays],
        out_specs=[spec(a) for a in outs] + [tok] * 2,
        compiler_params=pltpu.CompilerParams(vmem_limit_bytes=62 * MIB),
    )(*own, *arrays)
    count = len(params)
    return [out[k * count : (k + 1) * count] for k in range(3)] + list(out[3 * count :])


def contract_rows(left, right):
    return lax.dot_general(left, right, (((0,), (0,)), ((), ())), preferred_element_type=F32)


def contract_cols(left, right):
    return lax.dot_general(left, right, (((1,), (1,)), ((), ())), preferred_element_type=F32)


def paired(columns):
    turned, half = HEAD // 8, HEAD // 2
    heads = columns.reshape(columns.shape[0], -1, HEAD)
    cut = 2 * turned + half - turned
    order = [(0, turned), (2 * turned, cut), (turned, 2 * turned), (cut, HEAD)]
    return jnp.concatenate([heads[..., a:b] for a, b in order], axis=-1).reshape(columns.shape)


def unpaired(columns):
    turned, half = HEAD // 8, HEAD // 2
    heads = columns.reshape(columns.shape[0], -1, HEAD)
    order = [(0, turned), (half, half + turned), (turned, half), (half + turned, HEAD)]
    return jnp.concatenate([heads[..., a:b] for a, b in order], axis=-1).reshape(columns.shape)


def turn(values, cosine, sine):
    half = HEAD // 2
    one, two = values[:, :half], values[:, half:]
    return jnp.concatenate([one * cosine - two * sine, two * cosine + one * sine], axis=1)


def pack_small(columns, n):
    rb = D // n
    blocks = columns.reshape(SMALLR, n, rb).transpose(1, 0, 2)
    return jnp.pad(blocks, ((0, 0), (0, 0), (0, 128 - rb)))


def return_plain(n, gg, xg, a1, a2, z, dh, o, dq, dk, dv, ws, cosine, sine, small_all, sums):
    place = Place(n)
    R, rb, rows = n // 8, D // n, 8 * TOK
    a1, a2, gy, z, dh, o, dq = (v.reshape(rows, -1) for v in (a1, a2, gg, z, dh, o, dq))
    w_in, w_up, w_out, w_down = (g.reshape(D, -1) for g in ws)
    cosine, sine = cosine.reshape(rows, -1), sine.reshape(rows, -1)
    g1, g2 = small_all[0], small_all[2]
    xf = xg.reshape(rows, D).astype(F32)
    centred = xf - jnp.mean(xf, axis=-1, keepdims=True)
    xhat = centred * lax.rsqrt(jnp.mean(centred * centred, axis=-1, keepdims=True) + NORM_EPS)
    partial_out = (contract_cols(o, w_out) + contract_cols(z, w_down)).astype(BF)
    ins = {"k": dk, "v": dv, "p": partial_out.reshape(8, TOK, D)}
    back = {}
    for at, name in enumerate(ins):
        back |= return_keys(n, {name: ins[name]}, 4 + at)
    dq = turn(dq, cosine, -sine)
    dk = turn(back["k"].reshape(rows, HEAD).astype(F32), cosine, -sine)
    dj = jnp.concatenate([dq.astype(BF), dk.astype(BF), back["v"].reshape(rows, HEAD)], axis=1)
    da1 = contract_cols(dj, w_in)
    da2 = contract_cols(dh, w_up)
    e = (da1 * g1 + da2 * g2).astype(BF)
    norm_grads = [jnp.sum(v, axis=0) for v in (da1 * xhat, da1, da2 * xhat, da2)]
    dj = jnp.concatenate([unpaired(dj[:, : 2 * HEAD]), dj[:, 2 * HEAD :]], axis=1)
    dj_sum = jnp.sum(dj.astype(F32), axis=0).reshape(3, HEAD)
    own_cols = lax.dynamic_update_slice(
        jnp.zeros((SMALLR, D), F32), dj_sum, (jnp.int32(4), place.t * HEAD)
    )
    small_term = own_cols + sums
    small_term = small_term.at[:4].set(jnp.stack(norm_grads))
    small_blocks = pack_small(small_term, n).reshape(4, R, 2 * SMALLR, 128)
    grads = [
        contract_rows(left, right).astype(BF).reshape(4, R, 2 * rb, -1)
        for left, right in ((a1, dj), (a2, dh), (gy, o), (gy, z))
    ]
    *weight_grads, e_own, small_parts = return_grads(
        n, grads, e.reshape(8, TOK, D), small_blocks, 3
    )
    return back["p"], weight_grads, e_own, jnp.sum(small_parts, axis=0)[:SMALLC, :rb].T


def body(
    tokens, cotangent, lengths,
    attend_in, widening, attend_out, narrowing, small_params,
    first_attend_in, first_widening, first_attend_out, first_narrowing, first_small,
    second_attend_in, second_widening, second_attend_out, second_narrowing, second_small,
):
    n = lax.axis_size("fsdp")
    place = Place(n)
    R = place.R
    rb = D // n
    turned = HEAD // 8
    lanes = np.arange(HEAD // 2)
    frequency = np.where(lanes < turned, ROPE_BASE ** (-2.0 * lanes / (2 * turned)), 0.0)
    frequency = jnp.asarray(frequency.astype(np.float32)[None, :])

    small_rows = jnp.pad(small_params, ((0, 0), (0, 128 - SMALLC)))
    low_in = attend_in.astype(BF)
    low_in = jnp.concatenate([paired(low_in[:, : 2 * D]), low_in[:, 2 * D :]], axis=1)
    weights = [low_in] + [w.astype(BF) for w in (widening, attend_out, narrowing)]
    runs = (2, 4, TOK, HEAD)
    xg, gg, a1, a2, *ws, q, kg, vg, z, dh, dout, small_all, sums, stats_x, cosine, sine = forward(
        n, tokens, cotangent, weights, small_rows, lengths, frequency
    )
    xg, gg, a1, a2, z, dh, stats_x, cosine, sine = (
        v.reshape(8, TOK, v.shape[-1]) for v in (xg, gg, a1, a2, z, dh, stats_x, cosine, sine)
    )

    kg = kg.reshape(R, *runs)
    vg = vg.reshape(R, *runs)
    q4, dout4 = q.reshape(runs), dout.reshape(runs)
    o4, stats = attend(n, lengths, q4, dout4, kg, vg)
    dq4, dk5, dv5 = attend_back(n, lengths, q4, dout4, stats, kg, vg)
    o, dq = o4.reshape(8, TOK, HEAD), dq4.reshape(8, TOK, HEAD)
    dk, dv = dk5.reshape(R, 8, TOK, HEAD), dv5.reshape(R, 8, TOK, HEAD)
    if R == 4:
        p_own, dk, dv, up_sum, g_out, g_down, g_up = return_one(
            n, dk, dv, o, z, ws[2].reshape(D, -1), ws[3].reshape(D, -1), gg, a2, dh
        )
        *weight_grads, e_own, small_parts, _ = return_two(
            n, up_sum, g_up, g_out, g_down, dq, dk, dv, a1, xg, dh,
            ws[0].reshape(D, -1), ws[1].reshape(D, -1), cosine, sine, small_all, stats_x, sums,
        )
        own_lanes = lax.dynamic_slice(
            jnp.sum(small_parts, axis=0), (0, place.c * rb), (SMALLR, rb)
        )
        small_grad = own_lanes[:SMALLC].T
    else:
        p_own, weight_grads, e_own, small_grad = return_plain(
            n, gg, xg, a1, a2, z, dh, o, dq, dk, dv, ws, cosine, sine, small_all, sums
        )
    gr_in, gr_up, gr_out, gr_down = weight_grads
    rate_inner = 2.5 * D ** (-0.5)
    rate_outer = 2.5 * (D * 11 // LMAX) ** (-0.5)
    rate_down = 2.5 * FF ** (-0.5)
    rate_small = 0.5
    new, mean, square, block_out, token_grad = adam(
        (tokens, cotangent, e_own, p_own, small_all),
        (attend_in, widening, attend_out, narrowing),
        (gr_in, gr_up, gr_out, gr_down),
        (first_attend_in, first_widening, first_attend_out, first_narrowing),
        (second_attend_in, second_widening, second_attend_out, second_narrowing),
        (rate_inner, rate_inner, rate_outer, rate_down),
    )
    mean_small, square_small, new_small = adam_step(
        small_params, small_grad, first_small, second_small, rate_small
    )
    return (
        block_out,
        token_grad,
        *new,
        new_small,
        *mean,
        mean_small,
        *square,
        square_small,
    )


def solution(mesh):
    spec = P("fsdp", None)
    return jax.shard_map(
        body,
        mesh=mesh,
        in_specs=(spec, spec, P(), *[spec] * 15),
        out_specs=(spec,) * 17,
        check_vma=False,
    )
```

```python
import math

import jax
import jax.numpy as jnp
import numpy as np
from jax import lax
from jax.experimental import pallas as pl
from jax.experimental.pallas import tpu as pltpu
from jax.sharding import PartitionSpec as P

D = 2048
HEADS = 8
HEAD = D // HEADS
FF = 8192
FFT = FF // HEADS
LMAX = 4096
STEPS = 10
TOK = 256
RUN = 2 * TOK
BACK_RUNS = LMAX // RUN + 1

NORM_EPS = 1e-05
ADAM_EPS = 1e-08
BETA_ONE = 0.9
BETA_TWO = 0.95
WEIGHT_DECAY = 0.01
NEGATIVE = -1e30
ROPE_BASE = 10000.0
SMALLC = 13
SMALLR = 16

BF = jnp.bfloat16
F32 = jnp.float32
ANY = pl.BlockSpec(memory_space=pl.ANY)
VM = pl.BlockSpec(memory_space=pltpu.VMEM)
MIB = 1024 * 1024
WEIGHTS = ((3, HEAD), (1, FFT), (1, HEAD), (1, FFT))


class Place:
    def __init__(self, n):
        self.n = n
        self.S = n // 4
        self.R = self.S // 2
        self.bits = int(math.log2(self.R))
        me = lax.axis_index("fsdp")
        self.me = me
        self.zt = me // self.S
        self.rr = (me % self.S) // 2
        self.c = me % 2
        self.z1 = self.zt // 2
        self.z0 = self.zt % 2
        self.t = self.zt * 2 + self.c

    def zt_of(self, s):
        z1 = 1 - self.z1 if s & 1 else self.z1
        z0 = 1 - self.z0 if s & 2 else self.z0
        return z1 * 2 + z0

    def zt_of_run(self, u):
        z1 = self.z1 + (1 - 2 * self.z1) * (u % 2)
        z0 = self.z0 + (1 - 2 * self.z0) * (u // 2)
        return z1 * 2 + z0

    def c_of(self, s):
        return 1 - self.c if s & 4 else self.c

    def t_of(self, s):
        return self.zt_of(s) * 2 + self.c_of(s)

    def rr_of(self, i):
        out = 0
        for k in range(self.bits):
            bit = (self.rr // (1 << k)) % 2
            out = out + (1 - bit if i >> k & 1 else bit) * (1 << k)
        return out

    def dev_t(self, s):
        return self.zt_of(s) * self.S + self.rr * 2 + self.c_of(s)

    def dev_r(self, i):
        return self.zt * self.S + self.rr_of(i) * 2 + self.c


class Copies:
    def __init__(self, send, recv):
        self.send, self.recv, self.count, self.started = send, recv, 0, []

    def remote(self, src, dst, dev):
        k = self.count
        self.count += 1
        copy = pltpu.make_async_remote_copy(
            src_ref=src,
            dst_ref=dst,
            send_sem=self.send.at[k],
            recv_sem=self.recv.at[k],
            device_id=(dev,),
            device_id_type=pl.DeviceIdType.MESH,
        )
        copy.start()
        self.started.append(copy)
        return copy

    def local(self, src, dst):
        k = self.count
        self.count += 1
        copy = pltpu.make_async_copy(src, dst, self.send.at[k])
        copy.start()
        return copy

    def finish(self):
        for copy in self.started:
            copy.wait_send()


def greet(place, t_group, r_group):
    barrier = pltpu.get_barrier_semaphore()
    peers = [place.dev_t(s) for s in t_group] + [place.dev_r(i) for i in r_group]
    for dev in peers:
        pl.semaphore_signal(barrier, inc=1, device_id=(dev,), device_id_type=pl.DeviceIdType.MESH)
    pl.semaphore_wait(barrier, len(peers))


def top_bit(s):
    return 1 << (s.bit_length() - 1)


def orders(bits):
    up = [1 << k for k in range(bits)]
    return [up, up[::-1]]


def spread(order):
    have, out = [0], []
    for bit in order:
        new = [i | bit for i in have]
        out += [(i, bit) for i in new]
        have = have + new
    return out


def collected(order):
    left, out = list(range(1 << len(order))), []
    for bit in order:
        out.append((bit, [i for i in left if i & bit]))
        left = [i for i in left if not i & bit]
    return out


def add_rows(dst, a, b):
    lead = dst.shape[:-2]
    rows, columns = dst.shape[-2:]
    size = min(rows, max(16, 1 << int(math.log2(16384 // columns))))
    for flat in range(math.prod(lead)):
        where, rest = [], flat
        for extent in lead[::-1]:
            where.insert(0, rest % extent)
            rest //= extent

        def step(k, carry, where=tuple(where)):
            at = where + (pl.ds(pl.multiple_of(k * size, size), size), slice(None))
            dst[at] = (a[at].astype(F32) + b[at].astype(F32)).astype(dst.dtype)
            return carry

        lax.fori_loop(0, rows // size, step, 0)


def call(kernel, ins, in_specs, outs, out_specs, scratch, collective_id, copies, vmem=60):
    return pl.pallas_call(
        kernel,
        out_shape=outs,
        in_specs=in_specs,
        out_specs=out_specs,
        scratch_shapes=[
            *scratch,
            pltpu.SemaphoreType.DMA((copies,)),
            pltpu.SemaphoreType.DMA((copies,)),
        ],
        compiler_params=pltpu.CompilerParams(
            collective_id=collective_id, has_side_effects=True, vmem_limit_bytes=vmem * MIB
        ),
    )(*ins)


class Net:
    def __init__(self, send, recv):
        self.send, self.recv, self.makers, self.count = send, recv, [], 0

    def add(self, maker, many=1):
        base = self.count
        self.count += many

        def build(k=0):
            src, dst, dev = maker(k)
            return pltpu.make_async_remote_copy(
                src_ref=src,
                dst_ref=dst,
                send_sem=self.send.at[base + k],
                recv_sem=self.recv.at[base + k],
                device_id=(dev,),
                device_id_type=pl.DeviceIdType.MESH,
            )

        self.makers.append((build, many))
        return build

    def finish(self):
        for build, many in self.makers:
            if many == 1:
                build().wait_send()
            else:

                def one(k, carry, build=build):
                    build(k).wait_send()
                    return carry

                lax.fori_loop(0, many, one, 0)


class GatherT:
    def __init__(self, net, place, own, out):
        self.ops = {}
        for s in range(1, 8):
            hop = top_bit(s)
            src = own if s == hop else out.at[(s - hop) // 4, (s - hop) % 4]
            dst = out.at[s // 4, s % 4]
            parts = [slice(None)]
            if s in (1, 3):
                parts = [pl.ds(h * (D // 2), D // 2) for h in range(2)]
            for h, cols in enumerate(parts):
                self.ops[s, h] = net.add(
                    lambda k, src=src, dst=dst, cols=cols, hop=hop: (
                        src.at[:, cols], dst.at[:, cols], place.dev_t(hop),
                    )
                )

    def named(self, which):
        if isinstance(which, tuple):
            return [self.ops[which]]
        return [op for (s, _), op in self.ops.items() if s == which]

    def start(self, *which):
        for s in which:
            for op in self.named(s):
                op().start()

    def wait(self, *which):
        for s in which:
            for op in self.named(s):
                op().wait_recv()


class GatherR:
    def __init__(self, net, place, region, order):
        self.plan = spread(order)
        self.ops = {}
        self.later = [(i, bit) for i, bit in self.plan if i != bit]
        self.used = {i ^ bit for i, bit in self.later}
        for i, bit in self.plan:
            self.ops[i] = net.add(
                lambda k, i=i, bit=bit: (region(i ^ bit), region(i ^ bit), place.dev_r(bit))
            )

    def begin(self):
        for i, bit in self.plan:
            if i == bit:
                self.ops[i]().start()

    def advance(self):
        seen = set()
        for i, bit in self.later:
            if i ^ bit not in seen:
                self.ops[i ^ bit]().wait_recv()
                seen.add(i ^ bit)
            self.ops[i]().start()

    def end(self):
        for i, _ in self.plan:
            if i not in self.used:
                self.ops[i]().wait_recv()


def cosine_and_sine(x):
    turns = jnp.floor(x * (2.0 / math.pi) + 0.5)
    r = ((x - turns * 1.5703125) - turns * 4.837512969970703e-4) - turns * 7.549789954891882e-8
    z = r * r
    sine = ((-1.9515295891e-4 * z + 8.3321608736e-3) * z - 1.6666654611e-1) * z * r + r
    cosine = (
        ((2.443315711809948e-5 * z - 1.388731625493765e-3) * z + 4.166664568298827e-2) * z * z
        - 0.5 * z
        + 1.0
    )
    quarter = turns - 4.0 * jnp.floor(turns * 0.25)
    odd = (quarter == 1.0) | (quarter == 3.0)
    first, second = jnp.where(odd, sine, cosine), jnp.where(odd, cosine, sine)
    return (
        jnp.where((quarter == 1.0) | (quarter == 2.0), -first, first),
        jnp.where(quarter >= 2.0, -second, second),
    )


def shuffle_matrix():
    turned, half = HEAD // 8, HEAD // 2
    into = lax.broadcasted_iota(jnp.int32, (HEAD, HEAD), 1)
    source = lax.broadcasted_iota(jnp.int32, (HEAD, HEAD), 0)
    moved = jnp.where((into >= turned) & (into < half), into + turned, into)
    moved = jnp.where((into >= half) & (into < half + turned), into - (half - turned), moved)
    return jnp.where(source == moved, 1.0, 0.0).astype(F32)


def weight_halves(net, place, ref):
    both = orders(place.bits)
    return [
        GatherR(net, place, lambda i, h=h: ref.at[pl.ds(2 * h, 2), place.rr_of(i)], both[h])
        for h in range(2)
    ]


def forward_kernel(
    n, nseq, x, gy, wi, wu, wo, wd, small, lengths, frequency,
    xg, gg, a1g, a2g, oi, ou, oo, od, qo, kg, vg, zo, dho, dout, smt, sums, stats, cosine, sine,
    xv, gv, sm, ti, tu, to, td, slope, a2v, qkv, at, ztile, dht, bias, dhsum,
    send, recv, local, out_sem, g_sem,
):
    place = Place(n)
    rb = D // n
    net = Net(send, recv)
    weights = list(zip((wi, wu, wo, wd), (ti, tu, to, td), WEIGHTS))
    greet(place, range(1, 8), [1 << k for k in range(place.bits)])
    mine = pl.ds(pl.multiple_of(place.c * rb, rb), rb)

    small_t = [
        net.add(lambda k, s=s: (small, sm.at[place.zt, place.rr, mine, :], place.dev_t(s)))
        for s in range(1, 8)
    ]

    def columns(p, width, t):
        return pl.ds(pl.multiple_of(p * D + t * width, 128), width)

    def exchange(which):
        src, dst, (parts, width) = weights[which]
        return [
            net.add(
                lambda k, s=s, p=p: (
                    src.at[:, columns(p, width, place.t_of(s))],
                    dst.at[place.zt, place.rr, mine, pl.ds(p * width, width)],
                    place.dev_t(s),
                )
            )
            for s in range(1, 8)
            for p in range(parts)
        ]

    to_t = [exchange(k) for k in range(4)]
    small_r = GatherR(net, place, lambda i: sm.at[:, place.rr_of(i)], orders(place.bits)[0])
    to_r = [weight_halves(net, place, w[1]) for w in weights]
    x_t = GatherT(net, place, x, xv)
    g_t = GatherT(net, place, gy, gv)
    both = orders(place.bits)
    keys = []
    for own, out, order in ((qkv.at[1], kg, both[0]), (qkv.at[2], vg, both[1])):
        ops = {}
        for i, bit in spread(order):
            ops[i] = net.add(
                lambda s, i=i, bit=bit, own=own, out=out: (
                    own.at[s // 4, s % 4] if i == bit else out.at[i ^ bit, s // 4, s % 4],
                    out.at[i, s // 4, s % 4],
                    place.dev_r(bit),
                ),
                8,
            )
        keys.append((ops, spread(order)))

    def start(ops):
        for op in ops:
            op().start()

    def wait(ops):
        for op in ops:
            op().wait_recv()

    locals_ = [
        pltpu.make_async_copy(x, xv.at[0, 0], local.at[0]),
        pltpu.make_async_copy(gy, gv.at[0, 0], local.at[1]),
        pltpu.make_async_copy(small, sm.at[place.zt, place.rr, mine, :], local.at[2]),
    ]
    for src, dst, (parts, width) in weights:
        for p in range(parts):
            locals_.append(
                pltpu.make_async_copy(
                    src.at[:, columns(p, width, place.t)],
                    dst.at[place.zt, place.rr, mine, pl.ds(p * width, width)],
                    local.at[len(locals_)],
                )
            )
    for copy in locals_:
        copy.start()
    start(small_t)
    start(to_t[0])
    x_t.start(4)
    for copy in locals_:
        copy.wait()
    wait(small_t)
    small_r.begin()
    wait(to_t[0])
    for part in to_r[0]:
        part.begin()
    start(to_t[1])
    x_t.start(2)
    small_r.advance()
    for part in to_r[0]:
        part.advance()

    def tables(s, carry):
        core, u = s // 4, s % 4
        device = (
            place.zt_of_run(u) * place.S + place.rr * 2 + place.c + (1 - 2 * place.c) * core
        )
        token = device * TOK + lax.broadcasted_iota(jnp.int32, (TOK, HEAD // 2), 0)
        offset = token - start_of(token, lengths, nseq)
        angles = offset.astype(F32) * frequency[0:1, :]
        cosine[core, u], sine[core, u] = cosine_and_sine(angles)
        return carry

    lax.fori_loop(0, 8, tables, 0)
    wait(to_t[1])
    x_t.start(1)
    for part in to_r[1]:
        part.begin()
    small_r.end()

    smt[...] = sm[...].reshape(D, 128).T[:SMALLR, :]
    head_cols = pl.ds(pl.multiple_of(place.t * HEAD, HEAD), HEAD)
    shuffle = shuffle_matrix()
    three = jnp.dot(
        smt[0:8, head_cols], shuffle, precision=lax.Precision.HIGHEST, preferred_element_type=F32
    )
    for p in range(2):
        bias[0:1, p * HEAD : (p + 1) * HEAD] = three[4 + p : 5 + p, :]
    bias[0:1, 2 * HEAD : 3 * HEAD] = smt[6:7, head_cols]

    def repeat_matrix():
        lane = lax.broadcasted_iota(jnp.int32, (HEAD, FFT), 1)
        row = lax.broadcasted_iota(jnp.int32, (HEAD, FFT), 0)
        return jnp.where(lane // 4 == row, 1.0, 0.0).astype(F32)

    four = jnp.dot(
        smt[8:16, head_cols],
        repeat_matrix(),
        precision=lax.Precision.HIGHEST,
        preferred_element_type=F32,
    )
    lane8 = lax.broadcasted_iota(jnp.int32, (8, FFT), 1)
    row8 = lax.broadcasted_iota(jnp.int32, (8, FFT), 0)
    bias[1:2, :] = jnp.sum(jnp.where(lane8 % 4 + 1 == row8, four, 0.0), axis=0, keepdims=True)

    for part in to_r[0]:
        part.end()
    copy_out = [pltpu.make_async_copy(ti, oi, local.at[0])]
    copy_out[0].start()

    def norms(u):
        def chunk(r, carry):
            at_rows = (r // 16, pl.ds(pl.multiple_of(r % 16 * 16, 16), 16), slice(None))
            in_rows = (at_rows[0], u, *at_rows[1:])
            xf = xv[in_rows].astype(F32)
            average = jnp.mean(xf, axis=1, keepdims=True)
            centred = xf - average
            var = jnp.mean(centred * centred, axis=1, keepdims=True)
            inverse = lax.rsqrt(var + NORM_EPS)
            xhat = centred * inverse
            at[at_rows] = (xhat * smt[0:1, :] + smt[1:2, :]).astype(BF)
            a2v[in_rows] = (xhat * smt[2:3, :] + smt[3:4, :]).astype(BF)
            lanes = lax.broadcasted_iota(jnp.int32, (16, 128), 1)
            stats[in_rows] = jnp.where(lanes == 0, average, inverse)
            return carry

        lax.fori_loop(0, 2 * TOK // 16, chunk, 0, unroll=4)

    def place_of(k):
        return k % 2 * 2 + k // 2

    def events(k, table):
        for when, what in table.items():

            @pl.when(k == when)
            def _(what=what):
                for fn in what:
                    fn()

    def staged(buffer, out, u, sem):
        return pltpu.make_async_copy(buffer, out.at[:, u], out_sem.at[sem])

    def free(buffer, out, k, sem):
        @pl.when(k >= 1)
        def _():
            staged(buffer, out, 0, sem).wait()

    def forward_keys(s):
        for ops, plan in keys:
            seen = set()
            for i, bit in plan:
                if i != bit:
                    if i ^ bit not in seen:
                        ops[i ^ bit](s).wait_recv()
                        seen.add(i ^ bit)
                    ops[i](s).start()

    def hidden_units(k):
        u = place_of(k)

        def columns_of(c, carry):
            cols = pl.ds(pl.multiple_of(c * HEAD, HEAD), HEAD)
            hidden = jnp.dot(
                a2v[:, u].reshape(RUN, D),
                tu[:, :, :, cols].reshape(D, HEAD),
                preferred_element_type=F32,
            )
            slope[:, u, :, cols] = (hidden + bias[1:2, cols]).reshape(2, TOK, HEAD)
            return carry

        lax.fori_loop(0, FFT // HEAD, columns_of, 0)
        free(ztile, zo, k, 1)

        def chunk(r, carry):
            at_rows = (r // 16, pl.ds(pl.multiple_of(r % 16 * 16, 16), 16), slice(None))
            in_rows = (at_rows[0], u, *at_rows[1:])
            h = slope[in_rows]
            bell = jnp.exp(-0.5 * h * h)
            t = 1.0 / (1.0 + (0.3275911 * 0.5**0.5) * jnp.abs(h))
            series = t * (
                0.254829592
                + t * (-0.284496736 + t * (1.421413741 + t * (-1.453152027 + t * 1.061405429)))
            )
            tail = 0.5 * series * bell
            phi = jnp.where(h < 0.0, tail, 1.0 - tail)
            ztile[at_rows] = (h * phi).astype(BF)
            slope[in_rows] = phi + h * bell * (1.0 / math.sqrt(2.0 * math.pi))
            return carry

        lax.fori_loop(0, 2 * TOK // 16, chunk, 0, unroll=2)
        staged(ztile, zo, u, 1).start()

    def projections(k):
        u = place_of(k)
        free(at, a1g, k, 0)
        norms(u)
        half = HEAD // 2

        def part(p, carry):
            cols = pl.ds(pl.multiple_of(p * HEAD, HEAD), HEAD)
            joint = jnp.dot(
                at[...].reshape(RUN, D),
                ti[:, :, :, cols].reshape(D, HEAD),
                preferred_element_type=F32,
            )
            joint += bias[0:1, cols]
            turned = p < 2
            cs = jnp.where(turned, cosine[:, u].reshape(RUN, half), 1.0)
            sn = jnp.where(turned, sine[:, u].reshape(RUN, half), 0.0)
            scale = jnp.where(p == 0, HEAD**-0.5, 1.0).astype(F32)
            one, two = joint[:, :half], joint[:, half:]
            for at_col, value in ((0, one * cs - two * sn), (half, two * cs + one * sn)):
                value = (value.astype(BF).astype(F32) * scale).astype(BF)
                qkv[p, :, u, :, at_col : at_col + half] = value.reshape(2, TOK, half)
            return carry

        lax.fori_loop(0, 3, part, 0)
        staged(at, a1g, u, 0).start()
        for core in range(2):
            for ops, plan in keys:
                for i, bit in plan:
                    if i == bit:
                        ops[i](core * 4 + u).start()

    def first(k, carry):
        events(
            k,
            {
                0: [lambda: x_t.wait(4)],
                1: [
                    lambda: [p.advance() for p in to_r[1]],
                    lambda: x_t.wait(2),
                    lambda: x_t.start(6),
                    lambda: start(to_t[3]),
                    lambda: start(to_t[2]),
                    lambda: x_t.wait(6),
                ],
                2: [
                    lambda: x_t.wait((1, 0)),
                    lambda: x_t.start((3, 0)),
                    lambda: x_t.wait((1, 1)),
                    lambda: x_t.start((3, 1), 5),
                    lambda: [p.end() for p in to_r[1]],
                    lambda: pltpu.make_async_copy(tu, ou, local.at[1]).start(),
                ],
                3: [
                    lambda: wait(to_t[3]),
                    lambda: wait(to_t[2]),
                    lambda: [p.begin() for p in to_r[3] + to_r[2]],
                    lambda: g_t.start(1, 4),
                ],
                4: [lambda: x_t.wait(5)],
                5: [
                    lambda: [p.advance() for p in to_r[3] + to_r[2]],
                    lambda: x_t.wait(3),
                    lambda: x_t.start(7),
                    lambda: g_t.start(2),
                    lambda: x_t.wait(7),
                ],
                6: [lambda: g_t.wait((1, 0)), lambda: g_t.start((3, 0))],
                7: [lambda: g_t.wait((1, 1)), lambda: g_t.start((3, 1), 5)],
            },
        )
        late = k // 4

        @pl.when(k % 4 < 2)
        def _():
            projections(k - 2 * late)

        @pl.when(k % 4 >= 2)
        def _():
            hidden_units(k - 2 - 2 * late)

        @pl.when((k == 3) | (k >= 5))
        def _():
            pair = k - 3 - late
            for core in range(2):
                forward_keys(core * 4 + place_of(pair))

        return carry

    lax.fori_loop(0, 8, first, 0)
    own_out = [
        pltpu.make_async_copy(qkv.at[1], kg.at[0], local.at[4]),
        pltpu.make_async_copy(qkv.at[2], vg.at[0], local.at[5]),
        pltpu.make_async_copy(qkv.at[0], qo, local.at[7]),
        pltpu.make_async_copy(xv, xg, local.at[6]),
        pltpu.make_async_copy(a2v, a2g, local.at[8]),
    ]
    for copy in own_out:
        copy.start()
    copy_out.append(pltpu.make_async_copy(tu, ou, local.at[1]))

    def finish_keys(s, carry):
        for ops, plan in keys:
            used = {i ^ bit for i, bit in plan if i != bit}
            for i, bit in plan:
                if i not in used:
                    ops[i](s).wait_recv()
        return carry

    for part in to_r[3] + to_r[2]:
        part.end()
    copy_out += [
        pltpu.make_async_copy(to, oo, local.at[2]),
        pltpu.make_async_copy(td, od, local.at[3]),
    ]
    copy_out[2].start()
    copy_out[3].start()
    dhsum[...] = jnp.zeros_like(dhsum)

    def third(k, carry):
        u = place_of(k)
        events(
            k,
            {
                0: [lambda: g_t.wait(4)],
                1: [lambda: g_t.wait(2), lambda: g_t.start(6), lambda: g_t.wait(6)],
                2: [lambda: g_t.wait(5)],
                3: [lambda: g_t.wait(3), lambda: g_t.start(7), lambda: g_t.wait(7)],
            },
        )
        free(dht, dho, k, 2)
        pltpu.make_async_copy(gv.at[:, u], gg.at[:, u], g_sem.at[u]).start()
        def columns_of(c, carry):
            cols = pl.ds(pl.multiple_of(c * HEAD, HEAD), HEAD)
            dz = jnp.dot(
                gv[:, u].reshape(RUN, D),
                td[:, :, :, cols].reshape(D, HEAD),
                preferred_element_type=F32,
            )
            dh = (dz * slope[:, u, :, cols].reshape(RUN, HEAD)).astype(BF)
            dht[:, :, cols] = dh.reshape(2, TOK, HEAD)
            dhsum[0:1, cols] += jnp.sum(dh.astype(F32), axis=0, keepdims=True)
            return carry

        lax.fori_loop(0, FFT // HEAD, columns_of, 0)
        staged(dht, dho, u, 2).start()
        grad = gv[:, u].reshape(RUN, D)
        dout[:, u] = (
            jnp.dot(grad, to[...].reshape(D, HEAD), preferred_element_type=F32)
            .astype(BF)
            .reshape(2, TOK, HEAD)
        )
        return carry

    lax.fori_loop(0, 4, third, 0)
    four = jnp.dot(
        jnp.where(lane8 % 4 + 1 == row8, dhsum[0:1, :], 0.0),
        repeat_matrix().T,
        precision=lax.Precision.HIGHEST,
        preferred_element_type=F32,
    )
    sums[...] = jnp.zeros_like(sums)
    sums[8:16, head_cols] = four
    sums[8:9, :] = jnp.sum(gv[0, 0].astype(F32), axis=0, keepdims=True)
    sums[7:8, :] = sums[8:9, :]
    lax.fori_loop(0, 8, finish_keys, 0)
    for sem, (buffer, out) in enumerate(((at, a1g), (ztile, zo), (dht, dho))):
        staged(buffer, out, 0, sem).wait()
    for copy in copy_out + own_out:
        copy.wait()
    for u in range(4):
        pltpu.make_async_copy(gv.at[:, u], gg.at[:, u], g_sem.at[u]).wait()
    net.finish()


def forward(n, x, gy, weights, small, lengths, frequency):
    rb = D // n
    R = n // 8

    def shape(*dims, kind=BF):
        return jax.ShapeDtypeStruct(dims, kind)

    w_shapes = [(4, R, 2 * rb, parts * width) for parts, width in WEIGHTS]
    block, cols, head = (2, 4, TOK, D), (2, 4, TOK, FFT), (2, 4, TOK, HEAD)
    outs = [shape(*block) for _ in range(4)]
    outs += [shape(*w) for w in w_shapes]
    outs += [shape(*head), shape(R, *head), shape(R, *head), shape(*cols), shape(*cols)]
    outs += [shape(*head), shape(SMALLR, D, kind=F32), shape(SMALLR, D, kind=F32)]
    outs += [shape(2, 4, TOK, 128, kind=F32)]
    outs += [shape(2, 4, TOK, HEAD // 2, kind=F32) for _ in range(2)]
    out_specs = [ANY] * 13 + [VM] * 6
    scratch = [
        pltpu.VMEM(block, BF),
        pltpu.VMEM(block, BF),
        pltpu.VMEM((4, R, 2 * rb, 128), F32),
        *[pltpu.VMEM(w, BF) for w in w_shapes],
        pltpu.VMEM(cols, F32),
        pltpu.VMEM(block, BF),
        pltpu.VMEM((3, *head), BF),
        pltpu.VMEM((2, TOK, D), BF),
        pltpu.VMEM((2, TOK, FFT), BF),
        pltpu.VMEM((2, TOK, FFT), BF),
        pltpu.VMEM((8, FFT), F32),
        pltpu.VMEM((8, FFT), F32),
    ]
    copies = 7 + 7 * 6 + (R - 1) * (1 + 8 + 2 * 8) + 18

    def kernel(*refs):
        forward_kernel(n, lengths.shape[0], *refs)

    return pl.pallas_call(
        kernel,
        out_shape=outs,
        in_specs=[ANY] * 7 + [pl.BlockSpec(memory_space=pltpu.SMEM), VM],
        out_specs=out_specs,
        scratch_shapes=[
            *scratch,
            pltpu.SemaphoreType.DMA((copies,)),
            pltpu.SemaphoreType.DMA((copies,)),
            pltpu.SemaphoreType.DMA((16,)),
            pltpu.SemaphoreType.DMA((3,)),
            pltpu.SemaphoreType.DMA((4,)),
        ],
        compiler_params=pltpu.CompilerParams(
            collective_id=0, has_side_effects=True, vmem_limit_bytes=62 * MIB
        ),
    )(x, gy, *weights, small, lengths, frequency)


class SumT:
    def __init__(self, copies, place, data, slots, out):
        self.copies, self.place, self.data, self.slots, self.out = copies, place, data, slots, out
        self.ops = {}
        self.cur = {s: data.at[s] for s in range(8)}

    def send(self, s):
        hop = top_bit(s)
        self.ops[s] = self.copies.remote(self.cur[s], self.slots.at[s - 1], self.place.dev_t(hop))

    def add(self, s):
        to = s - top_bit(s)
        self.ops[s].wait_recv()
        slot = self.slots.at[s - 1]
        if to == 0 and s == 1:
            add_rows(self.out, self.cur[0], slot)
        else:
            add_rows(slot, self.cur[to], slot)
            self.cur[to] = slot

    def start(self):
        for s in (6, 7, 5, 4):
            self.send(s)

    def middle(self):
        for s in (6, 7):
            self.add(s)
            self.send(s - 4)
        self.add(5)

    def late(self):
        self.add(3)
        self.send(1)
        self.add(4)
        self.add(2)

    def end(self):
        self.add(1)


class SumR:
    def __init__(self, copies, place, piece, slots, order):
        self.copies, self.place, self.slots = copies, place, slots
        self.steps = collected(order)
        self.cur = {i: piece(i) for i in range(1 << len(order))}
        self.ops = {}

    def send(self, step):
        bit, members = self.steps[step]
        for i in members:
            self.ops[i] = self.copies.remote(
                self.cur[i], self.slots.at[i - 1], self.place.dev_r(bit)
            )

    def add(self, step):
        bit, members = self.steps[step]
        for i in members:
            self.ops[i].wait_recv()
            slot = self.slots.at[i - 1]
            add_rows(slot, self.cur[i ^ bit], slot)
            self.cur[i ^ bit] = slot


def return_keys_kernel(n, have, *refs):
    place = Place(n)
    refs = list(refs)
    count = len(have)
    ins, refs = refs[:count], refs[count:]
    outs, refs = refs[:count], refs[count:]
    slots, (send, recv) = refs[:count], refs[count:]
    copies = Copies(send, recv)
    both = orders(place.bits)
    r_group = [1 << b for b in range(place.bits)] if set(have) - {"p"} else []
    t_group = (1, 2, 4) if "p" in have else ()
    greet(place, t_group, r_group)
    total, sums = None, []
    for name, src, dst, slot in zip(have, ins, outs, slots):
        if name == "p":
            total = SumT(copies, place, src, slot, dst)
        else:
            order = both[0] if name == "k" else both[1]
            sums.append((SumR(copies, place, lambda i, src=src: src.at[i], slot, order), dst))
    for part, _ in sums:
        part.send(0)
    if total:
        total.start()
        total.middle()
    for step in range(place.bits):
        for part, _ in sums:
            part.add(step)
            if step + 1 < place.bits:
                part.send(step + 1)
    if total:
        total.late()
    for part, dst in sums:
        copy = copies.local(part.cur[0], dst)
        copy.wait()
    if total:
        total.end()
    copies.finish()


def return_keys(n, ins, collective_id):
    R = n // 8
    outs, scratch, copies = [], [], 0
    for name in ins:
        if name == "p":
            outs.append(jax.ShapeDtypeStruct((TOK, D), F32))
            scratch.append(pltpu.VMEM((7, TOK, D), BF))
            copies += 7
        else:
            outs.append(jax.ShapeDtypeStruct((8, TOK, HEAD), BF))
            scratch.append(pltpu.VMEM((R - 1, 8, TOK, HEAD), BF))
            copies += R

    def kernel(*refs):
        return_keys_kernel(n, tuple(ins), *refs)

    out = call(
        kernel,
        tuple(ins.values()),
        [VM] * len(ins),
        outs,
        [VM] * len(ins),
        scratch,
        collective_id,
        copies,
    )
    return dict(zip(ins, out))


def return_grads_kernel(
    n, gi, gu, go, gd, e, small, oi, ou, oo, od, oe, osmall, si, su, so, sd, se, ss, send, recv
):
    place = Place(n)
    copies = Copies(send, recv)
    rb = D // n
    both = orders(place.bits)
    greet(place, range(1, 8), [1 << b for b in range(place.bits)])
    total = SumT(copies, place, e, se, oe)
    total.start()

    tasks = []
    for src, slot, dst, (parts, width) in zip(
        (gu, gd, gi, go), (su, sd, si, so), (ou, od, oi, oo), [WEIGHTS[k] for k in (1, 3, 0, 2)]
    ):
        for half in range(2):

            def piece(i, src=src, half=half):
                return src.at[pl.ds(2 * half, 2), place.rr_of(i)]

            part = SumR(copies, place, piece, slot.at[half], both[half])
            tasks.append((part, half, dst, parts, width))
    small_sum = SumR(copies, place, lambda i: small.at[:, place.rr_of(i)], ss, both[0])
    for part, *_ in tasks:
        part.send(0)
    small_sum.send(0)
    total.middle()
    for step in range(place.bits):
        for part, *_ in tasks:
            part.add(step)
            if step + 1 < place.bits:
                part.send(step + 1)
        small_sum.add(step)
        if step + 1 < place.bits:
            small_sum.send(step + 1)
    total.late()

    finals = {}
    for k in range(4):
        pieces = [tasks[2 * k + half][0].cur[0] for half in range(2)]
        finals[k] = pieces
    ops = []
    for k in range(4):
        _, _, dst, parts, width = tasks[2 * k]
        for zz in range(4):
            for cc in range(2):
                src = finals[k][zz // 2].at[zz % 2, pl.ds(cc * rb, rb), :]
                ops.append((zz, cc, src, dst, parts, width))
    sends = []
    for k in range(4):
        _, _, dst, parts, width = tasks[2 * k]
        store = tasks[2 * k][0].slots
        slot = store
        del slot
        for s in range(8):
            for p in range(parts):
                cols = pl.ds(pl.multiple_of(p * D + place.t * width, 128), width)
                sends.append((k, s, p, cols, dst, width))
    remote = []
    joined = {}
    for k, (ref, outbuf) in enumerate(((gu, ou), (gd, od), (gi, oi), (go, oo))):
        del ref, outbuf
        joined[k] = finals[k]
    for k, s, p, cols, dst, width in sends:
        base = (su, sd, si, so)[k]
        last = tasks[2 * k][0].steps[-1][1][0], tasks[2 * k + 1][0].steps[-1][1][0]
        zt = place.zt_of(s)
        rows = pl.ds(pl.multiple_of(place.c_of(s) * rb, rb), rb)
        which = zt // 2
        index = (1 - which) * (last[0] - 1) + which * (last[1] - 1)
        src = base.at[which, index, zt % 2, rows, pl.ds(p * width, width)]
        if s == 0:
            remote.append(("local", copies.local(src, dst.at[:, cols])))
        else:
            remote.append(("remote", copies.remote(src, dst.at[:, cols], place.dev_t(s))))
    last = small_sum.steps[-1][1][0] - 1
    for s in range(8):
        rows = pl.ds(pl.multiple_of(place.c_of(s) * SMALLR, SMALLR), SMALLR)
        src = ss.at[last, place.zt_of(s), rows, :]
        if s == 0:
            remote.append(("local", copies.local(src, osmall.at[place.t])))
        else:
            remote.append(("remote", copies.remote(src, osmall.at[place.t], place.dev_t(s))))
    total.end()
    for kind, copy in remote:
        if kind == "local":
            copy.wait()
        else:
            copy.wait_recv()
    copies.finish()


def return_grads(n, grads, e, small, collective_id):
    R = n // 8
    rb = D // n
    outs = [jax.ShapeDtypeStruct((rb, parts * D if parts > 1 else HEADS * width), BF) for parts, width in WEIGHTS]
    outs += [jax.ShapeDtypeStruct((TOK, D), F32), jax.ShapeDtypeStruct((8, SMALLR, 128), F32)]
    scratch = [
        pltpu.VMEM((2, R - 1, 2, 2 * rb, parts * width), BF) for parts, width in WEIGHTS
    ] + [
        pltpu.VMEM((7, TOK, D), BF),
        pltpu.VMEM((R - 1, 4, 2 * SMALLR, 128), F32),
    ]
    copies = 7 + 9 * (R - 1) + 8 * 6 + 8

    def kernel(*refs):
        return_grads_kernel(n, *refs)

    return call(
        kernel,
        (*grads, e, small),
        [VM] * 6,
        outs,
        [ANY] * 4 + [VM, ANY],
        scratch,
        collective_id,
        copies,
    )


WIDE = 512


class FoldT:
    def __init__(self, net, place, data, cs, zs, ys, out):
        self.data, self.cs, self.zs, self.ys, self.out = data, cs, zs, ys, out
        self.hop_c = net.add(lambda k: (data.at[k], cs.at[k], place.dev_t(4)), 4)
        self.near_z0 = net.add(lambda k: (cs.at[2], zs.at[0], place.dev_t(2)))
        halves = [(slice(None), pl.ds(h * (D // 2), D // 2)) for h in range(2)]
        self.halves = halves
        self.far_z0 = [
            net.add(lambda k, h=h: (cs.at[(3, *h)], zs.at[(1, *h)], place.dev_t(2)))
            for h in halves
        ]
        self.hop_z1 = [
            net.add(lambda k, h=h: (zs.at[(1, *h)], ys.at[(0, *h)], place.dev_t(1)))
            for h in halves
        ]

    @staticmethod
    def order(idx):
        return 7 - 4 * (idx % 2) - 2 * (idx // 2 % 2) - idx // 4

    def loop(self, make, emit, after):
        def step(idx, carry):
            s = self.order(idx)
            make(s, idx)
            k = s % 4

            def far(where, value):
                self.data[(k, *where)] = value.astype(BF)

            def near(where, value):
                self.cs[(k, *where)] = (value + self.cs[(k, *where)].astype(F32)).astype(BF)

            @pl.when(s >= 4)
            def _():
                emit(s, idx, far)
                self.hop_c(k).start()

            @pl.when(s < 4)
            def _():
                self.hop_c(k).wait_recv()
                emit(s, idx, near)

                @pl.when(s == 3)
                def _():
                    self.far_z0[0]().start()

                @pl.when(s == 2)
                def _():
                    self.near_z0().start()

            after(idx)
            return carry

        lax.fori_loop(0, 8, step, 0)

    def more(self):
        self.far_z0[1]().start()

    def turn(self, h):
        self.far_z0[h]().wait_recv()
        mine, there = self.cs.at[(1, *self.halves[h])], self.zs.at[(1, *self.halves[h])]
        add_rows(there, mine, there)
        self.hop_z1[h]().start()

    def turn_own(self):
        self.near_z0().wait_recv()
        add_rows(self.zs.at[0], self.cs.at[0], self.zs.at[0])

    def end(self):
        for h in range(2):
            self.hop_z1[h]().wait_recv()
            where = self.halves[h]
            add_rows(self.out.at[where], self.zs.at[(0, *where)], self.ys.at[(0, *where)])


def fold_scratch():
    return [
        pltpu.VMEM((4, TOK, D), BF),
        pltpu.VMEM((4, TOK, D), BF),
        pltpu.VMEM((2, TOK, D), BF),
        pltpu.VMEM((1, TOK, D), BF),
    ]


class FoldR:
    def __init__(self, net, place, far, own, slots, order):
        one, two = order
        self.own, self.slots = own, slots
        self.both = net.add(lambda k: (far(3), slots.at[0], place.dev_r(one)))
        self.first = net.add(lambda k: (far(one), slots.at[1], place.dev_r(one)))
        self.second = net.add(lambda k: (slots.at[0], slots.at[2], place.dev_r(two)))

    def begin(self):
        self.both().start()
        self.first().start()

    def advance(self):
        self.both().wait_recv()
        add_rows(self.slots.at[0], self.own.at[1], self.slots.at[0])
        self.second().start()

    def gather(self):
        self.first().wait_recv()
        add_rows(self.slots.at[1], self.own.at[0], self.slots.at[1])

    def end(self, out=None):
        self.second().wait_recv()
        out = self.slots.at[2] if out is None else out
        add_rows(out, self.slots.at[1], self.slots.at[2])


def weight_folds(n, net, place, grads, own, slots):
    view = grads.reshape(4, n // 8, 2 * (D // n), grads.shape[-1])
    both = orders(2)
    halves, pieces = [], []
    for h in range(2):

        def piece(i, h=h):
            return view.at[pl.ds(2 * h, 2), place.rr_of(i)]

        halves.append(FoldR(net, place, piece, own.at[h], slots.at[h], both[h]))
        pieces.append((piece(0), own.at[h, 0]))
        pieces.append((piece(both[h][1]), own.at[h, 1]))
    return halves, pieces


def gradient_tiles(lhs, tiles, turned, sem, products):
    wide = tiles.shape[-1]
    count = D // wide

    def fetch(f):
        cols = pl.ds(pl.multiple_of(f * wide, wide), wide)
        return pltpu.make_async_copy(lhs.at[:, :, cols], tiles.at[f % 2], sem.at[f % 2])

    def put(f, stage, out, sems):
        rows = pl.ds(pl.multiple_of(f * wide, wide), wide)
        return pltpu.make_async_copy(stage.at[f % 2], out.at[rows, :], sems.at[f % 2])

    fetch(0).start()

    def step(f, carry):
        fetch(f).wait()

        @pl.when(f + 1 < count)
        def _():
            fetch(f + 1).start()

        def turn_block(s, carry):
            turned[:, pl.ds(pl.multiple_of(s * TOK, TOK), TOK)] = tiles[f % 2, s].T
            return carry

        lax.fori_loop(0, 8, turn_block, 0)
        for rhs, stage, out, sems in products:

            @pl.when(f >= 2)
            def _(stage=stage, out=out, sems=sems):
                put(f - 2, stage, out, sems).wait()

            def columns_of(c, carry, rhs=rhs, stage=stage):
                cols = pl.ds(pl.multiple_of(c * HEAD, HEAD), HEAD)
                right = rhs[:, :, cols].reshape(8 * TOK, HEAD)
                total = jnp.dot(turned[...], right, preferred_element_type=F32)
                stage[f % 2, :, cols] = total.astype(BF)
                return carry

            lax.fori_loop(0, rhs.shape[-1] // HEAD, columns_of, 0)
            put(f, stage, out, sems).start()
        return carry

    lax.fori_loop(0, count, step, 0)
    for f in (count - 2, count - 1):
        for _, stage, out, sems in products:
            put(f, stage, out, sems).wait()


def half_fold(net, place, grads, h, own, slots):
    order = orders(2)[h]
    cols = pl.ds(h * (FFT // 2), FFT // 2)

    def piece(i):
        return grads.at[:, place.rr_of(i), :, cols]

    fold = FoldR(net, place, piece, own, slots, order)
    return fold, [(piece(0), own.at[0]), (piece(order[1]), own.at[1])]


def return_one_kernel(
    n, dk, dv, o, z, w_out, w_down, gy, a2, dh,
    p_own, dk_own, dv_own, up_sum, g_out, g_down, g_up,
    zov, wdo, dhv, kown, vown, data, cs, zs, ys, ks, vs, tiles, turned, st_wide, st_head, uown, us,
    send, recv, load, fetch_sem, put_sem, near,
):
    place = Place(n)
    net = Net(send, recv)
    greet(place, (1, 2, 4), (1, 2))
    both = orders(2)
    keys = FoldR(net, place, lambda i: dk.at[i], kown, ks, both[0])
    values = FoldR(net, place, lambda i: dv.at[i], vown, vs, both[1])
    total = FoldT(net, place, data, cs, zs, ys, p_own)
    up, pieces = half_fold(
        net, place, g_up.reshape(4, n // 8, 2 * (D // n), FFT), 0, uown, us
    )
    keys.both().start()
    values.both().start()

    loads = [
        pltpu.make_async_copy(src, dst, load.at[k])
        for k, (src, dst) in enumerate(
            (
                (z, zov.at[:, :, :FFT]),
                (o, zov.at[:, :, FFT:]),
                (w_down, wdo.at[:, :FFT]),
                (w_out, wdo.at[:, FFT:]),
                (dk.at[2], kown.at[1]),
                (dv.at[1], vown.at[1]),
                (dk.at[0], kown.at[0]),
                (dv.at[0], vown.at[0]),
                (dh, dhv),
            )
        )
    ]
    for copy in loads:
        copy.start()
    for copy in loads[:4]:
        copy.wait()

    def make(s, idx):
        del s, idx

    def emit(s, idx, put):
        def chunk(k, carry):
            cols = pl.ds(pl.multiple_of(k * HEAD, HEAD), HEAD)
            put((slice(None), cols), contract_cols(zov[s], wdo[cols, :]))
            return carry

        lax.fori_loop(0, D // HEAD, chunk, 0)

    def after(idx):
        @pl.when(idx == 3)
        def _():
            total.more()
            keys.first().start()
            values.first().start()

        @pl.when(idx == 4)
        def _():
            total.turn(0)

        @pl.when(idx == 5)
        def _():
            for copy in loads[4:]:
                copy.wait()
            keys.advance()
            values.advance()

        @pl.when(idx == 6)
        def _():
            total.turn(1)

    total.loop(make, emit, after)
    gradient_tiles(a2, tiles, turned, fetch_sem, [(dhv, st_wide, g_up, put_sem.at[0])])
    own_loads = [
        pltpu.make_async_copy(src, dst, near.at[k]) for k, (src, dst) in enumerate(pieces)
    ]
    up.begin()
    for copy in own_loads:
        copy.start()
    keys.gather()
    values.gather()
    gradient_tiles(
        gy, tiles, turned, fetch_sem,
        [
            (zov.at[:, :, :FFT], st_wide, g_down, put_sem.at[0]),
            (zov.at[:, :, FFT:], st_head, g_out, put_sem.at[1]),
        ],
    )
    for copy in own_loads:
        copy.wait()
    up.advance()
    keys.end(dk_own)
    values.end(dv_own)
    total.turn_own()
    up.gather()
    up.end(up_sum)
    total.end()
    net.finish()


def return_one(n, dk, dv, o, z, w_out, w_down, gy, a2, dh):
    rows = 2 * (D // n)
    head, cols = (8, TOK, HEAD), (8, TOK, FFT)
    half = (4, rows, FFT // 2)
    outs = [
        jax.ShapeDtypeStruct((TOK, D), F32),
        jax.ShapeDtypeStruct(head, BF),
        jax.ShapeDtypeStruct(head, BF),
        jax.ShapeDtypeStruct(half, BF),
        jax.ShapeDtypeStruct((D, HEAD), BF),
        jax.ShapeDtypeStruct((D, FFT), BF),
        jax.ShapeDtypeStruct((D, FFT), BF),
    ]
    scratch = [
        pltpu.VMEM((8, TOK, FFT + HEAD), BF),
        pltpu.VMEM((D, FFT + HEAD), BF),
        pltpu.VMEM(cols, BF),
        pltpu.VMEM((2, *head), BF),
        pltpu.VMEM((2, *head), BF),
        *fold_scratch(),
        pltpu.VMEM((3, *head), BF),
        pltpu.VMEM((3, *head), BF),
        pltpu.VMEM((2, 8, TOK, WIDE), BF),
        pltpu.VMEM((WIDE, 8 * TOK), BF),
        pltpu.VMEM((2, WIDE, FFT), BF),
        pltpu.VMEM((2, WIDE, HEAD), BF),
        pltpu.VMEM((2, *half), BF),
        pltpu.VMEM((3, *half), BF),
    ]

    def kernel(*refs):
        return_one_kernel(n, *refs)

    return pl.pallas_call(
        kernel,
        out_shape=outs,
        in_specs=[ANY] * 9,
        out_specs=[VM] * 4 + [ANY] * 3,
        scratch_shapes=[
            *scratch,
            pltpu.SemaphoreType.DMA((18,)),
            pltpu.SemaphoreType.DMA((18,)),
            pltpu.SemaphoreType.DMA((9,)),
            pltpu.SemaphoreType.DMA((2,)),
            pltpu.SemaphoreType.DMA((2, 2)),
            pltpu.SemaphoreType.DMA((2,)),
        ],
        compiler_params=pltpu.CompilerParams(
            collective_id=2, has_side_effects=True, vmem_limit_bytes=62 * MIB
        ),
    )(dk, dv, o, z, w_out, w_down, gy, a2, dh)


def return_two_kernel(
    n, gi, gu0, gu, go, gd, dq, dk, dv, a1, x, dh, w_in, w_up, cosine, sine, smt, stats, sums,
    oi, ou, oo, od, e_own, osmall, gi_out,
    dqv, dkv, dvv, djp, djn, dhv, wi, wu, xt, cst, snt, data, cs, zs, ys,
    uown, us, ui, uo, ud, si, so, sd, term, blocks, sslots, tiles, turned, st_in,
    send, recv, load, near, x_sem, fetch_sem, put_sem, last_sem,
):
    del gi
    place = Place(n)
    net = Net(send, recv)
    rb = D // n
    R = place.R
    both = orders(2)
    greet(place, range(1, 8), (1, 2))
    names = ((gd, ud, sd, od, 3), (go, uo, so, oo, 2), (gi_out, ui, si, oi, 0))
    parts, pieces = [], []
    for src, own, slots, _, _ in names:
        halves, near_pieces = weight_folds(n, net, place, src, own, slots)
        parts.append(halves)
        pieces += near_pieces
    small = FoldR(
        net, place, lambda i: blocks.at[place.rr_of(i)], None, sslots, both[0]
    )
    total = FoldT(net, place, data, cs, zs, ys, e_own)
    up, up_pieces = half_fold(net, place, gu.reshape(4, R, 2 * rb, FFT), 1, uown, us)

    finals = []
    ends = []
    for _, _, slots, dst, k in names:
        count, width = WEIGHTS[k]
        ends.append(
            (
                lambda zt, rows, cols, slots=slots: slots.at[zt // 2, 2, zt % 2, rows, cols],
                dst, width, [(p * width, p * D) for p in range(count)],
            )
        )
    for h in range(2):
        summed = us.at[2] if h else gu0
        ends.append(
            (
                lambda zt, rows, cols, summed=summed: summed.at[zt, rows, cols],
                ou, FFT // 2, [(0, h * (FFT // 2))],
            )
        )
    for which, (summed, dst, width, spans) in enumerate(ends):
        stride = FFT if dst is ou else width
        ops = []
        for s in range(8):
            rows = pl.ds(pl.multiple_of(place.c_of(s) * rb, rb), rb)
            for p, (at, into) in enumerate(spans):
                cols = pl.ds(pl.multiple_of(into + place.t * stride, 128), width)
                piece = summed(place.zt_of(s), rows, pl.ds(at, width))
                if s == 0:
                    ops.append(
                        pltpu.make_async_copy(
                            piece, dst.at[:, cols], last_sem.at[which * 3 + p]
                        )
                    )
                else:
                    ops.append(
                        net.add(
                            lambda k, piece=piece, dst=dst, cols=cols, s=s: (
                                piece, dst.at[:, cols], place.dev_t(s),
                            )
                        )
                    )
        finals.append(ops)
    small_last = [
        net.add(
            lambda k, s=s: (
                sslots.at[2, place.zt_of(s)], osmall.at[place.t], place.dev_t(s),
            )
        )
        for s in range(1, 8)
    ]
    small_mine = pltpu.make_async_copy(
        sslots.at[2, place.zt], osmall.at[place.t], last_sem.at[15]
    )

    def send_finals(which):
        for k, op in enumerate(finals[which]):
            (op if k < len(ends[which][3]) else op()).start()

    def wait_finals(which):
        for k, op in enumerate(finals[which]):
            if k < len(ends[which][3]):
                op.wait()
            else:
                op().wait_recv()

    up.begin()
    for part in parts[0]:
        part.begin()
    send_finals(3)
    loads = [
        pltpu.make_async_copy(src, dst, load.at[k])
        for k, (src, dst) in enumerate(
            (
                (dq, dqv), (dk, dkv), (dv, dvv), (cosine, cst), (sine, snt),
                (w_in, wi), (dh, dhv), (w_up, wu),
            )
        )
    ]
    for copy in loads:
        copy.start()
    own_loads = [
        pltpu.make_async_copy(src, dst, near.at[k])
        for k, (src, dst) in enumerate(pieces + up_pieces)
    ]
    for copy in own_loads[:8] + own_loads[12:]:
        copy.start()

    def fetch_x(s, slot):
        return pltpu.make_async_copy(x.at[s], xt.at[slot], x_sem.at[slot])

    fetch_x(7, 0).start()
    term[...] = sums[...]
    shuffle = shuffle_matrix().astype(BF)
    head_cols = pl.ds(pl.multiple_of(place.t * HEAD, HEAD), HEAD)
    for copy in loads:
        copy.wait()
    chunk_cols = 256

    def paired_joint(s):
        csn, sn = cst[s], snt[s]
        half = HEAD // 2
        for p, src in enumerate((dqv, dkv)):
            one = src[s, :, :half].astype(F32)
            two = src[s, :, half:].astype(F32)
            djp[:, p * HEAD : p * HEAD + half] = (one * csn + two * sn).astype(BF)
            djp[:, p * HEAD + half : (p + 1) * HEAD] = (two * csn - one * sn).astype(BF)
        djp[:, 2 * HEAD :] = dvv[s]

    def natural_joint(s):
        for p in range(2):
            cols = slice(p * HEAD, (p + 1) * HEAD)
            natural = contract_cols(djp[:, cols], shuffle)
            djn[s, :, cols] = natural.astype(BF)
            term[4 + p : 5 + p, head_cols] += jnp.sum(natural, axis=0, keepdims=True)
        value = dvv[s]
        djn[s, :, 2 * HEAD :] = value
        term[6:7, head_cols] += jnp.sum(value.astype(F32), axis=0, keepdims=True)

    def make(s, idx):
        @pl.when(idx < 4)
        def _():
            paired_joint(s)
            natural_joint(s)

        @pl.when(idx >= 4)
        def _():
            paired_joint(s)

        fetch_x(s, idx % 2).wait()

        @pl.when(idx < 7)
        def _():
            fetch_x(total.order(idx + 1), (idx + 1) % 2).start()

    def emit(s, idx, put):
        average = stats[s, :, 0:1]
        inverse = stats[s, :, 1:2]

        def chunk(k, carry):
            cols = pl.ds(pl.multiple_of(k * chunk_cols, chunk_cols), chunk_cols)
            xhat = (xt[idx % 2, :, cols].astype(F32) - average) * inverse
            one = contract_cols(djp[...], wi[cols, :])
            two = contract_cols(dhv[s], wu[cols, :])
            for row, value in ((0, one * xhat), (1, one), (2, two * xhat), (3, two)):
                term[row : row + 1, cols] += jnp.sum(value, axis=0, keepdims=True)
            put((slice(None), cols), one * smt[0:1, cols] + two * smt[2:3, cols])
            return carry

        lax.fori_loop(0, D // chunk_cols, chunk, 0)

    def after(idx):
        @pl.when(idx == 1)
        def _():
            for copy in own_loads[12:]:
                copy.wait()
            up.advance()

        @pl.when(idx == 2)
        def _():
            total.more()
            for copy in own_loads[:4]:
                copy.wait()
            for part in parts[0]:
                part.advance()
            up.gather()
            up.end()
            send_finals(4)

        @pl.when(idx == 3)
        def _():
            total.turn(0)

            def rest(k, carry):
                paired_joint(6 - 2 * k)
                natural_joint(6 - 2 * k)
                return carry

            lax.fori_loop(0, 4, rest, 0)
            gradient_tiles(a1, tiles, turned, fetch_sem, [(djn, st_in, gi_out, put_sem)])
            for part in parts[2]:
                part.begin()
            for copy in own_loads[8:12]:
                copy.start()
            total.turn(1)
            for part in parts[0]:
                part.gather()
                part.end()
            send_finals(0)

        @pl.when(idx == 4)
        def _():
            for part in parts[1]:
                part.begin()

        @pl.when(idx == 6)
        def _():
            for copy in own_loads[8:12]:
                copy.wait()
            for part in parts[2]:
                part.advance()

        @pl.when(idx == 7)
        def _():
            for copy in own_loads[4:8]:
                copy.wait()
            for part in parts[1]:
                part.advance()

    total.loop(make, emit, after)

    for rr in range(R):
        for zt in range(4):
            at = (zt * R + rr) * 128
            blocks[rr, zt] = term[:, at : at + 128]
    small.both().start()
    small.first().start()
    for part in parts[2]:
        part.gather()
        part.end()
    send_finals(2)
    for part in parts[1]:
        part.gather()
        part.end()
    send_finals(1)
    small.both().wait_recv()
    sslots[0] = sslots[0] + blocks[place.rr_of(2)]
    small.second().start()
    total.turn_own()
    small.first().wait_recv()
    small.second().wait_recv()
    sslots[2] = sslots[2] + (sslots[1] + blocks[place.rr])
    small_mine.start()
    for op in small_last:
        op().start()
    total.end()
    for which in range(5):
        wait_finals(which)
    small_mine.wait()
    for op in small_last:
        op().wait_recv()
    net.finish()


def return_two(n, up_sum, g_up, g_out, g_down, dq, dk, dv, a1, x, dh, w_in, w_up, cosine, sine, smt, stats, sums):
    rb = D // n
    R = n // 8
    head, cols, block = (8, TOK, HEAD), (8, TOK, FFT), (8, TOK, D)
    outs = [jax.ShapeDtypeStruct((rb, HEADS * parts * width), BF) for parts, width in WEIGHTS]
    outs += [
        jax.ShapeDtypeStruct((TOK, D), F32),
        jax.ShapeDtypeStruct((8, SMALLR, 128), F32),
        jax.ShapeDtypeStruct((D, 3 * HEAD), BF),
    ]
    wide = [parts * width for parts, width in WEIGHTS]
    scratch = [
        pltpu.VMEM(head, F32),
        pltpu.VMEM(head, BF),
        pltpu.VMEM(head, BF),
        pltpu.VMEM((TOK, 3 * HEAD), BF),
        pltpu.VMEM((8, TOK, 3 * HEAD), BF),
        pltpu.VMEM(cols, BF),
        pltpu.VMEM((D, 3 * HEAD), BF),
        pltpu.VMEM((D, FFT), BF),
        pltpu.VMEM((2, TOK, D), BF),
        pltpu.VMEM((8, TOK, HEAD // 2), F32),
        pltpu.VMEM((8, TOK, HEAD // 2), F32),
        *fold_scratch(),
        pltpu.VMEM((2, 4, 2 * rb, FFT // 2), BF),
        pltpu.VMEM((3, 4, 2 * rb, FFT // 2), BF),
        *[pltpu.VMEM((2, 2, 2, 2 * rb, wide[k]), BF) for k in (0, 2, 3)],
        *[pltpu.VMEM((2, 3, 2, 2 * rb, wide[k]), BF) for k in (0, 2, 3)],
        pltpu.VMEM((SMALLR, D), F32),
        pltpu.VMEM((R, 4, SMALLR, 128), F32),
        pltpu.VMEM((3, 4, SMALLR, 128), F32),
        pltpu.VMEM((2, 8, TOK, HEAD), BF),
        pltpu.VMEM((HEAD, 8 * TOK), BF),
        pltpu.VMEM((2, HEAD, 3 * HEAD), BF),
    ]
    copies = 6 * 3 + 3 + 3 + 9 + 7 * 7 + 7

    def kernel(*refs):
        return_two_kernel(n, None, *refs)

    return pl.pallas_call(
        kernel,
        out_shape=outs,
        in_specs=[ANY] * 14 + [VM] * 3,
        out_specs=[ANY] * 4 + [VM] + [ANY] * 2,
        scratch_shapes=[
            *scratch,
            pltpu.SemaphoreType.DMA((copies,)),
            pltpu.SemaphoreType.DMA((copies,)),
            pltpu.SemaphoreType.DMA((8,)),
            pltpu.SemaphoreType.DMA((16,)),
            pltpu.SemaphoreType.DMA((2,)),
            pltpu.SemaphoreType.DMA((2,)),
            pltpu.SemaphoreType.DMA((2,)),
            pltpu.SemaphoreType.DMA((16,)),
        ],
        compiler_params=pltpu.CompilerParams(
            collective_id=3, has_side_effects=True, vmem_limit_bytes=62 * MIB
        ),
    )(up_sum, g_up, g_out, g_down, dq, dk, dv, a1, x, dh, w_in, w_up, cosine, sine, smt, stats, sums)


def token_row(base, core, size=RUN):
    lane = lax.broadcasted_iota(jnp.int32, (1, size), 1)
    return base + (lane + core * TOK) % RUN


def token_col(base, core, size=RUN):
    row = lax.broadcasted_iota(jnp.int32, (size, 1), 0)
    return base + (row + core * TOK) % RUN


def start_of(tokens, lengths, nseq):
    out, begin = tokens * 0, lengths[0] * 0
    for s in range(nseq):
        out = jnp.where(tokens >= begin, begin, out)
        begin = begin + lengths[s]
    return out


def run_facts(place, lengths, nseq, u):
    number = place.zt_of_run(u) * place.R + place.rr
    count = number - start_of(number * RUN, lengths, nseq) // RUN + 1
    return number, count, start_of(number * RUN + RUN - 1, lengths, nseq)


def scores_of(key, query):
    return lax.dot_general(key, query, (((1,), (1,)), ((), ())), preferred_element_type=F32)


def seen_mask(core, gq, gk, lengths, nseq):
    tq = token_row(gq * RUN, core)
    tk = token_col(gk * RUN, core)
    return (tk <= tq) & (tk >= start_of(tq, lengths, nseq))


def attend_kernel(
    n, nseq, lengths, q, dout, kg, vg, o, stats, m, l, acc, kv, sem
):
    u = pl.program_id(0)
    place = Place(n)
    number, count, last = run_facts(place, lengths, nseq, u)
    m[...] = jnp.full_like(m, NEGATIVE)
    l[...] = jnp.zeros_like(l)
    acc[...] = jnp.zeros_like(acc)

    def fetch(d, slot):
        far = number - d
        moved = (far // place.R) ^ place.zt
        i, ku = (far % place.R) ^ place.rr, moved % 2 * 2 + moved // 2
        return [
            pltpu.make_async_copy(src.at[i, :, ku], kv.at[slot, p], sem.at[slot, p])
            for p, src in enumerate((kg, vg))
        ]

    def block(slot, far, masked):
        query = q[...].reshape(RUN, HEAD)
        key = kv[slot, 0].reshape(RUN, HEAD)
        value = kv[slot, 1].reshape(RUN, HEAD)
        s = scores_of(key, query)
        if masked:
            s = jnp.where(seen_mask(place.c, number, number - far, lengths, nseq), s, NEGATIVE)
        old = m[0:1, :]
        new = jnp.maximum(old, jnp.max(s, axis=0, keepdims=True))
        p = jnp.exp(s - new)
        fade = jnp.exp(old - new)
        l[0:1, :] = l[0:1, :] * fade + jnp.sum(p, axis=0, keepdims=True)
        m[0:1, :] = new
        mixed = lax.dot_general(
            value, p.astype(BF), (((0,), (0,)), ((), ())), preferred_element_type=F32
        )
        acc[...] = acc[...] * fade + mixed

    for copy in fetch(0, 0):
        copy.start()

    def step(d, carry):
        slot = d % 2
        for copy in fetch(d, slot):
            copy.wait()

        @pl.when(d + 1 < count)
        def _():
            for copy in fetch(d + 1, 1 - slot):
                copy.start()

        edge = (d == 0) | ((number - d) * RUN < last)

        @pl.when(edge)
        def _():
            block(slot, d, True)

        @pl.when(jnp.logical_not(edge))
        def _():
            block(slot, d, False)

        return carry

    lax.fori_loop(0, count, step, 0)
    out = acc[...] / l[0:1, :]
    rows = out.T
    o[...] = rows.astype(BF).reshape(o.shape)
    grad = dout[...].reshape(RUN, HEAD).astype(F32).T
    stats[0, 0:1, :] = m[0:1, :] + jnp.log(l[0:1, :])
    stats[0, 1:2, :] = jnp.sum(out * grad, axis=0, keepdims=True)
    stats[0, 2:8, :] = jnp.zeros((6, RUN), F32)


def attend(n, lengths, q, dout, kg, vg):
    run = pl.BlockSpec((2, 1, TOK, HEAD), lambda u, *_: (0, u, 0, 0))

    def kernel(*refs):
        attend_kernel(n, lengths.shape[0], *refs)

    return pl.pallas_call(
        kernel,
        out_shape=[
            jax.ShapeDtypeStruct((2, 4, TOK, HEAD), BF),
            jax.ShapeDtypeStruct((4, 8, RUN), F32),
        ],
        grid_spec=pltpu.PrefetchScalarGridSpec(
            num_scalar_prefetch=1,
            grid=(4,),
            in_specs=[run, run, ANY, ANY],
            out_specs=[run, pl.BlockSpec((1, 8, RUN), lambda u, *_: (u, 0, 0))],
            scratch_shapes=[
                pltpu.VMEM((8, RUN), F32),
                pltpu.VMEM((8, RUN), F32),
                pltpu.VMEM((HEAD, RUN), F32),
                pltpu.VMEM((2, 2, 2, TOK, HEAD), BF),
                pltpu.SemaphoreType.DMA((2, 2)),
            ],
        ),
        compiler_params=pltpu.CompilerParams(vmem_limit_bytes=62 * MIB),
        cost_estimate=pl.CostEstimate(
            flops=4 * 16 * RUN * RUN * HEAD, bytes_accessed=12 * MIB, transcendentals=16 * RUN * RUN
        ),
    )(lengths, q, dout, kg, vg)


def attend_back_kernel(
    n, nseq, lengths, q, dout, stats, k, v, dq, dk, dv, tq, tk, tv, facts
):
    block_at = pl.program_id(0)
    steps = pl.num_programs(0)

    place = Place(n)

    @pl.when(block_at == 0)
    def _():
        tq[...] = jnp.zeros_like(tq)
        for u in range(4):
            for f, value in enumerate(run_facts(place, lengths, nseq, u)):
                facts[4 * f + u] = value

    tk[...] = jnp.zeros_like(tk)
    tv[...] = jnp.zeros_like(tv)
    here = place.zt_of_run(block_at % 4) * place.R + (place.rr ^ (block_at // 4))

    for u in range(4):
        far = facts[u] - here
        active = (far >= 0) & (far < facts[4 + u])
        edge = (far == 0) | (here * RUN < facts[8 + u])

        def block(masked, u=u):
            query = q[:, u].reshape(RUN, HEAD)
            grad = dout[:, u].reshape(RUN, HEAD)
            key = k[...].reshape(RUN, HEAD)
            value = v[...].reshape(RUN, HEAD)
            s = scores_of(key, query)
            p = jnp.exp(s - stats[u, 0:1, :])
            if masked:
                p = jnp.where(seen_mask(place.c, facts[u], here, lengths, nseq), p, 0.0)
            dp = scores_of(value, grad)
            ds = (p * (dp - stats[u, 1:2, :])).astype(BF)
            tv[...] += jnp.dot(p.astype(BF), grad, preferred_element_type=F32)
            tk[...] += jnp.dot(ds, query, preferred_element_type=F32)
            tq[u] += lax.dot_general(
                ds, key, (((0,), (0,)), ((), ())), preferred_element_type=F32
            )

        @pl.when(active & edge)
        def _(block=block):
            block(True)

        @pl.when(active & jnp.logical_not(edge))
        def _(block=block):
            block(False)

    dk[...] = tk[...].astype(BF).reshape(dk.shape)
    dv[...] = tv[...].astype(BF).reshape(dv.shape)

    @pl.when(block_at == steps - 1)
    def _():
        for u in range(4):
            dq[:, u] = (tq[u] * HEAD**-0.5).reshape(2, TOK, HEAD)


def attend_back(n, lengths, q, dout, stats, kg, vg):
    R = n // 8
    whole = pl.BlockSpec((2, 4, TOK, HEAD), lambda b, *_: (0, 0, 0, 0))
    key = pl.BlockSpec((1, 2, 1, TOK, HEAD), lambda b, *_: (b // 4, 0, b % 4, 0, 0))

    def kernel(*refs):
        attend_back_kernel(n, lengths.shape[0], *refs)

    return pl.pallas_call(
        kernel,
        out_shape=[
            jax.ShapeDtypeStruct((2, 4, TOK, HEAD), F32),
            jax.ShapeDtypeStruct((R, 2, 4, TOK, HEAD), BF),
            jax.ShapeDtypeStruct((R, 2, 4, TOK, HEAD), BF),
        ],
        grid_spec=pltpu.PrefetchScalarGridSpec(
            num_scalar_prefetch=1,
            grid=(4 * R,),
            in_specs=[
                whole,
                whole,
                pl.BlockSpec((4, 8, RUN), lambda b, *_: (0, 0, 0)),
                key,
                key,
            ],
            out_specs=[whole, key, key],
            scratch_shapes=[
                pltpu.VMEM((4, RUN, HEAD), F32),
                pltpu.VMEM((RUN, HEAD), F32),
                pltpu.VMEM((RUN, HEAD), F32),
                pltpu.SMEM((12,), jnp.int32),
            ],
        ),
        compiler_params=pltpu.CompilerParams(vmem_limit_bytes=62 * MIB),
        cost_estimate=pl.CostEstimate(
            flops=10 * 16 * RUN * RUN * HEAD, bytes_accessed=24 * MIB, transcendentals=16 * RUN * RUN
        ),
    )(lengths, q, dout, stats, kg, vg)


def adam_step(parameter, gradient, first_moment, second_moment, step_rate):
    first_new = BETA_ONE * first_moment + (1.0 - BETA_ONE) * gradient
    second_new = BETA_TWO * second_moment + (1.0 - BETA_TWO) * gradient * gradient
    first_hat = first_new * (1.0 / (1.0 - BETA_ONE**STEPS))
    second_hat = second_new * (1.0 / (1.0 - BETA_TWO**STEPS))
    parameter_new = parameter - step_rate * (
        first_hat / (jnp.sqrt(second_hat) + ADAM_EPS) + WEIGHT_DECAY * parameter
    )
    return (first_new, second_new, parameter_new)


def adam_kernel(rates, *refs):
    count = len(rates)
    x, gy, e, part, small = refs[:5]
    groups = [refs[5 + k * count : 5 + (k + 1) * count] for k in range(7)]
    block_out, token_grad = refs[5 + 7 * count :]
    for p, g, m, v, rate, p_out, m_out, v_out in zip(
        *groups[:4], rates, *groups[4:]
    ):
        m_out[...], v_out[...], p_out[...] = adam_step(
            p[...], g[...].astype(F32), m[...], v[...], rate
        )
    xf, grad = x[...].astype(F32), e[...]
    block_out[...] = (xf + part[...] + small[7:8, :] + small[8:9, :]).astype(BF)
    centred = xf - jnp.mean(xf, axis=-1, keepdims=True)
    inverse = lax.rsqrt(jnp.mean(centred * centred, axis=-1, keepdims=True) + NORM_EPS)
    xhat = centred * inverse
    token_grad[...] = gy[...].astype(F32) + inverse * (
        grad
        - jnp.mean(grad, axis=-1, keepdims=True)
        - xhat * jnp.mean(grad * xhat, axis=-1, keepdims=True)
    )


def adam(own, params, grads, firsts, seconds, rates):
    steps = 8

    def spec(a):
        return pl.BlockSpec((a.shape[0], a.shape[1] // steps), lambda k: (0, k))

    tok = pl.BlockSpec((TOK // steps, D), lambda k: (k, 0))
    small = pl.BlockSpec((SMALLR, D), lambda k: (0, 0))
    arrays = [*params, *grads, *firsts, *seconds]
    outs = [jax.ShapeDtypeStruct(p.shape, F32) for _ in range(3) for p in params]
    own_outs = [jax.ShapeDtypeStruct((TOK, D), BF), jax.ShapeDtypeStruct((TOK, D), F32)]

    def kernel(*refs):
        adam_kernel(rates, *refs)

    out = pl.pallas_call(
        kernel,
        out_shape=[*outs, *own_outs],
        grid=(steps,),
        in_specs=[tok] * 4 + [small] + [spec(a) for a in arrays],
        out_specs=[spec(a) for a in outs] + [tok] * 2,
        compiler_params=pltpu.CompilerParams(vmem_limit_bytes=62 * MIB),
    )(*own, *arrays)
    count = len(params)
    return [out[k * count : (k + 1) * count] for k in range(3)] + list(out[3 * count :])


def contract_rows(left, right):
    return lax.dot_general(left, right, (((0,), (0,)), ((), ())), preferred_element_type=F32)


def contract_cols(left, right):
    return lax.dot_general(left, right, (((1,), (1,)), ((), ())), preferred_element_type=F32)


def paired(columns):
    turned, half = HEAD // 8, HEAD // 2
    heads = columns.reshape(columns.shape[0], -1, HEAD)
    cut = 2 * turned + half - turned
    order = [(0, turned), (2 * turned, cut), (turned, 2 * turned), (cut, HEAD)]
    return jnp.concatenate([heads[..., a:b] for a, b in order], axis=-1).reshape(columns.shape)


def unpaired(columns):
    turned, half = HEAD // 8, HEAD // 2
    heads = columns.reshape(columns.shape[0], -1, HEAD)
    order = [(0, turned), (half, half + turned), (turned, half), (half + turned, HEAD)]
    return jnp.concatenate([heads[..., a:b] for a, b in order], axis=-1).reshape(columns.shape)


def turn(values, cosine, sine):
    half = HEAD // 2
    one, two = values[:, :half], values[:, half:]
    return jnp.concatenate([one * cosine - two * sine, two * cosine + one * sine], axis=1)


def pack_small(columns, n):
    rb = D // n
    blocks = columns.reshape(SMALLR, n, rb).transpose(1, 0, 2)
    return jnp.pad(blocks, ((0, 0), (0, 0), (0, 128 - rb)))


def return_plain(n, gg, xg, a1, a2, z, dh, o, dq, dk, dv, ws, cosine, sine, small_all, sums):
    place = Place(n)
    R, rb, rows = n // 8, D // n, 8 * TOK
    a1, a2, gy, z, dh, o, dq = (v.reshape(rows, -1) for v in (a1, a2, gg, z, dh, o, dq))
    w_in, w_up, w_out, w_down = (g.reshape(D, -1) for g in ws)
    cosine, sine = cosine.reshape(rows, -1), sine.reshape(rows, -1)
    g1, g2 = small_all[0], small_all[2]
    xf = xg.reshape(rows, D).astype(F32)
    centred = xf - jnp.mean(xf, axis=-1, keepdims=True)
    xhat = centred * lax.rsqrt(jnp.mean(centred * centred, axis=-1, keepdims=True) + NORM_EPS)
    partial_out = (contract_cols(o, w_out) + contract_cols(z, w_down)).astype(BF)
    ins = {"k": dk, "v": dv, "p": partial_out.reshape(8, TOK, D)}
    back = {}
    for at, name in enumerate(ins):
        back |= return_keys(n, {name: ins[name]}, 4 + at)
    dq = turn(dq, cosine, -sine)
    dk = turn(back["k"].reshape(rows, HEAD).astype(F32), cosine, -sine)
    dj = jnp.concatenate([dq.astype(BF), dk.astype(BF), back["v"].reshape(rows, HEAD)], axis=1)
    da1 = contract_cols(dj, w_in)
    da2 = contract_cols(dh, w_up)
    e = (da1 * g1 + da2 * g2).astype(BF)
    norm_grads = [jnp.sum(v, axis=0) for v in (da1 * xhat, da1, da2 * xhat, da2)]
    dj = jnp.concatenate([unpaired(dj[:, : 2 * HEAD]), dj[:, 2 * HEAD :]], axis=1)
    dj_sum = jnp.sum(dj.astype(F32), axis=0).reshape(3, HEAD)
    own_cols = lax.dynamic_update_slice(
        jnp.zeros((SMALLR, D), F32), dj_sum, (jnp.int32(4), place.t * HEAD)
    )
    small_term = own_cols + sums
    small_term = small_term.at[:4].set(jnp.stack(norm_grads))
    small_blocks = pack_small(small_term, n).reshape(4, R, 2 * SMALLR, 128)
    grads = [
        contract_rows(left, right).astype(BF).reshape(4, R, 2 * rb, -1)
        for left, right in ((a1, dj), (a2, dh), (gy, o), (gy, z))
    ]
    *weight_grads, e_own, small_parts = return_grads(
        n, grads, e.reshape(8, TOK, D), small_blocks, 3
    )
    return back["p"], weight_grads, e_own, jnp.sum(small_parts, axis=0)[:SMALLC, :rb].T


def body(
    tokens, cotangent, lengths,
    attend_in, widening, attend_out, narrowing, small_params,
    first_attend_in, first_widening, first_attend_out, first_narrowing, first_small,
    second_attend_in, second_widening, second_attend_out, second_narrowing, second_small,
):
    n = lax.axis_size("fsdp")
    place = Place(n)
    R = place.R
    rb = D // n
    turned = HEAD // 8
    lanes = np.arange(HEAD // 2)
    frequency = np.where(lanes < turned, ROPE_BASE ** (-2.0 * lanes / (2 * turned)), 0.0)
    frequency = jnp.asarray(frequency.astype(np.float32)[None, :])

    small_rows = jnp.pad(small_params, ((0, 0), (0, 128 - SMALLC)))
    low_in = attend_in.astype(BF)
    low_in = jnp.concatenate([paired(low_in[:, : 2 * D]), low_in[:, 2 * D :]], axis=1)
    weights = [low_in] + [w.astype(BF) for w in (widening, attend_out, narrowing)]
    runs = (2, 4, TOK, HEAD)
    xg, gg, a1, a2, *ws, q, kg, vg, z, dh, dout, small_all, sums, stats_x, cosine, sine = forward(
        n, tokens, cotangent, weights, small_rows, lengths, frequency
    )
    xg, gg, a1, a2, z, dh, stats_x, cosine, sine = (
        v.reshape(8, TOK, v.shape[-1]) for v in (xg, gg, a1, a2, z, dh, stats_x, cosine, sine)
    )

    kg = kg.reshape(R, *runs)
    vg = vg.reshape(R, *runs)
    q4, dout4 = q.reshape(runs), dout.reshape(runs)
    o4, stats = attend(n, lengths, q4, dout4, kg, vg)
    dq4, dk5, dv5 = attend_back(n, lengths, q4, dout4, stats, kg, vg)
    o, dq = o4.reshape(8, TOK, HEAD), dq4.reshape(8, TOK, HEAD)
    dk, dv = dk5.reshape(R, 8, TOK, HEAD), dv5.reshape(R, 8, TOK, HEAD)
    if R == 4:
        p_own, dk, dv, up_sum, g_out, g_down, g_up = return_one(
            n, dk, dv, o, z, ws[2].reshape(D, -1), ws[3].reshape(D, -1), gg, a2, dh
        )
        *weight_grads, e_own, small_parts, _ = return_two(
            n, up_sum, g_up, g_out, g_down, dq, dk, dv, a1, xg, dh,
            ws[0].reshape(D, -1), ws[1].reshape(D, -1), cosine, sine, small_all, stats_x, sums,
        )
        own_lanes = lax.dynamic_slice(
            jnp.sum(small_parts, axis=0), (0, place.c * rb), (SMALLR, rb)
        )
        small_grad = own_lanes[:SMALLC].T
    else:
        p_own, weight_grads, e_own, small_grad = return_plain(
            n, gg, xg, a1, a2, z, dh, o, dq, dk, dv, ws, cosine, sine, small_all, sums
        )
    gr_in, gr_up, gr_out, gr_down = weight_grads
    rate_inner = 2.5 * D ** (-0.5)
    rate_outer = 2.5 * (D * 11 // LMAX) ** (-0.5)
    rate_down = 2.5 * FF ** (-0.5)
    rate_small = 0.5
    new, mean, square, block_out, token_grad = adam(
        (tokens, cotangent, e_own, p_own, small_all),
        (attend_in, widening, attend_out, narrowing),
        (gr_in, gr_up, gr_out, gr_down),
        (first_attend_in, first_widening, first_attend_out, first_narrowing),
        (second_attend_in, second_widening, second_attend_out, second_narrowing),
        (rate_inner, rate_inner, rate_outer, rate_down),
    )
    mean_small, square_small, new_small = adam_step(
        small_params, small_grad, first_small, second_small, rate_small
    )
    return (
        block_out,
        token_grad,
        *new,
        new_small,
        *mean,
        mean_small,
        *square,
        square_small,
    )


def solution(mesh):
    spec = P("fsdp", None)
    return jax.shard_map(
        body,
        mesh=mesh,
        in_specs=(spec, spec, P(), *[spec] * 15),
        out_specs=(spec,) * 17,
        check_vma=False,
    )
```

```python
import math

import jax
import jax.numpy as jnp
import numpy as np
from jax import lax
from jax.experimental import pallas as pl
from jax.experimental.pallas import tpu as pltpu
from jax.sharding import PartitionSpec as P

D = 2048
HEADS = 8
HEAD = D // HEADS
FF = 8192
FFT = FF // HEADS
LMAX = 4096
STEPS = 10
TOK = 256
RUN = 2 * TOK
BACK_RUNS = LMAX // RUN + 1

NORM_EPS = 1e-05
ADAM_EPS = 1e-08
BETA_ONE = 0.9
BETA_TWO = 0.95
WEIGHT_DECAY = 0.01
NEGATIVE = -1e30
ROPE_BASE = 10000.0
SMALLC = 13
SMALLR = 16

BF = jnp.bfloat16
F32 = jnp.float32
ANY = pl.BlockSpec(memory_space=pl.ANY)
VM = pl.BlockSpec(memory_space=pltpu.VMEM)
MIB = 1024 * 1024
WEIGHTS = ((3, HEAD), (1, FFT), (1, HEAD), (1, FFT))


class Place:
    def __init__(self, n):
        self.n = n
        self.S = n // 4
        self.R = self.S // 2
        self.bits = int(math.log2(self.R))
        me = lax.axis_index("fsdp")
        self.me = me
        self.zt = me // self.S
        self.rr = (me % self.S) // 2
        self.c = me % 2
        self.z1 = self.zt // 2
        self.z0 = self.zt % 2
        self.t = self.zt * 2 + self.c

    def zt_of(self, s):
        z1 = 1 - self.z1 if s & 1 else self.z1
        z0 = 1 - self.z0 if s & 2 else self.z0
        return z1 * 2 + z0

    def zt_of_run(self, u):
        z1 = self.z1 + (1 - 2 * self.z1) * (u % 2)
        z0 = self.z0 + (1 - 2 * self.z0) * (u // 2)
        return z1 * 2 + z0

    def c_of(self, s):
        return 1 - self.c if s & 4 else self.c

    def t_of(self, s):
        return self.zt_of(s) * 2 + self.c_of(s)

    def rr_of(self, i):
        out = 0
        for k in range(self.bits):
            bit = (self.rr // (1 << k)) % 2
            out = out + (1 - bit if i >> k & 1 else bit) * (1 << k)
        return out

    def dev_t(self, s):
        return self.zt_of(s) * self.S + self.rr * 2 + self.c_of(s)

    def dev_r(self, i):
        return self.zt * self.S + self.rr_of(i) * 2 + self.c


class Copies:
    def __init__(self, send, recv):
        self.send, self.recv, self.count, self.started = send, recv, 0, []

    def remote(self, src, dst, dev):
        k = self.count
        self.count += 1
        copy = pltpu.make_async_remote_copy(
            src_ref=src,
            dst_ref=dst,
            send_sem=self.send.at[k],
            recv_sem=self.recv.at[k],
            device_id=(dev,),
            device_id_type=pl.DeviceIdType.MESH,
        )
        copy.start()
        self.started.append(copy)
        return copy

    def local(self, src, dst):
        k = self.count
        self.count += 1
        copy = pltpu.make_async_copy(src, dst, self.send.at[k])
        copy.start()
        return copy

    def finish(self):
        for copy in self.started:
            copy.wait_send()


def greet(place, t_group, r_group):
    barrier = pltpu.get_barrier_semaphore()
    peers = [place.dev_t(s) for s in t_group] + [place.dev_r(i) for i in r_group]
    for dev in peers:
        pl.semaphore_signal(barrier, inc=1, device_id=(dev,), device_id_type=pl.DeviceIdType.MESH)
    pl.semaphore_wait(barrier, len(peers))


def top_bit(s):
    return 1 << (s.bit_length() - 1)


def orders(bits):
    up = [1 << k for k in range(bits)]
    return [up, up[::-1]]


def spread(order):
    have, out = [0], []
    for bit in order:
        new = [i | bit for i in have]
        out += [(i, bit) for i in new]
        have = have + new
    return out


def collected(order):
    left, out = list(range(1 << len(order))), []
    for bit in order:
        out.append((bit, [i for i in left if i & bit]))
        left = [i for i in left if not i & bit]
    return out


def add_rows(dst, a, b):
    lead = dst.shape[:-2]
    rows, columns = dst.shape[-2:]
    size = min(rows, max(16, 1 << int(math.log2(16384 // columns))))
    for flat in range(math.prod(lead)):
        where, rest = [], flat
        for extent in lead[::-1]:
            where.insert(0, rest % extent)
            rest //= extent

        def step(k, carry, where=tuple(where)):
            at = where + (pl.ds(pl.multiple_of(k * size, size), size), slice(None))
            dst[at] = (a[at].astype(F32) + b[at].astype(F32)).astype(dst.dtype)
            return carry

        lax.fori_loop(0, rows // size, step, 0)


def call(kernel, ins, in_specs, outs, out_specs, scratch, collective_id, copies, vmem=60):
    return pl.pallas_call(
        kernel,
        out_shape=outs,
        in_specs=in_specs,
        out_specs=out_specs,
        scratch_shapes=[
            *scratch,
            pltpu.SemaphoreType.DMA((copies,)),
            pltpu.SemaphoreType.DMA((copies,)),
        ],
        compiler_params=pltpu.CompilerParams(
            collective_id=collective_id, has_side_effects=True, vmem_limit_bytes=vmem * MIB
        ),
    )(*ins)


class Net:
    def __init__(self, send, recv):
        self.send, self.recv, self.makers, self.count = send, recv, [], 0

    def add(self, maker, many=1):
        base = self.count
        self.count += many

        def build(k=0):
            src, dst, dev = maker(k)
            return pltpu.make_async_remote_copy(
                src_ref=src,
                dst_ref=dst,
                send_sem=self.send.at[base + k],
                recv_sem=self.recv.at[base + k],
                device_id=(dev,),
                device_id_type=pl.DeviceIdType.MESH,
            )

        self.makers.append((build, many))
        return build

    def finish(self):
        for build, many in self.makers:
            if many == 1:
                build().wait_send()
            else:

                def one(k, carry, build=build):
                    build(k).wait_send()
                    return carry

                lax.fori_loop(0, many, one, 0)


class GatherT:
    def __init__(self, net, place, own, out):
        self.ops = {}
        for s in range(1, 8):
            hop = top_bit(s)
            src = own if s == hop else out.at[(s - hop) // 4, (s - hop) % 4]
            self.ops[s] = net.add(
                lambda k, src=src, s=s, hop=hop: (src, out.at[s // 4, s % 4], place.dev_t(hop))
            )

    def start(self, *which):
        for s in which:
            self.ops[s]().start()

    def wait(self, *which):
        for s in which:
            self.ops[s]().wait_recv()


class GatherR:
    def __init__(self, net, place, region, order):
        self.plan = spread(order)
        self.ops = {}
        self.later = [(i, bit) for i, bit in self.plan if i != bit]
        self.used = {i ^ bit for i, bit in self.later}
        for i, bit in self.plan:
            self.ops[i] = net.add(
                lambda k, i=i, bit=bit: (region(i ^ bit), region(i ^ bit), place.dev_r(bit))
            )

    def begin(self):
        for i, bit in self.plan:
            if i == bit:
                self.ops[i]().start()

    def advance(self):
        seen = set()
        for i, bit in self.later:
            if i ^ bit not in seen:
                self.ops[i ^ bit]().wait_recv()
                seen.add(i ^ bit)
            self.ops[i]().start()

    def end(self):
        for i, _ in self.plan:
            if i not in self.used:
                self.ops[i]().wait_recv()


def cosine_and_sine(x):
    turns = jnp.floor(x * (2.0 / math.pi) + 0.5)
    r = ((x - turns * 1.5703125) - turns * 4.837512969970703e-4) - turns * 7.549789954891882e-8
    z = r * r
    sine = ((-1.9515295891e-4 * z + 8.3321608736e-3) * z - 1.6666654611e-1) * z * r + r
    cosine = (
        ((2.443315711809948e-5 * z - 1.388731625493765e-3) * z + 4.166664568298827e-2) * z * z
        - 0.5 * z
        + 1.0
    )
    quarter = turns - 4.0 * jnp.floor(turns * 0.25)
    odd = (quarter == 1.0) | (quarter == 3.0)
    first, second = jnp.where(odd, sine, cosine), jnp.where(odd, cosine, sine)
    return (
        jnp.where((quarter == 1.0) | (quarter == 2.0), -first, first),
        jnp.where(quarter >= 2.0, -second, second),
    )


def shuffle_matrix():
    turned, half = HEAD // 8, HEAD // 2
    into = lax.broadcasted_iota(jnp.int32, (HEAD, HEAD), 1)
    source = lax.broadcasted_iota(jnp.int32, (HEAD, HEAD), 0)
    moved = jnp.where((into >= turned) & (into < half), into + turned, into)
    moved = jnp.where((into >= half) & (into < half + turned), into - (half - turned), moved)
    return jnp.where(source == moved, 1.0, 0.0).astype(F32)


def weight_halves(net, place, ref):
    both = orders(place.bits)
    return [
        GatherR(net, place, lambda i, h=h: ref.at[pl.ds(2 * h, 2), place.rr_of(i)], both[h])
        for h in range(2)
    ]


def forward_kernel(
    n, nseq, x, gy, wi, wu, wo, wd, small, lengths, frequency,
    xg, gg, a1g, a2g, oi, ou, oo, od, qo, kg, vg, zo, dho, dout, smt, sums, stats, cosine, sine,
    xv, gv, sm, ti, tu, to, td, slope, a2v, qkv, at, ztile, dht, bias, dhsum,
    send, recv, local, out_sem, g_sem,
):
    place = Place(n)
    rb = D // n
    net = Net(send, recv)
    weights = list(zip((wi, wu, wo, wd), (ti, tu, to, td), WEIGHTS))
    greet(place, range(1, 8), [1 << k for k in range(place.bits)])
    mine = pl.ds(pl.multiple_of(place.c * rb, rb), rb)

    small_t = [
        net.add(lambda k, s=s: (small, sm.at[place.zt, place.rr, mine, :], place.dev_t(s)))
        for s in range(1, 8)
    ]

    def columns(p, width, t):
        return pl.ds(pl.multiple_of(p * D + t * width, 128), width)

    def exchange(which):
        src, dst, (parts, width) = weights[which]
        return [
            net.add(
                lambda k, s=s, p=p: (
                    src.at[:, columns(p, width, place.t_of(s))],
                    dst.at[place.zt, place.rr, mine, pl.ds(p * width, width)],
                    place.dev_t(s),
                )
            )
            for s in range(1, 8)
            for p in range(parts)
        ]

    to_t = [exchange(k) for k in range(4)]
    small_r = GatherR(net, place, lambda i: sm.at[:, place.rr_of(i)], orders(place.bits)[0])
    to_r = [weight_halves(net, place, w[1]) for w in weights]
    x_t = GatherT(net, place, x, xv)
    g_t = GatherT(net, place, gy, gv)
    both = orders(place.bits)
    keys = []
    for own, out, order in ((qkv.at[1], kg, both[0]), (qkv.at[2], vg, both[1])):
        ops = {}
        for i, bit in spread(order):
            ops[i] = net.add(
                lambda s, i=i, bit=bit, own=own, out=out: (
                    own.at[s // 4, s % 4] if i == bit else out.at[i ^ bit, s // 4, s % 4],
                    out.at[i, s // 4, s % 4],
                    place.dev_r(bit),
                ),
                8,
            )
        keys.append((ops, spread(order)))

    def start(ops):
        for op in ops:
            op().start()

    def wait(ops):
        for op in ops:
            op().wait_recv()

    locals_ = [
        pltpu.make_async_copy(x, xv.at[0, 0], local.at[0]),
        pltpu.make_async_copy(gy, gv.at[0, 0], local.at[1]),
        pltpu.make_async_copy(small, sm.at[place.zt, place.rr, mine, :], local.at[2]),
    ]
    for src, dst, (parts, width) in weights:
        for p in range(parts):
            locals_.append(
                pltpu.make_async_copy(
                    src.at[:, columns(p, width, place.t)],
                    dst.at[place.zt, place.rr, mine, pl.ds(p * width, width)],
                    local.at[len(locals_)],
                )
            )
    for copy in locals_:
        copy.start()
    start(small_t)
    start(to_t[0])
    x_t.start(4)
    for copy in locals_:
        copy.wait()
    wait(small_t)
    small_r.begin()
    wait(to_t[0])
    for part in to_r[0]:
        part.begin()
    start(to_t[1])
    x_t.start(2, 1)
    small_r.advance()
    for part in to_r[0]:
        part.advance()

    def tables(s, carry):
        core, u = s // 4, s % 4
        device = (
            place.zt_of_run(u) * place.S + place.rr * 2 + place.c + (1 - 2 * place.c) * core
        )
        token = device * TOK + lax.broadcasted_iota(jnp.int32, (TOK, HEAD // 2), 0)
        offset = token - start_of(token, lengths, nseq)
        angles = offset.astype(F32) * frequency[0:1, :]
        cosine[core, u], sine[core, u] = cosine_and_sine(angles)
        return carry

    lax.fori_loop(0, 8, tables, 0)
    wait(to_t[1])
    for part in to_r[1]:
        part.begin()
    start(to_t[3])
    start(to_t[2])
    small_r.end()

    smt[...] = sm[...].reshape(D, 128).T[:SMALLR, :]
    head_cols = pl.ds(pl.multiple_of(place.t * HEAD, HEAD), HEAD)
    shuffle = shuffle_matrix()
    three = jnp.dot(
        smt[0:8, head_cols], shuffle, precision=lax.Precision.HIGHEST, preferred_element_type=F32
    )
    for p in range(2):
        bias[0:1, p * HEAD : (p + 1) * HEAD] = three[4 + p : 5 + p, :]
    bias[0:1, 2 * HEAD : 3 * HEAD] = smt[6:7, head_cols]

    def repeat_matrix():
        lane = lax.broadcasted_iota(jnp.int32, (HEAD, FFT), 1)
        row = lax.broadcasted_iota(jnp.int32, (HEAD, FFT), 0)
        return jnp.where(lane // 4 == row, 1.0, 0.0).astype(F32)

    four = jnp.dot(
        smt[8:16, head_cols],
        repeat_matrix(),
        precision=lax.Precision.HIGHEST,
        preferred_element_type=F32,
    )
    lane8 = lax.broadcasted_iota(jnp.int32, (8, FFT), 1)
    row8 = lax.broadcasted_iota(jnp.int32, (8, FFT), 0)
    bias[1:2, :] = jnp.sum(jnp.where(lane8 % 4 + 1 == row8, four, 0.0), axis=0, keepdims=True)

    for part in to_r[0]:
        part.end()
    copy_out = [pltpu.make_async_copy(ti, oi, local.at[0])]
    copy_out[0].start()

    def norms(u):
        def chunk(r, carry):
            at_rows = (r // 16, pl.ds(pl.multiple_of(r % 16 * 16, 16), 16), slice(None))
            in_rows = (at_rows[0], u, *at_rows[1:])
            xf = xv[in_rows].astype(F32)
            average = jnp.mean(xf, axis=1, keepdims=True)
            centred = xf - average
            var = jnp.mean(centred * centred, axis=1, keepdims=True)
            inverse = lax.rsqrt(var + NORM_EPS)
            xhat = centred * inverse
            at[at_rows] = (xhat * smt[0:1, :] + smt[1:2, :]).astype(BF)
            a2v[in_rows] = (xhat * smt[2:3, :] + smt[3:4, :]).astype(BF)
            lanes = lax.broadcasted_iota(jnp.int32, (16, 128), 1)
            stats[in_rows] = jnp.where(lanes == 0, average, inverse)
            return carry

        lax.fori_loop(0, 2 * TOK // 16, chunk, 0, unroll=4)

    def place_of(k):
        return k % 2 * 2 + k // 2

    def events(k, table):
        for when, what in table.items():

            @pl.when(k == when)
            def _(what=what):
                for fn in what:
                    fn()

    def staged(buffer, out, u, sem):
        return pltpu.make_async_copy(buffer, out.at[:, u], out_sem.at[sem])

    def free(buffer, out, k, sem):
        @pl.when(k >= 1)
        def _():
            staged(buffer, out, 0, sem).wait()

    def forward_keys(s):
        for ops, plan in keys:
            seen = set()
            for i, bit in plan:
                if i != bit:
                    if i ^ bit not in seen:
                        ops[i ^ bit](s).wait_recv()
                        seen.add(i ^ bit)
                    ops[i](s).start()

    def hidden_units(k):
        u = place_of(k)

        def columns_of(c, carry):
            cols = pl.ds(pl.multiple_of(c * HEAD, HEAD), HEAD)
            hidden = jnp.dot(
                a2v[:, u].reshape(RUN, D),
                tu[:, :, :, cols].reshape(D, HEAD),
                preferred_element_type=F32,
            )
            slope[:, u, :, cols] = (hidden + bias[1:2, cols]).reshape(2, TOK, HEAD)
            return carry

        lax.fori_loop(0, FFT // HEAD, columns_of, 0)
        free(ztile, zo, k, 1)

        def chunk(r, carry):
            at_rows = (r // 16, pl.ds(pl.multiple_of(r % 16 * 16, 16), 16), slice(None))
            in_rows = (at_rows[0], u, *at_rows[1:])
            h = slope[in_rows]
            bell = jnp.exp(-0.5 * h * h)
            t = 1.0 / (1.0 + (0.3275911 * 0.5**0.5) * jnp.abs(h))
            series = t * (
                0.254829592
                + t * (-0.284496736 + t * (1.421413741 + t * (-1.453152027 + t * 1.061405429)))
            )
            tail = 0.5 * series * bell
            phi = jnp.where(h < 0.0, tail, 1.0 - tail)
            ztile[at_rows] = (h * phi).astype(BF)
            slope[in_rows] = phi + h * bell * (1.0 / math.sqrt(2.0 * math.pi))
            return carry

        lax.fori_loop(0, 2 * TOK // 16, chunk, 0, unroll=2)
        staged(ztile, zo, u, 1).start()

    def projections(k):
        u = place_of(k)
        free(at, a1g, k, 0)
        norms(u)
        half = HEAD // 2

        def part(p, carry):
            cols = pl.ds(pl.multiple_of(p * HEAD, HEAD), HEAD)
            joint = jnp.dot(
                at[...].reshape(RUN, D),
                ti[:, :, :, cols].reshape(D, HEAD),
                preferred_element_type=F32,
            )
            joint += bias[0:1, cols]
            turned = p < 2
            cs = jnp.where(turned, cosine[:, u].reshape(RUN, half), 1.0)
            sn = jnp.where(turned, sine[:, u].reshape(RUN, half), 0.0)
            scale = jnp.where(p == 0, HEAD**-0.5, 1.0).astype(F32)
            one, two = joint[:, :half], joint[:, half:]
            for at_col, value in ((0, one * cs - two * sn), (half, two * cs + one * sn)):
                value = (value.astype(BF).astype(F32) * scale).astype(BF)
                qkv[p, :, u, :, at_col : at_col + half] = value.reshape(2, TOK, half)
            return carry

        lax.fori_loop(0, 3, part, 0)
        staged(at, a1g, u, 0).start()
        for core in range(2):
            for ops, plan in keys:
                for i, bit in plan:
                    if i == bit:
                        ops[i](core * 4 + u).start()

    def first(k, carry):
        events(
            k,
            {
                0: [lambda: x_t.wait(4)],
                1: [
                    lambda: [p.advance() for p in to_r[1]],
                    lambda: x_t.wait(2),
                    lambda: x_t.start(6),
                    lambda: x_t.wait(6),
                ],
                2: [
                    lambda: x_t.wait(1),
                    lambda: x_t.start(3, 5),
                    lambda: [p.end() for p in to_r[1]],
                    lambda: pltpu.make_async_copy(tu, ou, local.at[1]).start(),
                ],
                3: [
                    lambda: wait(to_t[3]),
                    lambda: wait(to_t[2]),
                    lambda: [p.begin() for p in to_r[3] + to_r[2]],
                    lambda: g_t.start(1, 4),
                ],
                4: [lambda: x_t.wait(5)],
                5: [
                    lambda: [p.advance() for p in to_r[3] + to_r[2]],
                    lambda: x_t.wait(3),
                    lambda: x_t.start(7),
                    lambda: g_t.start(2),
                    lambda: x_t.wait(7),
                ],
                7: [lambda: g_t.wait(1), lambda: g_t.start(3, 5)],
            },
        )
        late = k // 4

        @pl.when(k % 4 < 2)
        def _():
            projections(k - 2 * late)

        @pl.when(k % 4 >= 2)
        def _():
            hidden_units(k - 2 - 2 * late)

        @pl.when((k == 3) | (k >= 5))
        def _():
            pair = k - 3 - late
            for core in range(2):
                forward_keys(core * 4 + place_of(pair))

        return carry

    lax.fori_loop(0, 8, first, 0)
    own_out = [
        pltpu.make_async_copy(qkv.at[1], kg.at[0], local.at[4]),
        pltpu.make_async_copy(qkv.at[2], vg.at[0], local.at[5]),
        pltpu.make_async_copy(qkv.at[0], qo, local.at[7]),
        pltpu.make_async_copy(xv, xg, local.at[6]),
        pltpu.make_async_copy(a2v, a2g, local.at[8]),
    ]
    for copy in own_out:
        copy.start()
    copy_out.append(pltpu.make_async_copy(tu, ou, local.at[1]))

    def finish_keys(s, carry):
        for ops, plan in keys:
            used = {i ^ bit for i, bit in plan if i != bit}
            for i, bit in plan:
                if i not in used:
                    ops[i](s).wait_recv()
        return carry

    for part in to_r[3] + to_r[2]:
        part.end()
    copy_out += [
        pltpu.make_async_copy(to, oo, local.at[2]),
        pltpu.make_async_copy(td, od, local.at[3]),
    ]
    copy_out[2].start()
    copy_out[3].start()
    dhsum[...] = jnp.zeros_like(dhsum)

    def third(k, carry):
        u = place_of(k)
        events(
            k,
            {
                0: [lambda: g_t.wait(4)],
                1: [lambda: g_t.wait(2), lambda: g_t.start(6), lambda: g_t.wait(6)],
                2: [lambda: g_t.wait(5)],
                3: [lambda: g_t.wait(3), lambda: g_t.start(7), lambda: g_t.wait(7)],
            },
        )
        free(dht, dho, k, 2)
        pltpu.make_async_copy(gv.at[:, u], gg.at[:, u], g_sem.at[u]).start()
        def columns_of(c, carry):
            cols = pl.ds(pl.multiple_of(c * HEAD, HEAD), HEAD)
            dz = jnp.dot(
                gv[:, u].reshape(RUN, D),
                td[:, :, :, cols].reshape(D, HEAD),
                preferred_element_type=F32,
            )
            dh = (dz * slope[:, u, :, cols].reshape(RUN, HEAD)).astype(BF)
            dht[:, :, cols] = dh.reshape(2, TOK, HEAD)
            dhsum[0:1, cols] += jnp.sum(dh.astype(F32), axis=0, keepdims=True)
            return carry

        lax.fori_loop(0, FFT // HEAD, columns_of, 0)
        staged(dht, dho, u, 2).start()
        grad = gv[:, u].reshape(RUN, D)
        dout[:, u] = (
            jnp.dot(grad, to[...].reshape(D, HEAD), preferred_element_type=F32)
            .astype(BF)
            .reshape(2, TOK, HEAD)
        )
        return carry

    lax.fori_loop(0, 4, third, 0)
    four = jnp.dot(
        jnp.where(lane8 % 4 + 1 == row8, dhsum[0:1, :], 0.0),
        repeat_matrix().T,
        precision=lax.Precision.HIGHEST,
        preferred_element_type=F32,
    )
    sums[...] = jnp.zeros_like(sums)
    sums[8:16, head_cols] = four
    sums[8:9, :] = jnp.sum(gv[0, 0].astype(F32), axis=0, keepdims=True)
    sums[7:8, :] = sums[8:9, :]
    lax.fori_loop(0, 8, finish_keys, 0)
    for sem, (buffer, out) in enumerate(((at, a1g), (ztile, zo), (dht, dho))):
        staged(buffer, out, 0, sem).wait()
    for copy in copy_out + own_out:
        copy.wait()
    for u in range(4):
        pltpu.make_async_copy(gv.at[:, u], gg.at[:, u], g_sem.at[u]).wait()
    net.finish()


def forward(n, x, gy, weights, small, lengths, frequency):
    rb = D // n
    R = n // 8

    def shape(*dims, kind=BF):
        return jax.ShapeDtypeStruct(dims, kind)

    w_shapes = [(4, R, 2 * rb, parts * width) for parts, width in WEIGHTS]
    block, cols, head = (2, 4, TOK, D), (2, 4, TOK, FFT), (2, 4, TOK, HEAD)
    outs = [shape(*block) for _ in range(4)]
    outs += [shape(*w) for w in w_shapes]
    outs += [shape(*head), shape(R, *head), shape(R, *head), shape(*cols), shape(*cols)]
    outs += [shape(*head), shape(SMALLR, D, kind=F32), shape(SMALLR, D, kind=F32)]
    outs += [shape(2, 4, TOK, 128, kind=F32)]
    outs += [shape(2, 4, TOK, HEAD // 2, kind=F32) for _ in range(2)]
    out_specs = [ANY] * 13 + [VM] * 6
    scratch = [
        pltpu.VMEM(block, BF),
        pltpu.VMEM(block, BF),
        pltpu.VMEM((4, R, 2 * rb, 128), F32),
        *[pltpu.VMEM(w, BF) for w in w_shapes],
        pltpu.VMEM(cols, F32),
        pltpu.VMEM(block, BF),
        pltpu.VMEM((3, *head), BF),
        pltpu.VMEM((2, TOK, D), BF),
        pltpu.VMEM((2, TOK, FFT), BF),
        pltpu.VMEM((2, TOK, FFT), BF),
        pltpu.VMEM((8, FFT), F32),
        pltpu.VMEM((8, FFT), F32),
    ]
    copies = 7 + 7 * 6 + (R - 1) * (1 + 8 + 2 * 8) + 14

    def kernel(*refs):
        forward_kernel(n, lengths.shape[0], *refs)

    return pl.pallas_call(
        kernel,
        out_shape=outs,
        in_specs=[ANY] * 7 + [pl.BlockSpec(memory_space=pltpu.SMEM), VM],
        out_specs=out_specs,
        scratch_shapes=[
            *scratch,
            pltpu.SemaphoreType.DMA((copies,)),
            pltpu.SemaphoreType.DMA((copies,)),
            pltpu.SemaphoreType.DMA((16,)),
            pltpu.SemaphoreType.DMA((3,)),
            pltpu.SemaphoreType.DMA((4,)),
        ],
        compiler_params=pltpu.CompilerParams(
            collective_id=0, has_side_effects=True, vmem_limit_bytes=62 * MIB
        ),
    )(x, gy, *weights, small, lengths, frequency)


class SumT:
    def __init__(self, copies, place, data, slots, out):
        self.copies, self.place, self.data, self.slots, self.out = copies, place, data, slots, out
        self.ops = {}
        self.cur = {s: data.at[s] for s in range(8)}

    def send(self, s):
        hop = top_bit(s)
        self.ops[s] = self.copies.remote(self.cur[s], self.slots.at[s - 1], self.place.dev_t(hop))

    def add(self, s):
        to = s - top_bit(s)
        self.ops[s].wait_recv()
        slot = self.slots.at[s - 1]
        if to == 0 and s == 1:
            add_rows(self.out, self.cur[0], slot)
        else:
            add_rows(slot, self.cur[to], slot)
            self.cur[to] = slot

    def start(self):
        for s in (6, 7, 5, 4):
            self.send(s)

    def middle(self):
        for s in (6, 7):
            self.add(s)
            self.send(s - 4)
        self.add(5)

    def late(self):
        self.add(3)
        self.send(1)
        self.add(4)
        self.add(2)

    def end(self):
        self.add(1)


class SumR:
    def __init__(self, copies, place, piece, slots, order):
        self.copies, self.place, self.slots = copies, place, slots
        self.steps = collected(order)
        self.cur = {i: piece(i) for i in range(1 << len(order))}
        self.ops = {}

    def send(self, step):
        bit, members = self.steps[step]
        for i in members:
            self.ops[i] = self.copies.remote(
                self.cur[i], self.slots.at[i - 1], self.place.dev_r(bit)
            )

    def add(self, step):
        bit, members = self.steps[step]
        for i in members:
            self.ops[i].wait_recv()
            slot = self.slots.at[i - 1]
            add_rows(slot, self.cur[i ^ bit], slot)
            self.cur[i ^ bit] = slot


def return_keys_kernel(n, have, *refs):
    place = Place(n)
    refs = list(refs)
    count = len(have)
    ins, refs = refs[:count], refs[count:]
    outs, refs = refs[:count], refs[count:]
    slots, (send, recv) = refs[:count], refs[count:]
    copies = Copies(send, recv)
    both = orders(place.bits)
    r_group = [1 << b for b in range(place.bits)] if set(have) - {"p"} else []
    t_group = (1, 2, 4) if "p" in have else ()
    greet(place, t_group, r_group)
    total, sums = None, []
    for name, src, dst, slot in zip(have, ins, outs, slots):
        if name == "p":
            total = SumT(copies, place, src, slot, dst)
        else:
            order = both[0] if name == "k" else both[1]
            sums.append((SumR(copies, place, lambda i, src=src: src.at[i], slot, order), dst))
    for part, _ in sums:
        part.send(0)
    if total:
        total.start()
        total.middle()
    for step in range(place.bits):
        for part, _ in sums:
            part.add(step)
            if step + 1 < place.bits:
                part.send(step + 1)
    if total:
        total.late()
    for part, dst in sums:
        copy = copies.local(part.cur[0], dst)
        copy.wait()
    if total:
        total.end()
    copies.finish()


def return_keys(n, ins, collective_id):
    R = n // 8
    outs, scratch, copies = [], [], 0
    for name in ins:
        if name == "p":
            outs.append(jax.ShapeDtypeStruct((TOK, D), F32))
            scratch.append(pltpu.VMEM((7, TOK, D), BF))
            copies += 7
        else:
            outs.append(jax.ShapeDtypeStruct((8, TOK, HEAD), BF))
            scratch.append(pltpu.VMEM((R - 1, 8, TOK, HEAD), BF))
            copies += R

    def kernel(*refs):
        return_keys_kernel(n, tuple(ins), *refs)

    out = call(
        kernel,
        tuple(ins.values()),
        [VM] * len(ins),
        outs,
        [VM] * len(ins),
        scratch,
        collective_id,
        copies,
    )
    return dict(zip(ins, out))


def return_grads_kernel(
    n, gi, gu, go, gd, e, small, oi, ou, oo, od, oe, osmall, si, su, so, sd, se, ss, send, recv
):
    place = Place(n)
    copies = Copies(send, recv)
    rb = D // n
    both = orders(place.bits)
    greet(place, range(1, 8), [1 << b for b in range(place.bits)])
    total = SumT(copies, place, e, se, oe)
    total.start()

    tasks = []
    for src, slot, dst, (parts, width) in zip(
        (gu, gd, gi, go), (su, sd, si, so), (ou, od, oi, oo), [WEIGHTS[k] for k in (1, 3, 0, 2)]
    ):
        for half in range(2):

            def piece(i, src=src, half=half):
                return src.at[pl.ds(2 * half, 2), place.rr_of(i)]

            part = SumR(copies, place, piece, slot.at[half], both[half])
            tasks.append((part, half, dst, parts, width))
    small_sum = SumR(copies, place, lambda i: small.at[:, place.rr_of(i)], ss, both[0])
    for part, *_ in tasks:
        part.send(0)
    small_sum.send(0)
    total.middle()
    for step in range(place.bits):
        for part, *_ in tasks:
            part.add(step)
            if step + 1 < place.bits:
                part.send(step + 1)
        small_sum.add(step)
        if step + 1 < place.bits:
            small_sum.send(step + 1)
    total.late()

    finals = {}
    for k in range(4):
        pieces = [tasks[2 * k + half][0].cur[0] for half in range(2)]
        finals[k] = pieces
    ops = []
    for k in range(4):
        _, _, dst, parts, width = tasks[2 * k]
        for zz in range(4):
            for cc in range(2):
                src = finals[k][zz // 2].at[zz % 2, pl.ds(cc * rb, rb), :]
                ops.append((zz, cc, src, dst, parts, width))
    sends = []
    for k in range(4):
        _, _, dst, parts, width = tasks[2 * k]
        store = tasks[2 * k][0].slots
        slot = store
        del slot
        for s in range(8):
            for p in range(parts):
                cols = pl.ds(pl.multiple_of(p * D + place.t * width, 128), width)
                sends.append((k, s, p, cols, dst, width))
    remote = []
    joined = {}
    for k, (ref, outbuf) in enumerate(((gu, ou), (gd, od), (gi, oi), (go, oo))):
        del ref, outbuf
        joined[k] = finals[k]
    for k, s, p, cols, dst, width in sends:
        base = (su, sd, si, so)[k]
        last = tasks[2 * k][0].steps[-1][1][0], tasks[2 * k + 1][0].steps[-1][1][0]
        zt = place.zt_of(s)
        rows = pl.ds(pl.multiple_of(place.c_of(s) * rb, rb), rb)
        which = zt // 2
        index = (1 - which) * (last[0] - 1) + which * (last[1] - 1)
        src = base.at[which, index, zt % 2, rows, pl.ds(p * width, width)]
        if s == 0:
            remote.append(("local", copies.local(src, dst.at[:, cols])))
        else:
            remote.append(("remote", copies.remote(src, dst.at[:, cols], place.dev_t(s))))
    last = small_sum.steps[-1][1][0] - 1
    for s in range(8):
        rows = pl.ds(pl.multiple_of(place.c_of(s) * SMALLR, SMALLR), SMALLR)
        src = ss.at[last, place.zt_of(s), rows, :]
        if s == 0:
            remote.append(("local", copies.local(src, osmall.at[place.t])))
        else:
            remote.append(("remote", copies.remote(src, osmall.at[place.t], place.dev_t(s))))
    total.end()
    for kind, copy in remote:
        if kind == "local":
            copy.wait()
        else:
            copy.wait_recv()
    copies.finish()


def return_grads(n, grads, e, small, collective_id):
    R = n // 8
    rb = D // n
    outs = [jax.ShapeDtypeStruct((rb, parts * D if parts > 1 else HEADS * width), BF) for parts, width in WEIGHTS]
    outs += [jax.ShapeDtypeStruct((TOK, D), F32), jax.ShapeDtypeStruct((8, SMALLR, 128), F32)]
    scratch = [
        pltpu.VMEM((2, R - 1, 2, 2 * rb, parts * width), BF) for parts, width in WEIGHTS
    ] + [
        pltpu.VMEM((7, TOK, D), BF),
        pltpu.VMEM((R - 1, 4, 2 * SMALLR, 128), F32),
    ]
    copies = 7 + 9 * (R - 1) + 8 * 6 + 8

    def kernel(*refs):
        return_grads_kernel(n, *refs)

    return call(
        kernel,
        (*grads, e, small),
        [VM] * 6,
        outs,
        [ANY] * 4 + [VM, ANY],
        scratch,
        collective_id,
        copies,
    )


WIDE = 512


class FoldT:
    def __init__(self, net, place, data, cs, zs, ys, out):
        self.data, self.cs, self.zs, self.ys, self.out = data, cs, zs, ys, out
        self.hop_c = net.add(lambda k: (data.at[k], cs.at[k], place.dev_t(4)), 4)
        self.hop_z0 = net.add(lambda k: (cs.at[2 + k], zs.at[k], place.dev_t(2)), 2)
        self.hop_z1 = net.add(lambda k: (zs.at[1], ys.at[0], place.dev_t(1)))

    @staticmethod
    def order(idx):
        return 7 - idx // 4 - 2 * (idx % 4)

    def loop(self, make, emit, after):
        def step(idx, carry):
            s = self.order(idx)
            make(s, idx)
            k = s % 4

            def far(where, value):
                self.data[(k, *where)] = value.astype(BF)

            def near(where, value):
                self.cs[(k, *where)] = (value + self.cs[(k, *where)].astype(F32)).astype(BF)

            @pl.when(s >= 4)
            def _():
                emit(s, idx, far)
                self.hop_c(k).start()

            @pl.when(s < 4)
            def _():
                self.hop_c(k).wait_recv()
                emit(s, idx, near)

                @pl.when(s >= 2)
                def _():
                    self.hop_z0(s - 2).start()

            after(idx)
            return carry

        lax.fori_loop(0, 8, step, 0)

    def turn_z1(self):
        self.hop_z0(1).wait_recv()
        add_rows(self.zs.at[1], self.cs.at[1], self.zs.at[1])
        self.hop_z1().start()

    def turn_own(self):
        self.hop_z0(0).wait_recv()
        add_rows(self.zs.at[0], self.cs.at[0], self.zs.at[0])

    def end(self):
        self.hop_z1().wait_recv()
        add_rows(self.out, self.zs.at[0], self.ys.at[0])


def fold_scratch():
    return [
        pltpu.VMEM((4, TOK, D), BF),
        pltpu.VMEM((4, TOK, D), BF),
        pltpu.VMEM((2, TOK, D), BF),
        pltpu.VMEM((1, TOK, D), BF),
    ]


class FoldR:
    def __init__(self, net, place, far, own, slots, order):
        one, two = order
        self.own, self.slots = own, slots
        self.both = net.add(lambda k: (far(3), slots.at[0], place.dev_r(one)))
        self.first = net.add(lambda k: (far(one), slots.at[1], place.dev_r(one)))
        self.second = net.add(lambda k: (slots.at[0], slots.at[2], place.dev_r(two)))

    def begin(self):
        self.both().start()
        self.first().start()

    def advance(self):
        self.both().wait_recv()
        add_rows(self.slots.at[0], self.own.at[1], self.slots.at[0])
        self.second().start()

    def gather(self):
        self.first().wait_recv()
        add_rows(self.slots.at[1], self.own.at[0], self.slots.at[1])

    def end(self, out=None):
        self.second().wait_recv()
        out = self.slots.at[2] if out is None else out
        add_rows(out, self.slots.at[1], self.slots.at[2])


def weight_folds(n, net, place, grads, own, slots):
    view = grads.reshape(4, n // 8, 2 * (D // n), grads.shape[-1])
    both = orders(2)
    halves, pieces = [], []
    for h in range(2):

        def piece(i, h=h):
            return view.at[pl.ds(2 * h, 2), place.rr_of(i)]

        halves.append(FoldR(net, place, piece, own.at[h], slots.at[h], both[h]))
        pieces.append((piece(0), own.at[h, 0]))
        pieces.append((piece(both[h][1]), own.at[h, 1]))
    return halves, pieces


def gradient_tiles(lhs, tiles, turned, sem, products):
    wide = tiles.shape[-1]
    count = D // wide

    def fetch(f):
        cols = pl.ds(pl.multiple_of(f * wide, wide), wide)
        return pltpu.make_async_copy(lhs.at[:, :, cols], tiles.at[f % 2], sem.at[f % 2])

    def put(f, stage, out, sems):
        rows = pl.ds(pl.multiple_of(f * wide, wide), wide)
        return pltpu.make_async_copy(stage.at[f % 2], out.at[rows, :], sems.at[f % 2])

    fetch(0).start()

    def step(f, carry):
        fetch(f).wait()

        @pl.when(f + 1 < count)
        def _():
            fetch(f + 1).start()

        def turn_block(s, carry):
            turned[:, pl.ds(pl.multiple_of(s * TOK, TOK), TOK)] = tiles[f % 2, s].T
            return carry

        lax.fori_loop(0, 8, turn_block, 0)
        for rhs, stage, out, sems in products:

            @pl.when(f >= 2)
            def _(stage=stage, out=out, sems=sems):
                put(f - 2, stage, out, sems).wait()

            def columns_of(c, carry, rhs=rhs, stage=stage):
                cols = pl.ds(pl.multiple_of(c * HEAD, HEAD), HEAD)
                right = rhs[:, :, cols].reshape(8 * TOK, HEAD)
                total = jnp.dot(turned[...], right, preferred_element_type=F32)
                stage[f % 2, :, cols] = total.astype(BF)
                return carry

            lax.fori_loop(0, rhs.shape[-1] // HEAD, columns_of, 0)
            put(f, stage, out, sems).start()
        return carry

    lax.fori_loop(0, count, step, 0)
    for f in (count - 2, count - 1):
        for _, stage, out, sems in products:
            put(f, stage, out, sems).wait()


def half_fold(net, place, grads, h, own, slots):
    order = orders(2)[h]
    cols = pl.ds(h * (FFT // 2), FFT // 2)

    def piece(i):
        return grads.at[:, place.rr_of(i), :, cols]

    fold = FoldR(net, place, piece, own, slots, order)
    return fold, [(piece(0), own.at[0]), (piece(order[1]), own.at[1])]


def return_one_kernel(
    n, dk, dv, o, z, w_out, w_down, gy, a2, dh,
    p_own, dk_own, dv_own, up_sum, g_out, g_down, g_up,
    zov, wdo, dhv, kown, vown, data, cs, zs, ys, ks, vs, tiles, turned, st_wide, st_head, uown, us,
    send, recv, load, fetch_sem, put_sem, near,
):
    place = Place(n)
    net = Net(send, recv)
    greet(place, (1, 2, 4), (1, 2))
    both = orders(2)
    keys = FoldR(net, place, lambda i: dk.at[i], kown, ks, both[0])
    values = FoldR(net, place, lambda i: dv.at[i], vown, vs, both[1])
    total = FoldT(net, place, data, cs, zs, ys, p_own)
    ups, pieces = [], []
    for h in range(2):
        fold, near_pieces = half_fold(
            net, place, g_up.reshape(4, n // 8, 2 * (D // n), FFT), h, uown.at[h], us.at[h]
        )
        ups.append(fold)
        pieces += near_pieces
    keys.both().start()
    values.both().start()

    loads = [
        pltpu.make_async_copy(src, dst, load.at[k])
        for k, (src, dst) in enumerate(
            (
                (z, zov.at[:, :, :FFT]),
                (o, zov.at[:, :, FFT:]),
                (w_down, wdo.at[:, :FFT]),
                (w_out, wdo.at[:, FFT:]),
                (dk.at[2], kown.at[1]),
                (dv.at[1], vown.at[1]),
                (dk.at[0], kown.at[0]),
                (dv.at[0], vown.at[0]),
                (dh, dhv),
            )
        )
    ]
    for copy in loads:
        copy.start()
    for copy in loads[:4]:
        copy.wait()

    def make(s, idx):
        del s, idx

    def emit(s, idx, put):
        def chunk(k, carry):
            cols = pl.ds(pl.multiple_of(k * HEAD, HEAD), HEAD)
            put((slice(None), cols), contract_cols(zov[s], wdo[cols, :]))
            return carry

        lax.fori_loop(0, D // HEAD, chunk, 0)

    def after(idx):
        @pl.when(idx == 3)
        def _():
            keys.first().start()
            values.first().start()

        @pl.when(idx == 6)
        def _():
            for copy in loads[4:]:
                copy.wait()
            keys.advance()
            values.advance()

    total.loop(make, emit, after)
    total.turn_z1()
    gradient_tiles(a2, tiles, turned, fetch_sem, [(dhv, st_wide, g_up, put_sem.at[0])])
    own_loads = [
        pltpu.make_async_copy(src, dst, near.at[k]) for k, (src, dst) in enumerate(pieces)
    ]
    for up in ups:
        up.begin()
    for copy in own_loads:
        copy.start()
    keys.gather()
    values.gather()
    gradient_tiles(
        gy, tiles, turned, fetch_sem,
        [
            (zov.at[:, :, :FFT], st_wide, g_down, put_sem.at[0]),
            (zov.at[:, :, FFT:], st_head, g_out, put_sem.at[1]),
        ],
    )
    for copy in own_loads:
        copy.wait()
    for up in ups:
        up.advance()
    keys.end(dk_own)
    values.end(dv_own)
    total.turn_own()
    for h, up in enumerate(ups):
        up.gather()
        up.end(up_sum.at[h])
    total.end()
    net.finish()


def return_one(n, dk, dv, o, z, w_out, w_down, gy, a2, dh):
    rows = 2 * (D // n)
    head, cols = (8, TOK, HEAD), (8, TOK, FFT)
    half = (4, rows, FFT // 2)
    outs = [
        jax.ShapeDtypeStruct((TOK, D), F32),
        jax.ShapeDtypeStruct(head, BF),
        jax.ShapeDtypeStruct(head, BF),
        jax.ShapeDtypeStruct((2, *half), BF),
        jax.ShapeDtypeStruct((D, HEAD), BF),
        jax.ShapeDtypeStruct((D, FFT), BF),
        jax.ShapeDtypeStruct((D, FFT), BF),
    ]
    scratch = [
        pltpu.VMEM((8, TOK, FFT + HEAD), BF),
        pltpu.VMEM((D, FFT + HEAD), BF),
        pltpu.VMEM(cols, BF),
        pltpu.VMEM((2, *head), BF),
        pltpu.VMEM((2, *head), BF),
        *fold_scratch(),
        pltpu.VMEM((3, *head), BF),
        pltpu.VMEM((3, *head), BF),
        pltpu.VMEM((2, 8, TOK, WIDE), BF),
        pltpu.VMEM((WIDE, 8 * TOK), BF),
        pltpu.VMEM((2, WIDE, FFT), BF),
        pltpu.VMEM((2, WIDE, HEAD), BF),
        pltpu.VMEM((2, 2, *half), BF),
        pltpu.VMEM((2, 3, *half), BF),
    ]

    def kernel(*refs):
        return_one_kernel(n, *refs)

    return pl.pallas_call(
        kernel,
        out_shape=outs,
        in_specs=[ANY] * 9,
        out_specs=[VM] * 4 + [ANY] * 3,
        scratch_shapes=[
            *scratch,
            pltpu.SemaphoreType.DMA((19,)),
            pltpu.SemaphoreType.DMA((19,)),
            pltpu.SemaphoreType.DMA((9,)),
            pltpu.SemaphoreType.DMA((2,)),
            pltpu.SemaphoreType.DMA((2, 2)),
            pltpu.SemaphoreType.DMA((4,)),
        ],
        compiler_params=pltpu.CompilerParams(
            collective_id=2, has_side_effects=True, vmem_limit_bytes=62 * MIB
        ),
    )(dk, dv, o, z, w_out, w_down, gy, a2, dh)


def return_two_kernel(
    n, gi, gu, go, gd, dq, dk, dv, a1, x, dh, w_in, w_up, cosine, sine, smt, stats, sums,
    oi, ou, oo, od, e_own, osmall, gi_out,
    dqv, dkv, dvv, djp, djn, dhv, wi, wu, xt, cst, snt, data, cs, zs, ys,
    ui, uo, ud, si, so, sd, term, blocks, sslots, tiles, turned, st_in,
    send, recv, load, near, x_sem, fetch_sem, put_sem, last_sem,
):
    del gi
    place = Place(n)
    net = Net(send, recv)
    rb = D // n
    R = place.R
    both = orders(2)
    greet(place, range(1, 8), (1, 2))
    names = ((gd, ud, sd, od, 3), (go, uo, so, oo, 2), (gi_out, ui, si, oi, 0))
    parts, pieces = [], []
    for src, own, slots, _, _ in names:
        halves, near_pieces = weight_folds(n, net, place, src, own, slots)
        parts.append(halves)
        pieces += near_pieces
    small = FoldR(
        net, place, lambda i: blocks.at[place.rr_of(i)], None, sslots, both[0]
    )
    total = FoldT(net, place, data, cs, zs, ys, e_own)

    finals = []
    ends = []
    for _, _, slots, dst, k in names:
        count, width = WEIGHTS[k]
        ends.append(
            (
                lambda zt, rows, cols, slots=slots: slots.at[zt // 2, 2, zt % 2, rows, cols],
                dst, width, [(p * width, p * D) for p in range(count)],
            )
        )
    for h in range(2):
        summed = gu.at[h]
        ends.append(
            (
                lambda zt, rows, cols, summed=summed: summed.at[zt, rows, cols],
                ou, FFT // 2, [(0, h * (FFT // 2))],
            )
        )
    for which, (summed, dst, width, spans) in enumerate(ends):
        stride = FFT if dst is ou else width
        ops = []
        for s in range(8):
            rows = pl.ds(pl.multiple_of(place.c_of(s) * rb, rb), rb)
            for p, (at, into) in enumerate(spans):
                cols = pl.ds(pl.multiple_of(into + place.t * stride, 128), width)
                piece = summed(place.zt_of(s), rows, pl.ds(at, width))
                if s == 0:
                    ops.append(
                        pltpu.make_async_copy(
                            piece, dst.at[:, cols], last_sem.at[which * 3 + p]
                        )
                    )
                else:
                    ops.append(
                        net.add(
                            lambda k, piece=piece, dst=dst, cols=cols, s=s: (
                                piece, dst.at[:, cols], place.dev_t(s),
                            )
                        )
                    )
        finals.append(ops)
    small_last = [
        net.add(
            lambda k, s=s: (
                sslots.at[2, place.zt_of(s)], osmall.at[place.t], place.dev_t(s),
            )
        )
        for s in range(1, 8)
    ]
    small_mine = pltpu.make_async_copy(
        sslots.at[2, place.zt], osmall.at[place.t], last_sem.at[15]
    )

    def send_finals(which):
        for k, op in enumerate(finals[which]):
            (op if k < len(ends[which][3]) else op()).start()

    def wait_finals(which):
        for k, op in enumerate(finals[which]):
            if k < len(ends[which][3]):
                op.wait()
            else:
                op().wait_recv()

    for part in parts[0]:
        part.begin()
    send_finals(3)
    send_finals(4)
    loads = [
        pltpu.make_async_copy(src, dst, load.at[k])
        for k, (src, dst) in enumerate(
            (
                (dq, dqv), (dk, dkv), (dv, dvv), (cosine, cst), (sine, snt),
                (w_in, wi), (dh, dhv), (w_up, wu),
            )
        )
    ]
    for copy in loads:
        copy.start()
    own_loads = [
        pltpu.make_async_copy(src, dst, near.at[k])
        for k, (src, dst) in enumerate(pieces)
    ]
    for copy in own_loads[:8]:
        copy.start()

    def fetch_x(s, slot):
        return pltpu.make_async_copy(x.at[s], xt.at[slot], x_sem.at[slot])

    fetch_x(7, 0).start()
    term[...] = sums[...]
    shuffle = shuffle_matrix().astype(BF)
    head_cols = pl.ds(pl.multiple_of(place.t * HEAD, HEAD), HEAD)
    for copy in loads:
        copy.wait()
    chunk_cols = 256

    def paired_joint(s):
        csn, sn = cst[s], snt[s]
        half = HEAD // 2
        for p, src in enumerate((dqv, dkv)):
            one = src[s, :, :half].astype(F32)
            two = src[s, :, half:].astype(F32)
            djp[:, p * HEAD : p * HEAD + half] = (one * csn + two * sn).astype(BF)
            djp[:, p * HEAD + half : (p + 1) * HEAD] = (two * csn - one * sn).astype(BF)
        djp[:, 2 * HEAD :] = dvv[s]

    def natural_joint(s):
        for p in range(2):
            cols = slice(p * HEAD, (p + 1) * HEAD)
            natural = contract_cols(djp[:, cols], shuffle)
            djn[s, :, cols] = natural.astype(BF)
            term[4 + p : 5 + p, head_cols] += jnp.sum(natural, axis=0, keepdims=True)
        value = dvv[s]
        djn[s, :, 2 * HEAD :] = value
        term[6:7, head_cols] += jnp.sum(value.astype(F32), axis=0, keepdims=True)

    def make(s, idx):
        @pl.when(idx < 4)
        def _():
            paired_joint(s)
            natural_joint(s)

        @pl.when(idx >= 4)
        def _():
            paired_joint(s)

        fetch_x(s, idx % 2).wait()

        @pl.when(idx < 7)
        def _():
            fetch_x(total.order(idx + 1), (idx + 1) % 2).start()

    def emit(s, idx, put):
        average = stats[s, :, 0:1]
        inverse = stats[s, :, 1:2]

        def chunk(k, carry):
            cols = pl.ds(pl.multiple_of(k * chunk_cols, chunk_cols), chunk_cols)
            xhat = (xt[idx % 2, :, cols].astype(F32) - average) * inverse
            one = contract_cols(djp[...], wi[cols, :])
            two = contract_cols(dhv[s], wu[cols, :])
            for row, value in ((0, one * xhat), (1, one), (2, two * xhat), (3, two)):
                term[row : row + 1, cols] += jnp.sum(value, axis=0, keepdims=True)
            put((slice(None), cols), one * smt[0:1, cols] + two * smt[2:3, cols])
            return carry

        lax.fori_loop(0, D // chunk_cols, chunk, 0)

    def after(idx):
        @pl.when(idx == 2)
        def _():
            for copy in own_loads[:4]:
                copy.wait()
            for part in parts[0]:
                part.advance()

        @pl.when(idx == 3)
        def _():
            def rest(k, carry):
                paired_joint(6 - 2 * k)
                natural_joint(6 - 2 * k)
                return carry

            lax.fori_loop(0, 4, rest, 0)
            gradient_tiles(a1, tiles, turned, fetch_sem, [(djn, st_in, gi_out, put_sem)])
            for part in parts[2]:
                part.begin()
            for copy in own_loads[8:12]:
                copy.start()
            total.turn_z1()
            for part in parts[0]:
                part.gather()
                part.end()
            send_finals(0)

        @pl.when(idx == 4)
        def _():
            for part in parts[1]:
                part.begin()

        @pl.when(idx == 6)
        def _():
            for copy in own_loads[8:12]:
                copy.wait()
            for part in parts[2]:
                part.advance()

        @pl.when(idx == 7)
        def _():
            for copy in own_loads[4:8]:
                copy.wait()
            for part in parts[1]:
                part.advance()

    total.loop(make, emit, after)

    for rr in range(R):
        for zt in range(4):
            at = (zt * R + rr) * 128
            blocks[rr, zt] = term[:, at : at + 128]
    small.both().start()
    small.first().start()
    for part in parts[2]:
        part.gather()
        part.end()
    send_finals(2)
    for part in parts[1]:
        part.gather()
        part.end()
    send_finals(1)
    small.both().wait_recv()
    sslots[0] = sslots[0] + blocks[place.rr_of(2)]
    small.second().start()
    total.turn_own()
    small.first().wait_recv()
    small.second().wait_recv()
    sslots[2] = sslots[2] + (sslots[1] + blocks[place.rr])
    small_mine.start()
    for op in small_last:
        op().start()
    total.end()
    for which in range(5):
        wait_finals(which)
    small_mine.wait()
    for op in small_last:
        op().wait_recv()
    net.finish()


def return_two(n, up_sum, g_out, g_down, dq, dk, dv, a1, x, dh, w_in, w_up, cosine, sine, smt, stats, sums):
    rb = D // n
    R = n // 8
    head, cols, block = (8, TOK, HEAD), (8, TOK, FFT), (8, TOK, D)
    outs = [jax.ShapeDtypeStruct((rb, HEADS * parts * width), BF) for parts, width in WEIGHTS]
    outs += [
        jax.ShapeDtypeStruct((TOK, D), F32),
        jax.ShapeDtypeStruct((8, SMALLR, 128), F32),
        jax.ShapeDtypeStruct((D, 3 * HEAD), BF),
    ]
    wide = [parts * width for parts, width in WEIGHTS]
    scratch = [
        pltpu.VMEM(head, F32),
        pltpu.VMEM(head, BF),
        pltpu.VMEM(head, BF),
        pltpu.VMEM((TOK, 3 * HEAD), BF),
        pltpu.VMEM((8, TOK, 3 * HEAD), BF),
        pltpu.VMEM(cols, BF),
        pltpu.VMEM((D, 3 * HEAD), BF),
        pltpu.VMEM((D, FFT), BF),
        pltpu.VMEM((2, TOK, D), BF),
        pltpu.VMEM((8, TOK, HEAD // 2), F32),
        pltpu.VMEM((8, TOK, HEAD // 2), F32),
        *fold_scratch(),
        *[pltpu.VMEM((2, 2, 2, 2 * rb, wide[k]), BF) for k in (0, 2, 3)],
        *[pltpu.VMEM((2, 3, 2, 2 * rb, wide[k]), BF) for k in (0, 2, 3)],
        pltpu.VMEM((SMALLR, D), F32),
        pltpu.VMEM((R, 4, SMALLR, 128), F32),
        pltpu.VMEM((3, 4, SMALLR, 128), F32),
        pltpu.VMEM((2, 8, TOK, HEAD), BF),
        pltpu.VMEM((HEAD, 8 * TOK), BF),
        pltpu.VMEM((2, HEAD, 3 * HEAD), BF),
    ]
    copies = 6 * 3 + 3 + 7 + 7 * 7 + 7

    def kernel(*refs):
        return_two_kernel(n, None, *refs)

    return pl.pallas_call(
        kernel,
        out_shape=outs,
        in_specs=[ANY] * 13 + [VM] * 3,
        out_specs=[ANY] * 4 + [VM] + [ANY] * 2,
        scratch_shapes=[
            *scratch,
            pltpu.SemaphoreType.DMA((copies,)),
            pltpu.SemaphoreType.DMA((copies,)),
            pltpu.SemaphoreType.DMA((8,)),
            pltpu.SemaphoreType.DMA((16,)),
            pltpu.SemaphoreType.DMA((2,)),
            pltpu.SemaphoreType.DMA((2,)),
            pltpu.SemaphoreType.DMA((2,)),
            pltpu.SemaphoreType.DMA((16,)),
        ],
        compiler_params=pltpu.CompilerParams(
            collective_id=3, has_side_effects=True, vmem_limit_bytes=62 * MIB
        ),
    )(up_sum, g_out, g_down, dq, dk, dv, a1, x, dh, w_in, w_up, cosine, sine, smt, stats, sums)


def token_row(base, core, size=RUN):
    lane = lax.broadcasted_iota(jnp.int32, (1, size), 1)
    return base + (lane + core * TOK) % RUN


def token_col(base, core, size=RUN):
    row = lax.broadcasted_iota(jnp.int32, (size, 1), 0)
    return base + (row + core * TOK) % RUN


def start_of(tokens, lengths, nseq):
    out, begin = tokens * 0, lengths[0] * 0
    for s in range(nseq):
        out = jnp.where(tokens >= begin, begin, out)
        begin = begin + lengths[s]
    return out


def run_facts(place, lengths, nseq, u):
    number = place.zt_of_run(u) * place.R + place.rr
    count = number - start_of(number * RUN, lengths, nseq) // RUN + 1
    return number, count, start_of(number * RUN + RUN - 1, lengths, nseq)


def scores_of(key, query):
    return lax.dot_general(key, query, (((1,), (1,)), ((), ())), preferred_element_type=F32)


def seen_mask(core, gq, gk, lengths, nseq):
    tq = token_row(gq * RUN, core)
    tk = token_col(gk * RUN, core)
    return (tk <= tq) & (tk >= start_of(tq, lengths, nseq))


def attend_kernel(
    n, nseq, lengths, q, dout, kg, vg, o, stats, m, l, acc, kv, sem
):
    u = pl.program_id(0)
    place = Place(n)
    number, count, last = run_facts(place, lengths, nseq, u)
    m[...] = jnp.full_like(m, NEGATIVE)
    l[...] = jnp.zeros_like(l)
    acc[...] = jnp.zeros_like(acc)

    def fetch(d, slot):
        far = number - d
        moved = (far // place.R) ^ place.zt
        i, ku = (far % place.R) ^ place.rr, moved % 2 * 2 + moved // 2
        return [
            pltpu.make_async_copy(src.at[i, :, ku], kv.at[slot, p], sem.at[slot, p])
            for p, src in enumerate((kg, vg))
        ]

    def block(slot, far, masked):
        query = q[...].reshape(RUN, HEAD)
        key = kv[slot, 0].reshape(RUN, HEAD)
        value = kv[slot, 1].reshape(RUN, HEAD)
        s = scores_of(key, query)
        if masked:
            s = jnp.where(seen_mask(place.c, number, number - far, lengths, nseq), s, NEGATIVE)
        old = m[0:1, :]
        new = jnp.maximum(old, jnp.max(s, axis=0, keepdims=True))
        p = jnp.exp(s - new)
        fade = jnp.exp(old - new)
        l[0:1, :] = l[0:1, :] * fade + jnp.sum(p, axis=0, keepdims=True)
        m[0:1, :] = new
        mixed = lax.dot_general(
            value, p.astype(BF), (((0,), (0,)), ((), ())), preferred_element_type=F32
        )
        acc[...] = acc[...] * fade + mixed

    for copy in fetch(0, 0):
        copy.start()

    def step(d, carry):
        slot = d % 2
        for copy in fetch(d, slot):
            copy.wait()

        @pl.when(d + 1 < count)
        def _():
            for copy in fetch(d + 1, 1 - slot):
                copy.start()

        edge = (d == 0) | ((number - d) * RUN < last)

        @pl.when(edge)
        def _():
            block(slot, d, True)

        @pl.when(jnp.logical_not(edge))
        def _():
            block(slot, d, False)

        return carry

    lax.fori_loop(0, count, step, 0)
    out = acc[...] / l[0:1, :]
    rows = out.T
    o[...] = rows.astype(BF).reshape(o.shape)
    grad = dout[...].reshape(RUN, HEAD).astype(F32).T
    stats[0, 0:1, :] = m[0:1, :] + jnp.log(l[0:1, :])
    stats[0, 1:2, :] = jnp.sum(out * grad, axis=0, keepdims=True)
    stats[0, 2:8, :] = jnp.zeros((6, RUN), F32)


def attend(n, lengths, q, dout, kg, vg):
    run = pl.BlockSpec((2, 1, TOK, HEAD), lambda u, *_: (0, u, 0, 0))

    def kernel(*refs):
        attend_kernel(n, lengths.shape[0], *refs)

    return pl.pallas_call(
        kernel,
        out_shape=[
            jax.ShapeDtypeStruct((2, 4, TOK, HEAD), BF),
            jax.ShapeDtypeStruct((4, 8, RUN), F32),
        ],
        grid_spec=pltpu.PrefetchScalarGridSpec(
            num_scalar_prefetch=1,
            grid=(4,),
            in_specs=[run, run, ANY, ANY],
            out_specs=[run, pl.BlockSpec((1, 8, RUN), lambda u, *_: (u, 0, 0))],
            scratch_shapes=[
                pltpu.VMEM((8, RUN), F32),
                pltpu.VMEM((8, RUN), F32),
                pltpu.VMEM((HEAD, RUN), F32),
                pltpu.VMEM((2, 2, 2, TOK, HEAD), BF),
                pltpu.SemaphoreType.DMA((2, 2)),
            ],
        ),
        compiler_params=pltpu.CompilerParams(vmem_limit_bytes=62 * MIB),
        cost_estimate=pl.CostEstimate(
            flops=4 * 16 * RUN * RUN * HEAD, bytes_accessed=12 * MIB, transcendentals=16 * RUN * RUN
        ),
    )(lengths, q, dout, kg, vg)


def attend_back_kernel(
    n, nseq, lengths, q, dout, stats, k, v, dq, dk, dv, tq, tk, tv, facts
):
    block_at = pl.program_id(0)
    steps = pl.num_programs(0)

    place = Place(n)

    @pl.when(block_at == 0)
    def _():
        tq[...] = jnp.zeros_like(tq)
        for u in range(4):
            for f, value in enumerate(run_facts(place, lengths, nseq, u)):
                facts[4 * f + u] = value

    tk[...] = jnp.zeros_like(tk)
    tv[...] = jnp.zeros_like(tv)
    here = place.zt_of_run(block_at % 4) * place.R + (place.rr ^ (block_at // 4))

    for u in range(4):
        far = facts[u] - here
        active = (far >= 0) & (far < facts[4 + u])
        edge = (far == 0) | (here * RUN < facts[8 + u])

        def block(masked, u=u):
            query = q[:, u].reshape(RUN, HEAD)
            grad = dout[:, u].reshape(RUN, HEAD)
            key = k[...].reshape(RUN, HEAD)
            value = v[...].reshape(RUN, HEAD)
            s = scores_of(key, query)
            p = jnp.exp(s - stats[u, 0:1, :])
            if masked:
                p = jnp.where(seen_mask(place.c, facts[u], here, lengths, nseq), p, 0.0)
            dp = scores_of(value, grad)
            ds = (p * (dp - stats[u, 1:2, :])).astype(BF)
            tv[...] += jnp.dot(p.astype(BF), grad, preferred_element_type=F32)
            tk[...] += jnp.dot(ds, query, preferred_element_type=F32)
            tq[u] += lax.dot_general(
                ds, key, (((0,), (0,)), ((), ())), preferred_element_type=F32
            )

        @pl.when(active & edge)
        def _(block=block):
            block(True)

        @pl.when(active & jnp.logical_not(edge))
        def _(block=block):
            block(False)

    dk[...] = tk[...].astype(BF).reshape(dk.shape)
    dv[...] = tv[...].astype(BF).reshape(dv.shape)

    @pl.when(block_at == steps - 1)
    def _():
        for u in range(4):
            dq[:, u] = (tq[u] * HEAD**-0.5).reshape(2, TOK, HEAD)


def attend_back(n, lengths, q, dout, stats, kg, vg):
    R = n // 8
    whole = pl.BlockSpec((2, 4, TOK, HEAD), lambda b, *_: (0, 0, 0, 0))
    key = pl.BlockSpec((1, 2, 1, TOK, HEAD), lambda b, *_: (b // 4, 0, b % 4, 0, 0))

    def kernel(*refs):
        attend_back_kernel(n, lengths.shape[0], *refs)

    return pl.pallas_call(
        kernel,
        out_shape=[
            jax.ShapeDtypeStruct((2, 4, TOK, HEAD), F32),
            jax.ShapeDtypeStruct((R, 2, 4, TOK, HEAD), BF),
            jax.ShapeDtypeStruct((R, 2, 4, TOK, HEAD), BF),
        ],
        grid_spec=pltpu.PrefetchScalarGridSpec(
            num_scalar_prefetch=1,
            grid=(4 * R,),
            in_specs=[
                whole,
                whole,
                pl.BlockSpec((4, 8, RUN), lambda b, *_: (0, 0, 0)),
                key,
                key,
            ],
            out_specs=[whole, key, key],
            scratch_shapes=[
                pltpu.VMEM((4, RUN, HEAD), F32),
                pltpu.VMEM((RUN, HEAD), F32),
                pltpu.VMEM((RUN, HEAD), F32),
                pltpu.SMEM((12,), jnp.int32),
            ],
        ),
        compiler_params=pltpu.CompilerParams(vmem_limit_bytes=62 * MIB),
        cost_estimate=pl.CostEstimate(
            flops=10 * 16 * RUN * RUN * HEAD, bytes_accessed=24 * MIB, transcendentals=16 * RUN * RUN
        ),
    )(lengths, q, dout, stats, kg, vg)


def adam_step(parameter, gradient, first_moment, second_moment, step_rate):
    first_new = BETA_ONE * first_moment + (1.0 - BETA_ONE) * gradient
    second_new = BETA_TWO * second_moment + (1.0 - BETA_TWO) * gradient * gradient
    first_hat = first_new * (1.0 / (1.0 - BETA_ONE**STEPS))
    second_hat = second_new * (1.0 / (1.0 - BETA_TWO**STEPS))
    parameter_new = parameter - step_rate * (
        first_hat / (jnp.sqrt(second_hat) + ADAM_EPS) + WEIGHT_DECAY * parameter
    )
    return (first_new, second_new, parameter_new)


def adam_kernel(rates, *refs):
    count = len(rates)
    x, gy, e, part, small = refs[:5]
    groups = [refs[5 + k * count : 5 + (k + 1) * count] for k in range(7)]
    block_out, token_grad = refs[5 + 7 * count :]
    for p, g, m, v, rate, p_out, m_out, v_out in zip(
        *groups[:4], rates, *groups[4:]
    ):
        m_out[...], v_out[...], p_out[...] = adam_step(
            p[...], g[...].astype(F32), m[...], v[...], rate
        )
    xf, grad = x[...].astype(F32), e[...]
    block_out[...] = (xf + part[...] + small[7:8, :] + small[8:9, :]).astype(BF)
    centred = xf - jnp.mean(xf, axis=-1, keepdims=True)
    inverse = lax.rsqrt(jnp.mean(centred * centred, axis=-1, keepdims=True) + NORM_EPS)
    xhat = centred * inverse
    token_grad[...] = gy[...].astype(F32) + inverse * (
        grad
        - jnp.mean(grad, axis=-1, keepdims=True)
        - xhat * jnp.mean(grad * xhat, axis=-1, keepdims=True)
    )


def adam(own, params, grads, firsts, seconds, rates):
    steps = 8

    def spec(a):
        return pl.BlockSpec((a.shape[0], a.shape[1] // steps), lambda k: (0, k))

    tok = pl.BlockSpec((TOK // steps, D), lambda k: (k, 0))
    small = pl.BlockSpec((SMALLR, D), lambda k: (0, 0))
    arrays = [*params, *grads, *firsts, *seconds]
    outs = [jax.ShapeDtypeStruct(p.shape, F32) for _ in range(3) for p in params]
    own_outs = [jax.ShapeDtypeStruct((TOK, D), BF), jax.ShapeDtypeStruct((TOK, D), F32)]

    def kernel(*refs):
        adam_kernel(rates, *refs)

    out = pl.pallas_call(
        kernel,
        out_shape=[*outs, *own_outs],
        grid=(steps,),
        in_specs=[tok] * 4 + [small] + [spec(a) for a in arrays],
        out_specs=[spec(a) for a in outs] + [tok] * 2,
        compiler_params=pltpu.CompilerParams(vmem_limit_bytes=62 * MIB),
    )(*own, *arrays)
    count = len(params)
    return [out[k * count : (k + 1) * count] for k in range(3)] + list(out[3 * count :])


def contract_rows(left, right):
    return lax.dot_general(left, right, (((0,), (0,)), ((), ())), preferred_element_type=F32)


def contract_cols(left, right):
    return lax.dot_general(left, right, (((1,), (1,)), ((), ())), preferred_element_type=F32)


def paired(columns):
    turned, half = HEAD // 8, HEAD // 2
    heads = columns.reshape(columns.shape[0], -1, HEAD)
    cut = 2 * turned + half - turned
    order = [(0, turned), (2 * turned, cut), (turned, 2 * turned), (cut, HEAD)]
    return jnp.concatenate([heads[..., a:b] for a, b in order], axis=-1).reshape(columns.shape)


def unpaired(columns):
    turned, half = HEAD // 8, HEAD // 2
    heads = columns.reshape(columns.shape[0], -1, HEAD)
    order = [(0, turned), (half, half + turned), (turned, half), (half + turned, HEAD)]
    return jnp.concatenate([heads[..., a:b] for a, b in order], axis=-1).reshape(columns.shape)


def turn(values, cosine, sine):
    half = HEAD // 2
    one, two = values[:, :half], values[:, half:]
    return jnp.concatenate([one * cosine - two * sine, two * cosine + one * sine], axis=1)


def pack_small(columns, n):
    rb = D // n
    blocks = columns.reshape(SMALLR, n, rb).transpose(1, 0, 2)
    return jnp.pad(blocks, ((0, 0), (0, 0), (0, 128 - rb)))


def return_plain(n, gg, xg, a1, a2, z, dh, o, dq, dk, dv, ws, cosine, sine, small_all, sums):
    place = Place(n)
    R, rb, rows = n // 8, D // n, 8 * TOK
    a1, a2, gy, z, dh, o, dq = (v.reshape(rows, -1) for v in (a1, a2, gg, z, dh, o, dq))
    w_in, w_up, w_out, w_down = (g.reshape(D, -1) for g in ws)
    cosine, sine = cosine.reshape(rows, -1), sine.reshape(rows, -1)
    g1, g2 = small_all[0], small_all[2]
    xf = xg.reshape(rows, D).astype(F32)
    centred = xf - jnp.mean(xf, axis=-1, keepdims=True)
    xhat = centred * lax.rsqrt(jnp.mean(centred * centred, axis=-1, keepdims=True) + NORM_EPS)
    partial_out = (contract_cols(o, w_out) + contract_cols(z, w_down)).astype(BF)
    ins = {"k": dk, "v": dv, "p": partial_out.reshape(8, TOK, D)}
    back = {}
    for at, name in enumerate(ins):
        back |= return_keys(n, {name: ins[name]}, 4 + at)
    dq = turn(dq, cosine, -sine)
    dk = turn(back["k"].reshape(rows, HEAD).astype(F32), cosine, -sine)
    dj = jnp.concatenate([dq.astype(BF), dk.astype(BF), back["v"].reshape(rows, HEAD)], axis=1)
    da1 = contract_cols(dj, w_in)
    da2 = contract_cols(dh, w_up)
    e = (da1 * g1 + da2 * g2).astype(BF)
    norm_grads = [jnp.sum(v, axis=0) for v in (da1 * xhat, da1, da2 * xhat, da2)]
    dj = jnp.concatenate([unpaired(dj[:, : 2 * HEAD]), dj[:, 2 * HEAD :]], axis=1)
    dj_sum = jnp.sum(dj.astype(F32), axis=0).reshape(3, HEAD)
    own_cols = lax.dynamic_update_slice(
        jnp.zeros((SMALLR, D), F32), dj_sum, (jnp.int32(4), place.t * HEAD)
    )
    small_term = own_cols + sums
    small_term = small_term.at[:4].set(jnp.stack(norm_grads))
    small_blocks = pack_small(small_term, n).reshape(4, R, 2 * SMALLR, 128)
    grads = [
        contract_rows(left, right).astype(BF).reshape(4, R, 2 * rb, -1)
        for left, right in ((a1, dj), (a2, dh), (gy, o), (gy, z))
    ]
    *weight_grads, e_own, small_parts = return_grads(
        n, grads, e.reshape(8, TOK, D), small_blocks, 3
    )
    return back["p"], weight_grads, e_own, jnp.sum(small_parts, axis=0)[:SMALLC, :rb].T


def body(
    tokens, cotangent, lengths,
    attend_in, widening, attend_out, narrowing, small_params,
    first_attend_in, first_widening, first_attend_out, first_narrowing, first_small,
    second_attend_in, second_widening, second_attend_out, second_narrowing, second_small,
):
    n = lax.axis_size("fsdp")
    place = Place(n)
    R = place.R
    rb = D // n
    turned = HEAD // 8
    lanes = np.arange(HEAD // 2)
    frequency = np.where(lanes < turned, ROPE_BASE ** (-2.0 * lanes / (2 * turned)), 0.0)
    frequency = jnp.asarray(frequency.astype(np.float32)[None, :])

    small_rows = jnp.pad(small_params, ((0, 0), (0, 128 - SMALLC)))
    low_in = attend_in.astype(BF)
    low_in = jnp.concatenate([paired(low_in[:, : 2 * D]), low_in[:, 2 * D :]], axis=1)
    weights = [low_in] + [w.astype(BF) for w in (widening, attend_out, narrowing)]
    runs = (2, 4, TOK, HEAD)
    xg, gg, a1, a2, *ws, q, kg, vg, z, dh, dout, small_all, sums, stats_x, cosine, sine = forward(
        n, tokens, cotangent, weights, small_rows, lengths, frequency
    )
    xg, gg, a1, a2, z, dh, stats_x, cosine, sine = (
        v.reshape(8, TOK, v.shape[-1]) for v in (xg, gg, a1, a2, z, dh, stats_x, cosine, sine)
    )

    kg = kg.reshape(R, *runs)
    vg = vg.reshape(R, *runs)
    q4, dout4 = q.reshape(runs), dout.reshape(runs)
    o4, stats = attend(n, lengths, q4, dout4, kg, vg)
    dq4, dk5, dv5 = attend_back(n, lengths, q4, dout4, stats, kg, vg)
    o, dq = o4.reshape(8, TOK, HEAD), dq4.reshape(8, TOK, HEAD)
    dk, dv = dk5.reshape(R, 8, TOK, HEAD), dv5.reshape(R, 8, TOK, HEAD)
    if R == 4:
        p_own, dk, dv, up_sum, g_out, g_down, _ = return_one(
            n, dk, dv, o, z, ws[2].reshape(D, -1), ws[3].reshape(D, -1), gg, a2, dh
        )
        *weight_grads, e_own, small_parts, _ = return_two(
            n, up_sum, g_out, g_down, dq, dk, dv, a1, xg, dh,
            ws[0].reshape(D, -1), ws[1].reshape(D, -1), cosine, sine, small_all, stats_x, sums,
        )
        own_lanes = lax.dynamic_slice(
            jnp.sum(small_parts, axis=0), (0, place.c * rb), (SMALLR, rb)
        )
        small_grad = own_lanes[:SMALLC].T
    else:
        p_own, weight_grads, e_own, small_grad = return_plain(
            n, gg, xg, a1, a2, z, dh, o, dq, dk, dv, ws, cosine, sine, small_all, sums
        )
    gr_in, gr_up, gr_out, gr_down = weight_grads
    rate_inner = 2.5 * D ** (-0.5)
    rate_outer = 2.5 * (D * 11 // LMAX) ** (-0.5)
    rate_down = 2.5 * FF ** (-0.5)
    rate_small = 0.5
    new, mean, square, block_out, token_grad = adam(
        (tokens, cotangent, e_own, p_own, small_all),
        (attend_in, widening, attend_out, narrowing),
        (gr_in, gr_up, gr_out, gr_down),
        (first_attend_in, first_widening, first_attend_out, first_narrowing),
        (second_attend_in, second_widening, second_attend_out, second_narrowing),
        (rate_inner, rate_inner, rate_outer, rate_down),
    )
    mean_small, square_small, new_small = adam_step(
        small_params, small_grad, first_small, second_small, rate_small
    )
    return (
        block_out,
        token_grad,
        *new,
        new_small,
        *mean,
        mean_small,
        *square,
        square_small,
    )


def solution(mesh):
    spec = P("fsdp", None)
    return jax.shard_map(
        body,
        mesh=mesh,
        in_specs=(spec, spec, P(), *[spec] * 15),
        out_specs=(spec,) * 17,
        check_vma=False,
    )
```
